256 devices in a mesh: rep: 32 (over y, z), voc: 8 (over x, core).
Axes of the slice: x: 4, y: 4, z: 8, core: 2. Of those that a mesh axis runs over, the one named last changes fastest.
Arguments:
- log_hidden: bfloat16 [2048, 8192], P('rep'), may hold values from -6 to 6
- positions: int32 [256], P('rep'), may hold values from 0 to 59
- offsets: int32 [256], P('rep'), may hold values from 1 to 4
- head_weight: bfloat16 [8192, 8192], P('voc', 'rep'), may hold values from -0.0625 to 0.0625
- head_bias: float32 [8192], P('rep'), may hold values from -3 to 3
- vocab_head: bfloat16 [128256, 8192], P(('rep', 'voc')), may hold values from -0.4375 to 0.4375
Outputs:
- loss: float32 [], replicated
- grad_weight: float32 [8192, 8192], P('voc', 'rep')
- grad_bias: float32 [8192], P('rep')
The draws below stay inside these ranges and needn't reach their ends.
Inputs may be any that keep to these rules, and one draw needn't show every extreme that they name: `positions`: a row within the replica's own block of 64 log rows, leaving room for the offset.
All inputs are finite; a program needn't handle non-finite values.
Results may differ from the reference program's by a relative error of at most 0.008.
Values may be sent and summed in bfloat16 or wider, within the bound.
No kernel may reach another device: no remote copies, remote signals or barrier semaphores. Data moves between devices by JAX's collectives and lax.ppermute only.
A program may use at most 128 MiB of HBM per device.

```python
import jax
import jax.numpy as jnp

D = 8192
VOCAB = 128256
POS_DEV = 8
LOG_DEV = 64
POSITIONS = 256
LOG = 2048


def plant(drawn, key, least, largest):
    index_at = [jax.random.randint(jax.random.fold_in(key, axis), (), 0, length) for axis, length in enumerate(drawn.shape)]
    main_axis = drawn.shape.index(max(drawn.shape))
    next_to = index_at[:main_axis] + [(index_at[main_axis] + 1) % drawn.shape[main_axis]] + index_at[main_axis + 1:]
    return drawn.at[tuple(index_at)].set(least).at[tuple(next_to)].set(largest)


def raised(result, rng, source, target, blocks, factor):
    def block_of(dim):
        return (jnp.arange(result.shape[dim]) // (result.shape[dim] // blocks)).reshape((-1,) + (1,) * (result.ndim - 1 - dim))

    one_side = jax.random.permutation(rng, blocks)[block_of(target)]
    far = (block_of(target) + blocks // 2) % blocks
    return jnp.where((block_of(source) == one_side) | (block_of(source) == far), factor * result, result)


def block_scale(own_key, shape, pieces, smallest, largest):
    def one(axis_at, parts):
        steps = jax.random.uniform(jax.random.fold_in(jax.random.fold_in(own_key, 6), axis_at), (parts,), jnp.float32, smallest / len(pieces), largest / len(pieces))
        return jnp.repeat(jnp.exp(steps), shape[axis_at] // parts).reshape((-1,) + (1,) * (len(shape) - axis_at - 1))

    factor_of = one(*pieces[0])
    for cut in pieces[1:]:
        factor_of = factor_of * one(*cut)
    return factor_of


def scatter_about(rng, extent, spread, limit, pieces=(), kind=jnp.bfloat16):
    result = spread * jax.random.normal(rng, extent, jnp.float32)
    if pieces:
        result = result * block_scale(rng, extent, pieces, -0.22, 0.18)
    return jnp.clip(result, -limit, limit).astype(kind)


def bell_draw_with(own_key, extent, spread, limit, pieces, heavy, kind=jnp.bfloat16):
    drawn = spread * jax.random.normal(own_key, extent, jnp.float32)
    if pieces:
        drawn = drawn * block_scale(own_key, extent, pieces, -0.22, 0.18)
    return jnp.clip(raised(drawn, jax.random.fold_in(own_key, 3), *heavy), -limit, limit).astype(kind)


def setup_inputs(seed: int = 0) -> dict:
    streams_of = jax.random.split(jax.random.key(seed), 7)
    log_hidden = scatter_about(streams_of[0], (LOG, D), 1.0, 6.0, ((0, 32),))
    positions = plant(jax.random.randint(streams_of[1], (POSITIONS,), 0, LOG_DEV - 4), jax.random.fold_in(streams_of[1], 1), 0, (LOG_DEV - 4) - 1).astype(jnp.int32)
    offsets = plant(jax.random.randint(streams_of[2], (POSITIONS,), 1, 5), jax.random.fold_in(streams_of[2], 1), 1, 4).astype(jnp.int32)
    head_weight = scatter_about(streams_of[3], (D, D), D ** -0.5, 0.0625, ((0, 8), (1, 32)))
    head_bias = scatter_about(streams_of[4], (D,), 0.5, 3.0, ((0, 32),), jnp.float32)
    vocab_head = bell_draw_with(streams_of[5], (VOCAB, D), (4 * (D // 9)) ** -0.5, 0.4375, ((0, 256),), (0, 1, 256, 6.0))
    return {"log_hidden": log_hidden, "positions": positions, "offsets": offsets, "head_weight": head_weight, "head_bias": head_bias, "vocab_head": vocab_head}


def silu_slope(preact):
    sigma = jax.nn.sigmoid(preact)
    return sigma * (1.0 + preact * (1.0 - sigma))


def reference(log_hidden, positions, offsets, head_weight, head_bias, vocab_head):
    owner_rows = (jnp.arange(POSITIONS, dtype=jnp.int32) // POS_DEV) * LOG_DEV
    source = (owner_rows + positions).astype(jnp.int32)
    inputs = log_hidden[source]
    targets = log_hidden[(source + offsets).astype(jnp.int32)]
    preact = jnp.dot(inputs, head_weight, preferred_element_type=jnp.float32) + head_bias
    heads = (inputs.astype(jnp.float32) + jax.nn.silu(preact)).astype(jnp.bfloat16)
    teacher = jnp.dot(targets, vocab_head.T, preferred_element_type=jnp.float32)
    student = jnp.dot(heads, vocab_head.T, preferred_element_type=jnp.float32)
    lse_teacher = jnp.log(jnp.sum(jnp.exp(teacher), axis=1, keepdims=True))
    lse_student = jnp.log(jnp.sum(jnp.exp(student), axis=1, keepdims=True))
    log_target = teacher - lse_teacher
    log_student = student - lse_student
    target_prob = jnp.exp(log_target)
    student_prob = jnp.exp(log_student)
    loss = jnp.sum(target_prob * (log_target - log_student)) / POSITIONS
    grad_logits = (student_prob - target_prob).astype(jnp.bfloat16)
    grad_heads = jnp.dot(grad_logits, vocab_head, preferred_element_type=jnp.float32)
    grad_pre = grad_heads * silu_slope(preact)
    grad_bias = jnp.sum(grad_pre, axis=0)
    grad_weight = jnp.dot(inputs.T, grad_pre.astype(jnp.bfloat16), preferred_element_type=jnp.float32)
    return (loss, grad_weight, grad_bias)
```

```python
import jax
import jax.numpy as jnp
from jax import lax
from jax.sharding import PartitionSpec as P

BF16 = jnp.bfloat16
F32 = jnp.float32


def exchange(blocks, axis):
    return lax.all_to_all(blocks, axis, split_axis=0, concat_axis=0, tiled=True)


def gathered(block, axis, count):
    return exchange(jnp.broadcast_to(block[None], (count, *block.shape)), axis)


def thirds(value):
    high = lax.reduce_precision(value, 8, 7)
    middle = lax.reduce_precision(value - high, 8, 7)
    return jnp.stack([high, middle, value - high - middle])


def shards(reps, vocs, log_hidden, positions, offsets, head_weight, head_bias, vocab_head):
    in_width, out_width = head_weight.shape
    own = positions.shape[0]
    count = own * reps
    rows = count // vocs
    voc_index = lax.axis_index("voc")
    inputs = jnp.take(log_hidden, positions, axis=0, mode="clip")
    targets = jnp.take(log_hidden, positions + offsets, axis=0, mode="clip")
    with jax.named_scope("gather_inputs"):
        input_block = lax.dynamic_slice_in_dim(inputs, voc_index * in_width, in_width, 1)
        input_cols = inputs.reshape(own, reps, out_width).transpose(1, 0, 2)
        sent = jnp.concatenate(
            [jnp.broadcast_to(input_block[None], (reps, own, in_width)), input_cols], axis=2
        )
        got = exchange(sent, "rep")
        input_rows = got[:, :, :in_width].reshape(count, in_width)
        residual = got[:, :, in_width:].reshape(count, out_width)
        residual = lax.dynamic_slice_in_dim(residual, voc_index * rows, rows, 0)
    with jax.named_scope("gather_targets"):
        target_block = lax.dynamic_slice_in_dim(targets, voc_index * in_width, in_width, 1)
        target_rows = gathered(target_block, "rep", reps).reshape(count, in_width)
        target_all = lax.all_gather(target_rows, "voc", axis=1, tiled=True)
    with jax.named_scope("head"):
        partial_pre = jnp.dot(input_rows, head_weight, preferred_element_type=F32)
        parts = exchange(partial_pre.reshape(vocs, rows, out_width), "voc")
        preact = jnp.sum(parts, axis=0) + head_bias
        heads = (residual.astype(F32) + jax.nn.silu(preact)).astype(BF16)
    with jax.named_scope("gather_heads"):
        head_rows = gathered(heads, "rep", reps).transpose(1, 0, 2).reshape(rows, -1)
        head_all = lax.all_gather(head_rows, "voc", axis=0, tiled=True)
    contract = (((1,), (1,)), ((), ()))
    with jax.named_scope("logits"):
        teacher = lax.dot_general(vocab_head, target_all, contract, preferred_element_type=F32)
        student = lax.dot_general(vocab_head, head_all, contract, preferred_element_type=F32)
        exp_teacher = jnp.exp(teacher)
        sums = jnp.stack(
            [
                jnp.sum(exp_teacher, axis=0),
                jnp.sum(jnp.exp(student), axis=0),
                jnp.sum(exp_teacher * (teacher - student), axis=0),
                jnp.zeros((count,), F32),
            ]
        ).reshape(8, -1)
    with jax.named_scope("totals"):
        sums = jnp.sum(gathered(sums, "voc", vocs), axis=0)
        sums = jnp.sum(gathered(sums, "rep", reps), axis=0).reshape(4, count)
        log_teacher, log_student = jnp.log(sums[0]), jnp.log(sums[1])
        loss = jnp.sum(sums[2] / sums[0] - log_teacher + log_student) / count
    with jax.named_scope("grad"):
        grad_logits = (jnp.exp(student - log_student) - jnp.exp(teacher - log_teacher)).astype(BF16)
        outer = (((0,), (0,)), ((), ()))
        grad_part = lax.dot_general(
            grad_logits, vocab_head, outer, preferred_element_type=F32
        ).astype(BF16)
    with jax.named_scope("reduce_grad"):
        grad_rows = lax.psum_scatter(grad_part, "voc", scatter_dimension=0, tiled=True)
        sent = grad_rows.reshape(rows, reps, out_width).transpose(1, 0, 2)
        grad_heads = jnp.sum(exchange(sent, "rep").astype(F32), axis=0)
    with jax.named_scope("finish"):
        sigma = jax.nn.sigmoid(preact)
        grad_pre = grad_heads * (sigma * (1.0 + preact * (1.0 - sigma)))
        bias_part = thirds(jnp.sum(grad_pre, axis=0))
        sent = jnp.concatenate(
            [grad_pre, bias_part, jnp.zeros((13, out_width), F32)], axis=0
        ).astype(BF16)
        got = gathered(sent, "voc", vocs)
        grad_all = got[:, :rows].reshape(count, out_width)
        grad_bias = jnp.sum(got[:, rows : rows + 3].astype(F32), axis=(0, 1))
        grad_weight = lax.dot_general(
            input_rows, grad_all, (((0,), (0,)), ((), ())), preferred_element_type=F32
        )
    return (loss, grad_weight, grad_bias)


def solution(mesh):
    reps, vocs = mesh.shape["rep"], mesh.shape["voc"]

    def body(*args):
        return shards(reps, vocs, *args)

    return jax.shard_map(
        body,
        mesh=mesh,
        in_specs=(
            P("rep", None),
            P("rep"),
            P("rep"),
            P("voc", "rep"),
            P("rep"),
            P(("rep", "voc"), None),
        ),
        out_specs=(P(), P("voc", "rep"), P("rep")),
        check_vma=False,
    )
```

```python
import jax
import jax.numpy as jnp
from jax import lax
from jax.sharding import Mesh, PartitionSpec as P

BF16 = jnp.bfloat16
F32 = jnp.float32
REP = ("y", "z")
VOC = ("x", "c")
SIZES = {"y": 4, "z": 8, "x": 4, "c": 2}


def exchange(blocks, axis):
    return lax.all_to_all(blocks, axis, split_axis=0, concat_axis=0, tiled=True)


def gathered(block, axis, count):
    return exchange(jnp.broadcast_to(block[None], (count, *block.shape)), axis)


def swap(block, axis, step):
    return lax.ppermute(block, axis, [(i, i ^ step) for i in range(SIZES[axis])])


def thirds(value):
    high = lax.reduce_precision(value, 8, 7)
    middle = lax.reduce_precision(value - high, 8, 7)
    return jnp.stack([high, middle, value - high - middle])


def from_peers(block, axis):
    return [block] + [swap(block, axis, step) for step in range(1, SIZES[axis])]


def summed(blocks, axis):
    total = blocks[0].astype(F32)
    for step in range(1, SIZES[axis]):
        total = total + swap(blocks[step], axis, step).astype(F32)
    return total.astype(BF16)


def gather_heads(heads):
    rows, width = heads.shape
    half = rows // 2
    lines = gathered(heads, "z", 8).transpose(1, 0, 2).reshape(rows, -1)
    first, second = lines[:half], lines[half:]
    first = jnp.concatenate(from_peers(first, "y"), axis=1)
    second = jnp.concatenate(from_peers(second, "x"), axis=0)
    first_parts = from_peers(first, "x")
    second_parts = from_peers(second, "y")
    mine = jnp.concatenate([*first_parts, jnp.concatenate(second_parts, axis=1)], axis=0)
    return jnp.concatenate([mine, swap(mine, "c", 1)], axis=0)


def scatter_grad(part):
    rows, depth = part.shape
    own, other = part[: rows // 2], part[rows // 2 :]
    mine = (own.astype(F32) + swap(other, "c", 1).astype(F32)).astype(BF16)
    half = rows // 4
    block = half // 4
    width = depth // 4
    first = [mine[i * block : (i + 1) * block] for i in range(4)]
    second = [mine[half:, i * width : (i + 1) * width] for i in range(4)]
    first, second = summed(first, "x"), summed(second, "y")
    first = [first[:, i * width : (i + 1) * width] for i in range(4)]
    second = [second[i * block : (i + 1) * block] for i in range(4)]
    first, second = summed(first, "y"), summed(second, "x")
    lines = jnp.concatenate([first, second], axis=0)
    sent = lines.reshape(2 * block, 8, -1).transpose(1, 0, 2)
    return jnp.sum(exchange(sent, "z").astype(F32), axis=0)


def shards(log_hidden, positions, offsets, head_weight, head_bias, vocab_head):
    reps, vocs = 32, 8
    in_width, out_width = head_weight.shape
    own = positions.shape[0]
    count = own * reps
    rows = count // vocs
    at_x, at_y, at_c = lax.axis_index("x"), lax.axis_index("y"), lax.axis_index("c")
    voc_index = at_x * 2 + at_c
    inputs = jnp.take(log_hidden, positions, axis=0, mode="clip")
    targets = jnp.take(log_hidden, positions + offsets, axis=0, mode="clip")
    with jax.named_scope("gather_targets"):
        target_all = lax.all_gather(targets, REP, axis=0, tiled=True)
    with jax.named_scope("gather_inputs"):
        input_block = lax.dynamic_slice_in_dim(inputs, voc_index * in_width, in_width, 1)
        input_cols = inputs.reshape(own, reps, out_width).transpose(1, 0, 2)
        sent = jnp.concatenate(
            [jnp.broadcast_to(input_block[None], (reps, own, in_width)), input_cols], axis=2
        )
        got = exchange(sent, REP)
        input_rows = got[:, :, :in_width].reshape(count, in_width)
        residual = got[:, :, in_width:].reshape(count, out_width)
        residual = lax.dynamic_slice_in_dim(residual, voc_index * rows, rows, 0)
    with jax.named_scope("turn_columns"):
        quarter = vocab_head.shape[1] // 4
        turned = jnp.concatenate(
            [
                lax.dynamic_slice_in_dim(vocab_head, (at_y ^ step) * quarter, quarter, 1)
                for step in range(4)
            ],
            axis=1,
        )
    with jax.named_scope("head"):
        partial_pre = jnp.dot(input_rows, head_weight, preferred_element_type=F32)
        parts = exchange(partial_pre.reshape(vocs, rows, out_width), VOC)
        preact = jnp.sum(parts, axis=0) + head_bias
        heads = (residual.astype(F32) + jax.nn.silu(preact)).astype(BF16)
    with jax.named_scope("gather_heads"):
        head_all = gather_heads(heads)
    steps = jnp.arange(16)
    order = ((at_x ^ (steps % 4)) * 2 + (at_c ^ (steps // 8))) * 2 + (steps // 4) % 2
    with jax.named_scope("turn_targets"):
        target_all = target_all.reshape(16, count // 16, -1)[order].reshape(count, -1)
    contract = (((1,), (1,)), ((), ()))
    with jax.named_scope("logits"):
        teacher = lax.dot_general(vocab_head, target_all, contract, preferred_element_type=F32)
        student = lax.dot_general(turned, head_all, contract, preferred_element_type=F32)
        exp_teacher = jnp.exp(teacher)
        sums = jnp.stack(
            [
                jnp.sum(exp_teacher, axis=0),
                jnp.sum(jnp.exp(student), axis=0),
                jnp.sum(exp_teacher * (teacher - student), axis=0),
                jnp.zeros((count,), F32),
            ]
        )
        back = (steps // 2 % 2 ^ at_c) * 8 + steps % 2 * 4 + (steps // 4 ^ at_x)
        sums = sums.reshape(4, 16, -1)[:, back].reshape(8, -1)
    with jax.named_scope("totals"):
        sums = jnp.sum(gathered(sums, VOC, vocs), axis=0)
        sums = jnp.sum(gathered(sums, REP, reps), axis=0).reshape(4, count)
        log_teacher, log_student = jnp.log(sums[0]), jnp.log(sums[1])
        loss = jnp.sum(sums[2] / sums[0] - log_teacher + log_student) / count
        log_teacher = log_teacher.reshape(16, -1)[order].reshape(count)
        log_student = log_student.reshape(16, -1)[order].reshape(count)
    with jax.named_scope("grad"):
        grad_logits = (jnp.exp(student - log_student) - jnp.exp(teacher - log_teacher)).astype(BF16)
        outer = (((0,), (0,)), ((), ()))
        grad_part = lax.dot_general(
            grad_logits, turned, outer, preferred_element_type=F32
        ).astype(BF16)
    with jax.named_scope("reduce_grad"):
        grad_heads = scatter_grad(grad_part)
    with jax.named_scope("finish"):
        sigma = jax.nn.sigmoid(preact)
        grad_pre = grad_heads * (sigma * (1.0 + preact * (1.0 - sigma)))
        bias_part = thirds(jnp.sum(grad_pre, axis=0))
        sent = jnp.concatenate(
            [grad_pre, bias_part, jnp.zeros((13, out_width), F32)], axis=0
        ).astype(BF16)
        got = gathered(sent, VOC, vocs)
        grad_all = got[:, :rows].reshape(count, out_width)
        grad_bias = jnp.sum(got[:, rows : rows + 3].astype(F32), axis=(0, 1))
        grad_weight = lax.dot_general(
            input_rows, grad_all, (((0,), (0,)), ((), ())), preferred_element_type=F32
        )
    return (loss, grad_weight, grad_bias)


def solution(mesh):
    fine = Mesh(mesh.devices.reshape(tuple(SIZES.values())), tuple(SIZES))
    return jax.shard_map(
        shards,
        mesh=fine,
        in_specs=(
            P(REP, None),
            P(REP),
            P(REP),
            P(VOC, REP),
            P(REP),
            P((*REP, *VOC), None),
        ),
        out_specs=(P(), P(VOC, REP), P(REP)),
        check_vma=False,
    )
```

```python
import jax
import jax.numpy as jnp
from jax import lax
from jax.experimental import pallas as pl
from jax.experimental.pallas import tpu as pltpu
from jax.sharding import Mesh, PartitionSpec as P

BF16 = jnp.bfloat16
F32 = jnp.float32
REP = ("y", "z")
VOC = ("x", "c")
CHUNKS = 4
VMEM_LIMIT = 32 * 1024 * 1024
HEAD_COST = 45_000_000_000
SIZES = {"y": 4, "z": 8, "x": 4, "c": 2}


def exchange(blocks, axis):
    return lax.all_to_all(blocks, axis, split_axis=0, concat_axis=0, tiled=True)


def gathered(block, axis, count):
    return exchange(jnp.broadcast_to(block[None], (count, *block.shape)), axis)


def swap(block, axis, step):
    return lax.ppermute(block, axis, [(i, i ^ step) for i in range(SIZES[axis])])


def thirds(value):
    high = lax.reduce_precision(value, 8, 7)
    middle = lax.reduce_precision(value - high, 8, 7)
    return jnp.stack([high, middle, value - high - middle])


def from_peers(block, axis):
    return [block] + [swap(block, axis, step) for step in range(1, SIZES[axis])]


def summed(blocks, axis):
    total = blocks[0].astype(F32)
    for step in range(1, SIZES[axis]):
        total = total + swap(blocks[step], axis, step).astype(F32)
    return total.astype(BF16)


def cost(flops, bytes_accessed, transcendentals=0):
    return pl.CostEstimate(
        flops=flops, bytes_accessed=bytes_accessed, transcendentals=transcendentals
    )


def whole(shape):
    return pl.BlockSpec(shape, lambda *at: (0,) * len(shape))


def scalar_call(kernel, steps, in_specs, out_specs, out_shape, estimate, scratch=()):
    return pl.pallas_call(
        kernel,
        grid_spec=pltpu.PrefetchScalarGridSpec(
            num_scalar_prefetch=1,
            grid=(steps,),
            in_specs=in_specs,
            out_specs=out_specs,
            scratch_shapes=scratch,
        ),
        out_shape=out_shape,
        compiler_params=pltpu.CompilerParams(vmem_limit_bytes=VMEM_LIMIT),
        cost_estimate=estimate,
    )


NT = (((1,), (1,)), ((), ()))


def teacher_kernel(place, target_ref, vocab_ref, out_ref, total):
    step = pl.program_id(0)
    product = lax.dot_general(
        target_ref[...], vocab_ref[...], NT, preferred_element_type=F32
    )

    @pl.when(step == 0)
    def _():
        total[...] = product

    @pl.when(step > 0)
    def _():
        total[...] += product

    @pl.when(step == CHUNKS - 1)
    def _():
        for at in range(16):
            start = pl.multiple_of(place[at] * 16, 16)
            out_ref[at * 16 : (at + 1) * 16] = total[pl.ds(start, 16)]


def teacher_logits(place, target_all, vocab_head):
    (count, depth), entries = target_all.shape, vocab_head.shape[0]
    width = depth // CHUNKS
    return scalar_call(
        teacher_kernel,
        CHUNKS,
        [
            pl.BlockSpec((count, width), lambda step, place: (0, step)),
            pl.BlockSpec((entries, width), lambda step, place: (0, step)),
        ],
        whole((count, entries)),
        jax.ShapeDtypeStruct((count, entries), F32),
        cost(2 * count * entries * depth, 2 * (count + entries) * depth),
        [pltpu.VMEM((count, entries), F32)],
    )(place, target_all, vocab_head)


def student_kernel(place, *refs):
    firsts, seconds = refs[:8], refs[8:16]
    vocab_ref, teacher_ref, out_ref, sums_ref, turned = refs[16:]
    step = pl.program_id(0)

    for at in range(CHUNKS):

        @pl.when(step == at)
        def _():
            rows = []
            for core in range(2):
                rows += [ref[...] for ref in firsts[4 * core : 4 * core + 4]]
                rows.append(seconds[4 * core + at][...])
            product = lax.dot_general(
                jnp.concatenate(rows, axis=0), vocab_ref[...], NT, preferred_element_type=F32
            )
            if at == 0:
                out_ref[...] = product
            else:
                out_ref[...] += product

    @pl.when(step == CHUNKS - 1)
    def _():
        student, teacher = out_ref[...], teacher_ref[...]
        exp_teacher = jnp.exp(teacher)
        columns = [
            jnp.sum(exp_teacher, axis=1, keepdims=True),
            jnp.sum(jnp.exp(student), axis=1, keepdims=True),
            jnp.sum(exp_teacher * (teacher - student), axis=1, keepdims=True),
        ]
        lane = lax.broadcasted_iota(jnp.int32, turned.shape, 1)
        table = jnp.zeros(turned.shape, F32)
        for at, column in enumerate(columns):
            table = jnp.where(lane == at, column, table)
        for at in range(16):
            start = pl.multiple_of(place[at] * 16, 16)
            turned[pl.ds(start, 16)] = table[at * 16 : (at + 1) * 16]
        sums_ref[...] = turned[...].T[:8]


def student_logits(place, firsts, seconds, vocab_head, teacher):
    count, entries = teacher.shape
    depth = vocab_head.shape[1]
    width = depth // CHUNKS
    return scalar_call(
        student_kernel,
        CHUNKS,
        [pl.BlockSpec((firsts[0].shape[0], width), lambda step, place: (0, step))] * 8
        + [whole(seconds[0].shape)] * 8
        + [
            pl.BlockSpec((entries, width), lambda step, place: (0, step ^ place[16])),
            whole((count, entries)),
        ],
        [whole((count, entries)), whole((8, count))],
        [
            jax.ShapeDtypeStruct((count, entries), F32),
            jax.ShapeDtypeStruct((8, count), F32),
        ],
        cost(2 * count * entries * depth, 2 * (count + entries) * depth, 2 * count * entries),
        [pltpu.VMEM((count, 128), F32)],
    )(place, *firsts, *seconds, vocab_head, teacher)


def grad_kernel(
    place, teacher_ref, student_ref, logs_ref, vocab_ref, own_ref, other_ref, table, turned, grad
):
    count = grad.shape[0]

    @pl.when(pl.program_id(0) == 0)
    def _():
        table[...] = jnp.concatenate([logs_ref[...], jnp.zeros((120, count), F32)], axis=0).T
        for at in range(16):
            start = pl.multiple_of(place[at] * 16, 16)
            turned[at * 16 : (at + 1) * 16] = table[pl.ds(start, 16)]
        student = jnp.exp(student_ref[...] - turned[:, 1:2])
        teacher = jnp.exp(teacher_ref[...] - turned[:, 0:1])
        grad[...] = (student - teacher).astype(BF16)

    product = jnp.dot(grad[...], vocab_ref[...], preferred_element_type=F32).astype(BF16)
    own_ref[...] = product[: count // 2]
    other_ref[...] = product[count // 2 :]


def grad_rows(place, teacher, student, logs, vocab_head):
    count, entries = teacher.shape
    depth = vocab_head.shape[1]
    width = depth // CHUNKS
    half = pl.BlockSpec((count // 2, width), lambda step, place: (0, step))
    return scalar_call(
        grad_kernel,
        CHUNKS,
        [
            whole((count, entries)),
            whole((count, entries)),
            whole((8, count)),
            pl.BlockSpec((entries, width), lambda step, place: (0, step ^ place[16])),
        ],
        [half, half],
        [jax.ShapeDtypeStruct((count // 2, depth), BF16)] * 2,
        cost(2 * count * entries * depth, 2 * (count + entries) * depth, 2 * count * entries),
        [
            pltpu.VMEM((count, 128), F32),
            pltpu.VMEM((count, 128), F32),
            pltpu.VMEM((count, entries), BF16),
        ],
    )(place, teacher, student, logs, vocab_head)


def join_kernel(*refs):
    firsts, seconds, (first_ref, second_ref) = refs[:4], refs[4:8], refs[8:]
    (rows, width), (block, _) = firsts[0].shape, seconds[0].shape
    for at in range(4):
        first_ref[:, at * width : (at + 1) * width] = firsts[at][...]
        second_ref[at * block : (at + 1) * block] = seconds[at][...]


def join(firsts, seconds):
    (rows, width), (block, across) = firsts[0].shape, seconds[0].shape
    return pl.pallas_call(
        join_kernel,
        out_shape=[
            jax.ShapeDtypeStruct((rows, 4 * width), BF16),
            jax.ShapeDtypeStruct((4 * block, across), BF16),
        ],
        compiler_params=pltpu.CompilerParams(vmem_limit_bytes=VMEM_LIMIT),
        cost_estimate=cost(0, 16 * rows * width),
    )(*firsts, *seconds)


def head_kernel(rows_ref, weight_ref, out_ref):
    out_ref[...] = jnp.dot(rows_ref[...], weight_ref[...], preferred_element_type=F32)


def head_partial(rows, weight):
    return pl.pallas_call(
        head_kernel,
        out_shape=jax.ShapeDtypeStruct((rows.shape[0], weight.shape[1]), F32),
        compiler_params=pltpu.CompilerParams(vmem_limit_bytes=VMEM_LIMIT),
        cost_estimate=cost(HEAD_COST, 2 * (rows.size + weight.size)),
    )(rows, weight)


def gather_heads(heads):
    rows, width = heads.shape
    half = rows // 2
    lines = gathered(heads, "z", 8).transpose(1, 0, 2).reshape(rows, -1)
    first, second = join(from_peers(lines[:half], "y"), from_peers(lines[half:], "x"))
    firsts, seconds = from_peers(first, "x"), from_peers(second, "y")
    firsts = firsts + [swap(block, "c", 1) for block in firsts]
    seconds = seconds + [swap(block, "c", 1) for block in seconds]
    return firsts, seconds


def scatter_grad(own, other):
    rows, depth = own.shape
    mine = (own.astype(F32) + swap(other, "c", 1).astype(F32)).astype(BF16)
    half = rows // 2
    block = half // 4
    width = depth // 4
    first = [mine[i * block : (i + 1) * block] for i in range(4)]
    second = [mine[half:, i * width : (i + 1) * width] for i in range(4)]
    first, second = summed(first, "x"), summed(second, "y")
    first = [first[:, i * width : (i + 1) * width] for i in range(4)]
    second = [second[i * block : (i + 1) * block] for i in range(4)]
    first, second = summed(first, "y"), summed(second, "x")
    lines = jnp.concatenate([first, second], axis=0)
    sent = lines.reshape(2 * block, 8, -1).transpose(1, 0, 2)
    return jnp.sum(exchange(sent, "z").astype(F32), axis=0)


def shards(log_hidden, positions, offsets, head_weight, head_bias, vocab_head):
    reps, vocs = 32, 8
    in_width, out_width = head_weight.shape
    own = positions.shape[0]
    count = own * reps
    rows = count // vocs
    at_x, at_y, at_c = lax.axis_index("x"), lax.axis_index("y"), lax.axis_index("c")
    voc_index = at_x * 2 + at_c
    inputs = jnp.take(log_hidden, positions, axis=0, mode="clip")
    targets = jnp.take(log_hidden, positions + offsets, axis=0, mode="clip")
    with jax.named_scope("gather_targets"):
        target_all = lax.all_gather(targets, REP, axis=0, tiled=True)
    with jax.named_scope("gather_inputs"):
        input_block = lax.dynamic_slice_in_dim(inputs, voc_index * in_width, in_width, 1)
        input_cols = inputs.reshape(own, reps, out_width).transpose(1, 0, 2)
        sent = jnp.concatenate(
            [jnp.broadcast_to(input_block[None], (reps, own, in_width)), input_cols], axis=2
        )
        got = exchange(sent, REP)
        input_rows = got[:, :, :in_width].reshape(count, in_width)
        residual = got[:, :, in_width:].reshape(count, out_width)
        residual = lax.dynamic_slice_in_dim(residual, voc_index * rows, rows, 0)
    with jax.named_scope("head"):
        partial_pre = head_partial(input_rows, head_weight)
        parts = exchange(partial_pre.reshape(vocs, rows, out_width), VOC)
        preact = jnp.sum(parts, axis=0) + head_bias
        heads = (residual.astype(F32) + jax.nn.silu(preact)).astype(BF16)
    steps = jnp.arange(16)
    order = ((at_x ^ (steps % 4)) * 2 + (at_c ^ (steps // 8))) * 2 + (steps // 4) % 2
    place = jnp.concatenate([order, at_y[None]]).astype(jnp.int32)
    with jax.named_scope("teacher"):
        teacher = teacher_logits(place, target_all, vocab_head)
    with jax.named_scope("gather_heads"):
        firsts, seconds = gather_heads(heads)
    with jax.named_scope("student"):
        student, sums = student_logits(place, firsts, seconds, vocab_head, teacher)
    with jax.named_scope("totals"):
        sums = jnp.sum(gathered(sums, VOC, vocs), axis=0)
        sums = jnp.sum(gathered(sums, REP, reps), axis=0)
        logs = jnp.log(sums)
        loss = jnp.sum(sums[2] / sums[0] - logs[0] + logs[1]) / count
    with jax.named_scope("grad"):
        own_rows, other_rows = grad_rows(place, teacher, student, logs, vocab_head)
    with jax.named_scope("reduce_grad"):
        grad_heads = scatter_grad(own_rows, other_rows)
    with jax.named_scope("finish"):
        sigma = jax.nn.sigmoid(preact)
        grad_pre = grad_heads * (sigma * (1.0 + preact * (1.0 - sigma)))
        bias_part = thirds(jnp.sum(grad_pre, axis=0))
        sent = jnp.concatenate(
            [grad_pre, bias_part, jnp.zeros((13, out_width), F32)], axis=0
        ).astype(BF16)
        got = gathered(sent, VOC, vocs)
        grad_all = got[:, :rows].reshape(count, out_width)
        grad_bias = jnp.sum(got[:, rows : rows + 3].astype(F32), axis=(0, 1))
        grad_weight = lax.dot_general(
            input_rows, grad_all, (((0,), (0,)), ((), ())), preferred_element_type=F32
        )
    return (loss, grad_weight, grad_bias)


def solution(mesh):
    fine = Mesh(mesh.devices.reshape(tuple(SIZES.values())), tuple(SIZES))
    return jax.shard_map(
        shards,
        mesh=fine,
        in_specs=(
            P(REP, None),
            P(REP),
            P(REP),
            P(VOC, REP),
            P(REP),
            P((*REP, *VOC), None),
        ),
        out_specs=(P(), P(VOC, REP), P(REP)),
        check_vma=False,
    )
```

```python
import functools

import jax
import jax.numpy as jnp
from jax import lax
from jax.experimental import pallas as pl
from jax.experimental.pallas import tpu as pltpu
from jax.sharding import Mesh, PartitionSpec as P

BF16 = jnp.bfloat16
F32 = jnp.float32
REP = ("y", "z")
VOC = ("x", "c")
CHUNKS = 4
PADDED = 512
LIMIT = 24 * 1024 * 1024
HEAD_COST = 45_000_000_000
SIZES = {"y": 4, "z": 8, "x": 4, "c": 2}


def exchange(blocks, axis):
    return lax.all_to_all(blocks, axis, split_axis=0, concat_axis=0, tiled=True)


def gathered(block, axis, count):
    return exchange(jnp.broadcast_to(block[None], (count, *block.shape)), axis)


def swap(block, axis, step):
    return lax.ppermute(block, axis, [(i, i ^ step) for i in range(SIZES[axis])])


def thirds(value):
    high = lax.reduce_precision(value, 8, 7)
    middle = lax.reduce_precision(value - high, 8, 7)
    return jnp.stack([high, middle, value - high - middle])


def from_peers(block, axis):
    return [block] + [swap(block, axis, step) for step in range(1, SIZES[axis])]


def summed(blocks, axis):
    total = blocks[0].astype(F32)
    for step in range(1, SIZES[axis]):
        total = total + swap(blocks[step], axis, step).astype(F32)
    return total.astype(BF16)


def cost(flops, bytes_accessed, transcendentals=0):
    return pl.CostEstimate(
        flops=flops, bytes_accessed=bytes_accessed, transcendentals=transcendentals
    )


def local_call(kernel, out_shape, estimate, scratch=(), limit=LIMIT, scalars=True):
    def call(*operands):
        specs = [pl.BlockSpec(memory_space=pltpu.VMEM)] * len(operands)
        if scalars:
            specs[0] = pl.BlockSpec(memory_space=pltpu.SMEM)
        return pl.pallas_call(
            kernel,
            in_specs=specs,
            out_specs=jax.tree.map(lambda _: pl.BlockSpec(memory_space=pltpu.VMEM), out_shape),
            out_shape=out_shape,
            scratch_shapes=scratch,
            compiler_params=pltpu.CompilerParams(vmem_limit_bytes=limit),
            cost_estimate=estimate,
        )(*operands)

    return call


def shape(*sizes, dtype=F32):
    return jax.ShapeDtypeStruct(sizes, dtype)


def prepare_kernel(place, vocab_ref, across_ref, down_ref, wide):
    entries, depth = vocab_ref.shape
    width = depth // CHUNKS
    wide[...] = jnp.zeros(wide.shape, F32)
    for at in range(CHUNKS):
        start = pl.multiple_of((place[16] ^ at) * width, width)
        wide[:entries] = vocab_ref[:, pl.ds(start, width)].astype(F32)
        block = wide[...]
        across_ref[:, at * width : (at + 1) * width] = block.astype(BF16)
        down_ref[at * width : (at + 1) * width] = block.T.astype(BF16)


def prepare(place, vocab_head):
    depth = vocab_head.shape[1]
    return local_call(
        prepare_kernel,
        [shape(PADDED, depth, dtype=BF16), shape(depth, PADDED, dtype=BF16)],
        cost(0, 6 * PADDED * depth),
        [pltpu.VMEM((PADDED, depth // CHUNKS), F32)],
    )(place, vocab_head)


def teacher_kernel(place, target_ref, down_ref, out_ref, total):
    width = down_ref.shape[0] // CHUNKS
    for at in range(CHUNKS):
        start = pl.multiple_of((place[16] ^ at) * width, width)
        product = jnp.dot(
            target_ref[:, pl.ds(start, width)],
            down_ref[at * width : (at + 1) * width],
            preferred_element_type=F32,
        )
        total[...] = product if at == 0 else total[...] + product
    for at in range(16):
        start = pl.multiple_of(place[at] * 16, 16)
        out_ref[at * 16 : (at + 1) * 16] = total[pl.ds(start, 16)]


def teacher_logits(place, target_all, down):
    count, depth = target_all.shape
    return local_call(
        teacher_kernel,
        shape(count, PADDED),
        cost(2 * count * PADDED * depth, 2 * (count + PADDED) * depth),
        [pltpu.VMEM((count, PADDED), F32)],
    )(place, target_all, down)


def student_part(entries, core, firsts, seconds, teacher_ref, down_ref, out_ref):
    width = down_ref.shape[0] // CHUNKS
    rows = out_ref.shape[0]
    for at in range(CHUNKS):
        blocks = [ref[:, at * width : (at + 1) * width] for ref in firsts] + [seconds[at][...]]
        product = jnp.dot(
            jnp.concatenate(blocks, axis=0),
            down_ref[at * width : (at + 1) * width],
            preferred_element_type=F32,
        )
        out_ref[...] = product if at == 0 else out_ref[...] + product
    student, teacher = out_ref[...], teacher_ref[core * rows : (core + 1) * rows]
    real = lax.broadcasted_iota(jnp.int32, student.shape, 1) < entries
    exp_teacher = jnp.where(real, jnp.exp(teacher), 0.0)
    columns = [
        jnp.sum(exp_teacher, axis=1, keepdims=True),
        jnp.sum(jnp.where(real, jnp.exp(student), 0.0), axis=1, keepdims=True),
        jnp.sum(exp_teacher * (teacher - student), axis=1, keepdims=True),
    ]
    lane = lax.broadcasted_iota(jnp.int32, (rows, 128), 1)
    table = jnp.zeros((rows, 128), F32)
    for at, column in enumerate(columns):
        table = jnp.where(lane == at, column, table)
    return table


def own_student_kernel(entries, *refs):
    teacher_ref, down_ref, out_ref, table_ref = refs[8:]
    table_ref[...] = student_part(
        entries, 0, refs[:4], refs[4:8], teacher_ref, down_ref, out_ref
    )


def other_student_kernel(entries, place, *refs):
    teacher_ref, down_ref, own_ref, out_ref, sums_ref, turned = refs[8:]
    other = student_part(entries, 1, refs[:4], refs[4:8], teacher_ref, down_ref, out_ref)
    for core, table in enumerate((own_ref[...], other)):
        for at in range(8):
            start = pl.multiple_of(place[core * 8 + at] * 16, 16)
            turned[pl.ds(start, 16)] = table[at * 16 : (at + 1) * 16]
    sums_ref[...] = turned[...].T[:8]


def own_student(entries, blocks, teacher, down):
    rows = teacher.shape[0] // 2
    return local_call(
        functools.partial(own_student_kernel, entries),
        [shape(rows, PADDED), shape(rows, 128)],
        cost(2 * rows * down.size, 2 * down.size, 2 * rows * PADDED),
        scalars=False,
    )(*blocks, teacher, down)


def other_student(entries, place, blocks, teacher, down, table):
    rows = teacher.shape[0] // 2
    return local_call(
        functools.partial(other_student_kernel, entries),
        [shape(rows, PADDED), shape(8, 2 * rows)],
        cost(2 * rows * down.size, 2 * down.size, 2 * rows * PADDED),
        [pltpu.VMEM((2 * rows, 128), F32)],
    )(place, *blocks, teacher, down, table)


def grad_kernel(core, place, teacher_ref, student_ref, logs_ref, across_ref, out_ref, table, turned):
    rows, depth = out_ref.shape
    width = depth // CHUNKS
    table[...] = jnp.concatenate(
        [logs_ref[...], jnp.zeros((120, 2 * rows), F32)], axis=0
    ).T
    for at in range(8):
        start = pl.multiple_of(place[core * 8 + at] * 16, 16)
        turned[at * 16 : (at + 1) * 16] = table[pl.ds(start, 16)]
    student = jnp.exp(student_ref[...] - turned[:, 1:2])
    teacher = jnp.exp(teacher_ref[core * rows : (core + 1) * rows] - turned[:, 0:1])
    grad = (student - teacher).astype(BF16)
    for at in range(CHUNKS):
        columns = slice(at * width, (at + 1) * width)
        out_ref[:, columns] = jnp.dot(
            grad, across_ref[:, columns], preferred_element_type=F32
        ).astype(BF16)


def grad_rows(core, place, teacher, student, logs, across):
    rows, depth = student.shape[0], across.shape[1]
    return local_call(
        functools.partial(grad_kernel, core),
        shape(rows, depth, dtype=BF16),
        cost(2 * rows * across.size, 2 * across.size, 2 * rows * PADDED),
        [pltpu.VMEM((2 * rows, 128), F32), pltpu.VMEM((rows, 128), F32)],
    )(place, teacher, student, logs, across)


def pass_kernel(*refs):
    pass


def settled(blocks):
    return pl.pallas_call(
        pass_kernel,
        in_specs=[pl.BlockSpec(memory_space=pl.ANY)] * len(blocks),
        out_specs=[pl.BlockSpec(memory_space=pl.ANY)] * len(blocks),
        out_shape=[jax.ShapeDtypeStruct(block.shape, block.dtype) for block in blocks],
        input_output_aliases={at: at for at in range(len(blocks))},
        cost_estimate=cost(0, 0),
    )(*blocks)


def join_kernel(*refs):
    firsts, seconds, (first_ref, second_ref) = refs[:4], refs[4:8], refs[8:]
    (rows, width), (block, _) = firsts[0].shape, seconds[0].shape
    for at in range(4):
        first_ref[:, at * width : (at + 1) * width] = firsts[at][...]
        second_ref[at * block : (at + 1) * block] = seconds[at][...]


def join(firsts, seconds):
    (rows, width), (block, across) = firsts[0].shape, seconds[0].shape
    return pl.pallas_call(
        join_kernel,
        out_shape=[
            jax.ShapeDtypeStruct((rows, 4 * width), BF16),
            jax.ShapeDtypeStruct((4 * block, across), BF16),
        ],
        compiler_params=pltpu.CompilerParams(vmem_limit_bytes=LIMIT),
        cost_estimate=cost(0, 16 * rows * width),
    )(*firsts, *seconds)


def head_kernel(rows_ref, weight_ref, down_ref, out_ref):
    out_ref[...] = jnp.dot(rows_ref[...], weight_ref[...], preferred_element_type=F32)


def head_partial(rows, weight, down):
    return pl.pallas_call(
        head_kernel,
        in_specs=[pl.BlockSpec(memory_space=pltpu.VMEM)] * 2 + [pl.BlockSpec(memory_space=pl.ANY)],
        out_shape=jax.ShapeDtypeStruct((rows.shape[0], weight.shape[1]), F32),
        compiler_params=pltpu.CompilerParams(vmem_limit_bytes=LIMIT),
        cost_estimate=cost(HEAD_COST, 2 * (rows.size + weight.size)),
    )(rows, weight, down)


def gather_heads(heads):
    rows, width = heads.shape
    half = rows // 2
    lines = gathered(heads, "z", 8).transpose(1, 0, 2).reshape(rows, -1)
    first, second = join(from_peers(lines[:half], "y"), from_peers(lines[half:], "x"))
    blocks = settled(from_peers(first, "x") + from_peers(second, "y"))
    return blocks, [swap(block, "c", 1) for block in blocks]


def scatter_grad(own, other):
    rows, depth = own.shape
    mine = (own.astype(F32) + swap(other, "c", 1).astype(F32)).astype(BF16)
    half = rows // 2
    block = half // 4
    width = depth // 4
    first = [mine[i * block : (i + 1) * block] for i in range(4)]
    second = [mine[half:, i * width : (i + 1) * width] for i in range(4)]
    first, second = summed(first, "x"), summed(second, "y")
    first = [first[:, i * width : (i + 1) * width] for i in range(4)]
    second = [second[i * block : (i + 1) * block] for i in range(4)]
    first, second = summed(first, "y"), summed(second, "x")
    lines = jnp.concatenate([first, second], axis=0)
    sent = lines.reshape(2 * block, 8, -1).transpose(1, 0, 2)
    return jnp.sum(exchange(sent, "z").astype(F32), axis=0)


def shards(log_hidden, positions, offsets, head_weight, head_bias, vocab_head):
    reps, vocs = 32, 8
    in_width, out_width = head_weight.shape
    own = positions.shape[0]
    count = own * reps
    rows = count // vocs
    at_x, at_y, at_c = lax.axis_index("x"), lax.axis_index("y"), lax.axis_index("c")
    voc_index = at_x * 2 + at_c
    inputs = jnp.take(log_hidden, positions, axis=0, mode="clip")
    targets = jnp.take(log_hidden, positions + offsets, axis=0, mode="clip")
    with jax.named_scope("gather_targets"):
        target_all = lax.all_gather(targets, REP, axis=0, tiled=True)
    with jax.named_scope("gather_inputs"):
        input_block = lax.dynamic_slice_in_dim(inputs, voc_index * in_width, in_width, 1)
        input_cols = inputs.reshape(own, reps, out_width).transpose(1, 0, 2)
        sent = jnp.concatenate(
            [jnp.broadcast_to(input_block[None], (reps, own, in_width)), input_cols], axis=2
        )
        got = exchange(sent, REP)
        input_rows = got[:, :, :in_width].reshape(count, in_width)
        residual = got[:, :, in_width:].reshape(count, out_width)
        residual = lax.dynamic_slice_in_dim(residual, voc_index * rows, rows, 0)
    steps = jnp.arange(16)
    order = ((at_x ^ (steps % 4)) * 2 + (at_c ^ (steps // 8))) * 2 + (steps // 4) % 2
    place = jnp.concatenate([order, at_y[None]]).astype(jnp.int32)
    with jax.named_scope("prepare"):
        across, down = prepare(place, vocab_head)
    with jax.named_scope("head"):
        partial_pre = head_partial(input_rows, head_weight, down)
        parts = exchange(partial_pre.reshape(vocs, rows, out_width), VOC)
        preact = jnp.sum(parts, axis=0) + head_bias
        heads = (residual.astype(F32) + jax.nn.silu(preact)).astype(BF16)
    with jax.named_scope("teacher"):
        teacher = teacher_logits(place, target_all, down)
    with jax.named_scope("gather_heads"):
        own_blocks, other_blocks = gather_heads(heads)
    with jax.named_scope("student"):
        entries = vocab_head.shape[0]
        own_logits, table = own_student(entries, own_blocks, teacher, down)
        other_logits, sums = other_student(entries, place, other_blocks, teacher, down, table)
    with jax.named_scope("totals"):
        sums = jnp.sum(gathered(sums, VOC, vocs), axis=0)
        sums = jnp.sum(gathered(sums, REP, reps), axis=0)
        logs = jnp.log(sums)
        loss = jnp.sum(sums[2] / sums[0] - logs[0] + logs[1]) / count
    with jax.named_scope("grad"):
        other_rows = grad_rows(1, place, teacher, other_logits, logs, across)
        own_rows = grad_rows(0, place, teacher, own_logits, logs, across)
    with jax.named_scope("reduce_grad"):
        grad_heads = scatter_grad(own_rows, other_rows)
    with jax.named_scope("finish"):
        sigma = jax.nn.sigmoid(preact)
        grad_pre = grad_heads * (sigma * (1.0 + preact * (1.0 - sigma)))
        bias_part = thirds(jnp.sum(grad_pre, axis=0))
        sent = jnp.concatenate(
            [grad_pre, bias_part, jnp.zeros((13, out_width), F32)], axis=0
        ).astype(BF16)
        got = gathered(sent, VOC, vocs)
        grad_all = got[:, :rows].reshape(count, out_width)
        grad_bias = jnp.sum(got[:, rows : rows + 3].astype(F32), axis=(0, 1))
        grad_weight = lax.dot_general(
            input_rows, grad_all, (((0,), (0,)), ((), ())), preferred_element_type=F32
        )
    return (loss, grad_weight, grad_bias)


def solution(mesh):
    fine = Mesh(mesh.devices.reshape(tuple(SIZES.values())), tuple(SIZES))
    return jax.shard_map(
        shards,
        mesh=fine,
        in_specs=(
            P(REP, None),
            P(REP),
            P(REP),
            P(VOC, REP),
            P(REP),
            P((*REP, *VOC), None),
        ),
        out_specs=(P(), P(VOC, REP), P(REP)),
        check_vma=False,
    )
```

```python
import functools

import jax
import jax.numpy as jnp
from jax import lax
from jax.experimental import pallas as pl
from jax.experimental.pallas import tpu as pltpu
from jax.sharding import Mesh, PartitionSpec as P

BF16 = jnp.bfloat16
F32 = jnp.float32
REP = ("y", "z")
VOC = ("x", "c")
CHUNKS = 4
PADDED = 512
LIMIT = 24 * 1024 * 1024
HEAD_COST = 45_000_000_000
SIZES = {"y": 4, "z": 8, "x": 4, "c": 2}


def exchange(blocks, axis):
    return lax.all_to_all(blocks, axis, split_axis=0, concat_axis=0, tiled=True)


def gathered(block, axis, count):
    return exchange(jnp.broadcast_to(block[None], (count, *block.shape)), axis)


def swap(block, axis, step):
    return lax.ppermute(block, axis, [(i, i ^ step) for i in range(SIZES[axis])])


def thirds(value):
    high = lax.reduce_precision(value, 8, 7)
    middle = lax.reduce_precision(value - high, 8, 7)
    return jnp.stack([high, middle, value - high - middle])


def from_peers(block, axis):
    return [block] + [swap(block, axis, step) for step in range(1, SIZES[axis])]


def summed(blocks, axis):
    total = blocks[0].astype(F32)
    for step in range(1, SIZES[axis]):
        total = total + swap(blocks[step], axis, step).astype(F32)
    return total.astype(BF16)


def cost(flops, bytes_accessed, transcendentals=0):
    return pl.CostEstimate(
        flops=flops, bytes_accessed=bytes_accessed, transcendentals=transcendentals
    )


def local_call(kernel, out_shape, estimate, scratch=(), limit=LIMIT, scalars=True):
    def call(*operands):
        specs = [pl.BlockSpec(memory_space=pltpu.VMEM)] * len(operands)
        if scalars:
            specs[0] = pl.BlockSpec(memory_space=pltpu.SMEM)
        return pl.pallas_call(
            kernel,
            in_specs=specs,
            out_specs=jax.tree.map(lambda _: pl.BlockSpec(memory_space=pltpu.VMEM), out_shape),
            out_shape=out_shape,
            scratch_shapes=scratch,
            compiler_params=pltpu.CompilerParams(vmem_limit_bytes=limit),
            cost_estimate=estimate,
        )(*operands)

    return call


def shape(*sizes, dtype=F32):
    return jax.ShapeDtypeStruct(sizes, dtype)


def prepare_kernel(place, vocab_ref, across_ref, down_ref, done_ref, wide):
    done_ref[...] = jnp.zeros(done_ref.shape, F32)
    entries, depth = vocab_ref.shape
    width = depth // CHUNKS
    wide[...] = jnp.zeros(wide.shape, F32)
    for at in range(CHUNKS):
        start = pl.multiple_of((place[16] ^ at) * width, width)
        wide[:entries] = vocab_ref[:, pl.ds(start, width)].astype(F32)
        block = wide[...]
        across_ref[:, at * width : (at + 1) * width] = block.astype(BF16)
        down_ref[at * width : (at + 1) * width] = block.T.astype(BF16)


def prepare(place, vocab_head):
    depth = vocab_head.shape[1]
    return local_call(
        prepare_kernel,
        [shape(PADDED, depth, dtype=BF16), shape(depth, PADDED, dtype=BF16), shape(8, 128)],
        cost(0, 6 * PADDED * depth),
        [pltpu.VMEM((PADDED, depth // CHUNKS), F32)],
    )(place, vocab_head)


def teacher_kernel(place, target_ref, down_ref, out_ref, total):
    width = down_ref.shape[0] // CHUNKS
    for at in range(CHUNKS):
        start = pl.multiple_of((place[16] ^ at) * width, width)
        product = jnp.dot(
            target_ref[:, pl.ds(start, width)],
            down_ref[at * width : (at + 1) * width],
            preferred_element_type=F32,
        )
        total[...] = product if at == 0 else total[...] + product
    for at in range(16):
        start = pl.multiple_of(place[at] * 16, 16)
        out_ref[at * 16 : (at + 1) * 16] = total[pl.ds(start, 16)]


def teacher_logits(place, target_all, down):
    count, depth = target_all.shape
    return local_call(
        teacher_kernel,
        shape(count, PADDED),
        cost(2 * count * PADDED * depth, 2 * (count + PADDED) * depth),
        [pltpu.VMEM((count, PADDED), F32)],
    )(place, target_all, down)


def student_part(entries, core, firsts, seconds, teacher_ref, down_ref, out_ref):
    width = down_ref.shape[0] // CHUNKS
    rows = out_ref.shape[0]
    for at in range(CHUNKS):
        blocks = [ref[:, at * width : (at + 1) * width] for ref in firsts] + [seconds[at][...]]
        product = jnp.dot(
            jnp.concatenate(blocks, axis=0),
            down_ref[at * width : (at + 1) * width],
            preferred_element_type=F32,
        )
        out_ref[...] = product if at == 0 else out_ref[...] + product
    student, teacher = out_ref[...], teacher_ref[core * rows : (core + 1) * rows]
    real = lax.broadcasted_iota(jnp.int32, student.shape, 1) < entries
    exp_teacher = jnp.where(real, jnp.exp(teacher), 0.0)
    columns = [
        jnp.sum(exp_teacher, axis=1, keepdims=True),
        jnp.sum(jnp.where(real, jnp.exp(student), 0.0), axis=1, keepdims=True),
        jnp.sum(exp_teacher * (teacher - student), axis=1, keepdims=True),
    ]
    lane = lax.broadcasted_iota(jnp.int32, (rows, 128), 1)
    table = jnp.zeros((rows, 128), F32)
    for at, column in enumerate(columns):
        table = jnp.where(lane == at, column, table)
    return table


def own_student_kernel(entries, *refs):
    teacher_ref, down_ref, out_ref, table_ref = refs[8:]
    table_ref[...] = student_part(
        entries, 0, refs[:4], refs[4:8], teacher_ref, down_ref, out_ref
    )


def other_student_kernel(entries, place, *refs):
    teacher_ref, down_ref, own_ref, out_ref, sums_ref, turned = refs[8:]
    other = student_part(entries, 1, refs[:4], refs[4:8], teacher_ref, down_ref, out_ref)
    for core, table in enumerate((own_ref[...], other)):
        for at in range(8):
            start = pl.multiple_of(place[core * 8 + at] * 16, 16)
            turned[pl.ds(start, 16)] = table[at * 16 : (at + 1) * 16]
    sums = turned[...].T[:8]
    for at in range(16):
        sums_ref[at] = sums


def own_student(entries, blocks, teacher, down):
    rows = teacher.shape[0] // 2
    return local_call(
        functools.partial(own_student_kernel, entries),
        [shape(rows, PADDED), shape(rows, 128)],
        cost(2 * rows * down.size, 2 * down.size, 2 * rows * PADDED),
        scalars=False,
    )(*blocks, teacher, down)


def other_student(entries, place, blocks, teacher, down, table):
    rows = teacher.shape[0] // 2
    return local_call(
        functools.partial(other_student_kernel, entries),
        [shape(rows, PADDED), shape(16, 8, 2 * rows)],
        cost(2 * rows * down.size, 2 * down.size, 2 * rows * PADDED),
        [pltpu.VMEM((2 * rows, 128), F32)],
    )(place, *blocks, teacher, down, table)


def grad_kernel(core, place, teacher_ref, student_ref, logs_ref, across_ref, out_ref, table, turned):
    rows, depth = out_ref.shape
    width = depth // CHUNKS
    table[...] = jnp.concatenate(
        [logs_ref[...], jnp.zeros((120, 2 * rows), F32)], axis=0
    ).T
    for at in range(8):
        start = pl.multiple_of(place[core * 8 + at] * 16, 16)
        turned[at * 16 : (at + 1) * 16] = table[pl.ds(start, 16)]
    student = jnp.exp(student_ref[...] - turned[:, 1:2])
    teacher = jnp.exp(teacher_ref[core * rows : (core + 1) * rows] - turned[:, 0:1])
    grad = (student - teacher).astype(BF16)
    for at in range(CHUNKS):
        columns = slice(at * width, (at + 1) * width)
        out_ref[:, columns] = jnp.dot(
            grad, across_ref[:, columns], preferred_element_type=F32
        ).astype(BF16)


def grad_rows(core, place, teacher, student, logs, across):
    rows, depth = student.shape[0], across.shape[1]
    return local_call(
        functools.partial(grad_kernel, core),
        shape(rows, depth, dtype=BF16),
        cost(2 * rows * across.size, 2 * across.size, 2 * rows * PADDED),
        [pltpu.VMEM((2 * rows, 128), F32), pltpu.VMEM((rows, 128), F32)],
    )(place, teacher, student, logs, across)


def pass_kernel(*refs):
    pass


def settled(blocks, teacher):
    return pl.pallas_call(
        pass_kernel,
        in_specs=[pl.BlockSpec(memory_space=pl.ANY)] * (len(blocks) + 1),
        out_specs=[pl.BlockSpec(memory_space=pl.ANY)] * len(blocks),
        out_shape=[shape(*block.shape, dtype=block.dtype) for block in blocks],
        input_output_aliases={at: at for at in range(len(blocks))},
        compiler_params=pltpu.CompilerParams(vmem_limit_bytes=1024 * 1024),
        cost_estimate=cost(0, 0),
    )(*blocks, teacher)


def total_kernel(last, parts_ref, out_ref):
    sums = parts_ref[0]
    for at in range(1, 16):
        sums = sums + parts_ref[at]
    if last:
        logs = jnp.log(sums[:2])
        terms = sums[2:3] / sums[:1] - logs[:1] + logs[1:]
        out_ref[...] = jnp.zeros(out_ref.shape, F32)
        out_ref[:2] = logs
        out_ref[2:3] = terms
    else:
        for at in range(16):
            out_ref[at] = sums


def totalled(parts, last):
    _, rows, count = parts.shape
    return local_call(
        functools.partial(total_kernel, last),
        shape(rows, count) if last else shape(*parts.shape),
        cost(parts.size, 4 * parts.size),
        limit=2 * 1024 * 1024,
        scalars=False,
    )(parts)


def join_kernel(*refs):
    firsts, seconds, (first_ref, second_ref) = refs[:4], refs[4:8], refs[8:]
    (rows, width), (block, _) = firsts[0].shape, seconds[0].shape
    for at in range(4):
        first_ref[:, at * width : (at + 1) * width] = firsts[at][...]
        second_ref[at * block : (at + 1) * block] = seconds[at][...]


def join(firsts, seconds):
    (rows, width), (block, across) = firsts[0].shape, seconds[0].shape
    return pl.pallas_call(
        join_kernel,
        out_shape=[
            jax.ShapeDtypeStruct((rows, 4 * width), BF16),
            jax.ShapeDtypeStruct((4 * block, across), BF16),
        ],
        compiler_params=pltpu.CompilerParams(vmem_limit_bytes=LIMIT),
        cost_estimate=cost(0, 16 * rows * width),
    )(*firsts, *seconds)


def head_kernel(rows_ref, weight_ref, done_ref, out_ref):
    out_ref[...] = jnp.dot(rows_ref[...], weight_ref[...], preferred_element_type=F32)


def head_partial(rows, weight, done):
    return pl.pallas_call(
        head_kernel,
        in_specs=[pl.BlockSpec(memory_space=pltpu.VMEM)] * 3,
        out_shape=jax.ShapeDtypeStruct((rows.shape[0], weight.shape[1]), F32),
        compiler_params=pltpu.CompilerParams(vmem_limit_bytes=LIMIT),
        cost_estimate=cost(HEAD_COST, 2 * (rows.size + weight.size)),
    )(rows, weight, done)


def gather_heads(heads, teacher):
    rows, width = heads.shape
    half = rows // 2
    lines = gathered(heads, "z", 8).transpose(1, 0, 2).reshape(rows, -1)
    first, second = join(from_peers(lines[:half], "y"), from_peers(lines[half:], "x"))
    blocks = settled(from_peers(first, "x") + from_peers(second, "y"), teacher)
    return blocks, [swap(block, "c", 1) for block in blocks]


def scatter_grad(own, other):
    rows, depth = own.shape
    mine = (own.astype(F32) + swap(other, "c", 1).astype(F32)).astype(BF16)
    half = rows // 2
    block = half // 4
    width = depth // 4
    first = [mine[i * block : (i + 1) * block] for i in range(4)]
    second = [mine[half:, i * width : (i + 1) * width] for i in range(4)]
    first, second = summed(first, "x"), summed(second, "y")
    first = [first[:, i * width : (i + 1) * width] for i in range(4)]
    second = [second[i * block : (i + 1) * block] for i in range(4)]
    first, second = summed(first, "y"), summed(second, "x")
    lines = jnp.concatenate([first, second], axis=0)
    sent = lines.reshape(2 * block, 8, -1).transpose(1, 0, 2)
    return jnp.sum(exchange(sent, "z").astype(F32), axis=0)


def shards(log_hidden, positions, offsets, head_weight, head_bias, vocab_head):
    reps, vocs = 32, 8
    in_width, out_width = head_weight.shape
    own = positions.shape[0]
    count = own * reps
    rows = count // vocs
    at_x, at_y, at_c = lax.axis_index("x"), lax.axis_index("y"), lax.axis_index("c")
    voc_index = at_x * 2 + at_c
    inputs = jnp.take(log_hidden, positions, axis=0, mode="clip")
    targets = jnp.take(log_hidden, positions + offsets, axis=0, mode="clip")
    with jax.named_scope("gather_targets"):
        target_all = lax.all_gather(targets, REP, axis=0, tiled=True)
    with jax.named_scope("gather_inputs"):
        input_block = lax.dynamic_slice_in_dim(inputs, voc_index * in_width, in_width, 1)
        input_cols = inputs.reshape(own, reps, out_width).transpose(1, 0, 2)
        sent = jnp.concatenate(
            [jnp.broadcast_to(input_block[None], (reps, own, in_width)), input_cols], axis=2
        )
        got = exchange(sent, REP)
        input_rows = got[:, :, :in_width].reshape(count, in_width)
        residual = got[:, :, in_width:].reshape(count, out_width)
        residual = lax.dynamic_slice_in_dim(residual, voc_index * rows, rows, 0)
    steps = jnp.arange(16)
    order = ((at_x ^ (steps % 4)) * 2 + (at_c ^ (steps // 8))) * 2 + (steps // 4) % 2
    place = jnp.concatenate([order, at_y[None]]).astype(jnp.int32)
    with jax.named_scope("prepare"):
        across, down, done = prepare(place, vocab_head)
    with jax.named_scope("head"):
        partial_pre = head_partial(input_rows, head_weight, done)
        parts = exchange(partial_pre.reshape(vocs, rows, out_width), VOC)
        preact = jnp.sum(parts, axis=0) + head_bias
        heads = (residual.astype(F32) + jax.nn.silu(preact)).astype(BF16)
    with jax.named_scope("teacher"):
        teacher = teacher_logits(place, target_all, down)
    with jax.named_scope("gather_heads"):
        own_blocks, other_blocks = gather_heads(heads, teacher)
    with jax.named_scope("student"):
        entries = vocab_head.shape[0]
        own_logits, table = own_student(entries, own_blocks, teacher, down)
        other_logits, sums = other_student(entries, place, other_blocks, teacher, down, table)
    with jax.named_scope("totals"):
        sums = totalled(exchange(sums, ("z", "c")), False)
        logs = totalled(exchange(sums, ("y", "x")), True)
        loss = jnp.sum(logs[2]) / count
    with jax.named_scope("grad"):
        other_rows = grad_rows(1, place, teacher, other_logits, logs, across)
        own_rows = grad_rows(0, place, teacher, own_logits, logs, across)
    with jax.named_scope("reduce_grad"):
        grad_heads = scatter_grad(own_rows, other_rows)
    with jax.named_scope("finish"):
        sigma = jax.nn.sigmoid(preact)
        grad_pre = grad_heads * (sigma * (1.0 + preact * (1.0 - sigma)))
        bias_part = thirds(jnp.sum(grad_pre, axis=0))
        sent = jnp.concatenate(
            [grad_pre, bias_part, jnp.zeros((13, out_width), F32)], axis=0
        ).astype(BF16)
        got = gathered(sent, VOC, vocs)
        grad_all = got[:, :rows].reshape(count, out_width)
        grad_bias = jnp.sum(got[:, rows : rows + 3].astype(F32), axis=(0, 1))
        grad_weight = lax.dot_general(
            input_rows, grad_all, (((0,), (0,)), ((), ())), preferred_element_type=F32
        )
    return (loss, grad_weight, grad_bias)


def solution(mesh):
    fine = Mesh(mesh.devices.reshape(tuple(SIZES.values())), tuple(SIZES))
    return jax.shard_map(
        shards,
        mesh=fine,
        in_specs=(
            P(REP, None),
            P(REP),
            P(REP),
            P(VOC, REP),
            P(REP),
            P((*REP, *VOC), None),
        ),
        out_specs=(P(), P(VOC, REP), P(REP)),
        check_vma=False,
    )
```

```python
import functools

import jax
import jax.numpy as jnp
from jax import lax
from jax.experimental import pallas as pl
from jax.experimental.pallas import tpu as pltpu
from jax.sharding import Mesh, PartitionSpec as P

BF16 = jnp.bfloat16
F32 = jnp.float32
REP = ("y", "z")
VOC = ("x", "c")
CHUNKS = 4
PADDED = 512
LIMIT = 24 * 1024 * 1024
HEAD_COST = 60_000_000_000
SIZES = {"y": 4, "z": 8, "x": 4, "c": 2}


def exchange(blocks, axis):
    return lax.all_to_all(blocks, axis, split_axis=0, concat_axis=0, tiled=True)


def gathered(block, axis, count):
    return exchange(jnp.broadcast_to(block[None], (count, *block.shape)), axis)


def swap(block, axis, step):
    return lax.ppermute(block, axis, [(i, i ^ step) for i in range(SIZES[axis])])


def thirds(value):
    high = lax.reduce_precision(value, 8, 7)
    middle = lax.reduce_precision(value - high, 8, 7)
    return jnp.stack([high, middle, value - high - middle])


def from_peers(block, axis):
    return [block] + [swap(block, axis, step) for step in range(1, SIZES[axis])]


def summed(blocks, axis):
    total = blocks[0].astype(F32)
    for step in range(1, SIZES[axis]):
        total = total + swap(blocks[step], axis, step).astype(F32)
    return total.astype(BF16)


def cost(flops, bytes_accessed, transcendentals=0):
    return pl.CostEstimate(
        flops=flops, bytes_accessed=bytes_accessed, transcendentals=transcendentals
    )


def local_call(kernel, out_shape, estimate, scratch=(), limit=LIMIT, scalars=True):
    def call(*operands):
        specs = [pl.BlockSpec(memory_space=pltpu.VMEM)] * len(operands)
        if scalars:
            specs[0] = pl.BlockSpec(memory_space=pltpu.SMEM)
        return pl.pallas_call(
            kernel,
            in_specs=specs,
            out_specs=jax.tree.map(lambda _: pl.BlockSpec(memory_space=pltpu.VMEM), out_shape),
            out_shape=out_shape,
            scratch_shapes=scratch,
            compiler_params=pltpu.CompilerParams(vmem_limit_bytes=limit),
            cost_estimate=estimate,
        )(*operands)

    return call


def shape(*sizes, dtype=F32):
    return jax.ShapeDtypeStruct(sizes, dtype)


def prepare_kernel(place, vocab_ref, across_ref, down_ref, done_ref, wide):
    done_ref[...] = jnp.zeros(done_ref.shape, F32)
    entries, depth = vocab_ref.shape
    width = depth // CHUNKS
    wide[...] = jnp.zeros(wide.shape, F32)
    for at in range(CHUNKS):
        start = pl.multiple_of((place[16] ^ at) * width, width)
        wide[:entries] = vocab_ref[:, pl.ds(start, width)].astype(F32)
        block = wide[...]
        across_ref[:, at * width : (at + 1) * width] = block.astype(BF16)
        down_ref[at * width : (at + 1) * width] = block.T.astype(BF16)


def prepare(place, vocab_head):
    depth = vocab_head.shape[1]
    return local_call(
        prepare_kernel,
        [shape(PADDED, depth, dtype=BF16), shape(depth, PADDED, dtype=BF16), shape(8, 128)],
        cost(0, 6 * PADDED * depth),
        [pltpu.VMEM((PADDED, depth // CHUNKS), F32)],
    )(place, vocab_head)


def teacher_kernel(place, own_ref, other_ref, down_ref, out_ref, total):
    width = down_ref.shape[0] // CHUNKS
    for half, target_ref in enumerate((own_ref, other_ref)):
        for at in range(2):
            group = (place[17] ^ half) * 2 + at
            start = pl.multiple_of((group ^ place[16]) * width, width)
            product = jnp.dot(
                target_ref[:, at * width : (at + 1) * width],
                down_ref[pl.ds(start, width)],
                preferred_element_type=F32,
            )
            total[...] = product if half + at == 0 else total[...] + product
    for at in range(16):
        start = pl.multiple_of(place[at] * 16, 16)
        out_ref[at * 16 : (at + 1) * 16] = total[pl.ds(start, 16)]


def teacher_logits(place, own_half, other_half, down):
    count, depth = own_half.shape[0], down.shape[0]
    return local_call(
        teacher_kernel,
        shape(count, PADDED),
        cost(2 * count * PADDED * depth, 2 * (count + PADDED) * depth),
        [pltpu.VMEM((count, PADDED), F32)],
    )(place, own_half, other_half, down)


def student_part(entries, core, firsts, seconds, teacher_ref, down_ref, out_ref):
    width = down_ref.shape[0] // CHUNKS
    rows = out_ref.shape[0]
    for at in range(CHUNKS):
        blocks = [ref[:, at * width : (at + 1) * width] for ref in firsts] + [seconds[at][...]]
        product = jnp.dot(
            jnp.concatenate(blocks, axis=0),
            down_ref[at * width : (at + 1) * width],
            preferred_element_type=F32,
        )
        out_ref[...] = product if at == 0 else out_ref[...] + product
    student, teacher = out_ref[...], teacher_ref[core * rows : (core + 1) * rows]
    real = lax.broadcasted_iota(jnp.int32, student.shape, 1) < entries
    exp_teacher = jnp.where(real, jnp.exp(teacher), 0.0)
    columns = [
        jnp.sum(exp_teacher, axis=1, keepdims=True),
        jnp.sum(jnp.where(real, jnp.exp(student), 0.0), axis=1, keepdims=True),
        jnp.sum(exp_teacher * (teacher - student), axis=1, keepdims=True),
    ]
    lane = lax.broadcasted_iota(jnp.int32, (rows, 128), 1)
    table = jnp.zeros((rows, 128), F32)
    for at, column in enumerate(columns):
        table = jnp.where(lane == at, column, table)
    return table


def packed(table):
    lanes = table.shape[1] // 2
    return jnp.concatenate([table[:, :lanes], table[:, lanes:]], axis=0)


def own_student_kernel(entries, *refs):
    teacher_ref, down_ref, out_ref, table_ref = refs[8:]
    table_ref[...] = student_part(
        entries, 0, refs[:4], refs[4:8], teacher_ref, down_ref, out_ref
    )


def other_student_kernel(entries, place, *refs):
    teacher_ref, down_ref, own_ref, out_ref, sums_ref, turned = refs[8:]
    other = student_part(entries, 1, refs[:4], refs[4:8], teacher_ref, down_ref, out_ref)
    for core, table in enumerate((own_ref[...], other)):
        for at in range(8):
            start = pl.multiple_of(place[core * 8 + at] * 16, 16)
            turned[pl.ds(start, 16)] = table[at * 16 : (at + 1) * 16]
    sums = packed(turned[...].T[:4])
    for at in range(sums_ref.shape[0]):
        sums_ref[at] = sums


def own_student(entries, blocks, teacher, down):
    rows = teacher.shape[0] // 2
    return local_call(
        functools.partial(own_student_kernel, entries),
        [shape(rows, PADDED), shape(rows, 128)],
        cost(2 * rows * down.size, 2 * down.size, 2 * rows * PADDED),
        scalars=False,
    )(*blocks, teacher, down)


def other_student(entries, place, blocks, teacher, down, table):
    rows = teacher.shape[0] // 2
    return local_call(
        functools.partial(other_student_kernel, entries),
        [shape(rows, PADDED), shape(8, 8, rows)],
        cost(2 * rows * down.size, 2 * down.size, 2 * rows * PADDED),
        [pltpu.VMEM((2 * rows, 128), F32)],
    )(place, *blocks, teacher, down, table)


def grad_kernel(core, place, teacher_ref, student_ref, logs_ref, across_ref, out_ref, table, turned):
    rows, depth = out_ref.shape
    width = depth // CHUNKS
    table[...] = jnp.concatenate(
        [logs_ref[...], jnp.zeros((120, 2 * rows), F32)], axis=0
    ).T
    for at in range(8):
        start = pl.multiple_of(place[core * 8 + at] * 16, 16)
        turned[at * 16 : (at + 1) * 16] = table[pl.ds(start, 16)]
    student = jnp.exp(student_ref[...] - turned[:, 1:2])
    teacher = jnp.exp(teacher_ref[core * rows : (core + 1) * rows] - turned[:, 0:1])
    grad = (student - teacher).astype(BF16)
    for at in range(CHUNKS):
        columns = slice(at * width, (at + 1) * width)
        out_ref[:, columns] = jnp.dot(
            grad, across_ref[:, columns], preferred_element_type=F32
        ).astype(BF16)


def grad_rows(core, place, teacher, student, logs, across):
    rows, depth = student.shape[0], across.shape[1]
    return local_call(
        functools.partial(grad_kernel, core),
        shape(rows, depth, dtype=BF16),
        cost(2 * rows * across.size, 2 * across.size, 2 * rows * PADDED),
        [pltpu.VMEM((2 * rows, 128), F32), pltpu.VMEM((rows, 128), F32)],
    )(place, teacher, student, logs, across)


def pass_kernel(*refs):
    pass


def settled(blocks, awaited):
    return pl.pallas_call(
        pass_kernel,
        in_specs=[pl.BlockSpec(memory_space=pl.ANY)] * (len(blocks) + 1),
        out_specs=[pl.BlockSpec(memory_space=pl.ANY)] * len(blocks),
        out_shape=[shape(*block.shape, dtype=block.dtype) for block in blocks],
        input_output_aliases={at: at for at in range(len(blocks))},
        compiler_params=pltpu.CompilerParams(vmem_limit_bytes=1024 * 1024),
        cost_estimate=cost(0, 0),
    )(*blocks, awaited)


def summed_parts(parts_ref):
    parts = [parts_ref[at] for at in range(parts_ref.shape[0])]
    while len(parts) > 1:
        parts = [parts[at] + parts[at + 1] for at in range(0, len(parts), 2)]
    return parts[0]


def total_kernel(parts_ref, out_ref):
    sums = summed_parts(parts_ref)
    for at in range(out_ref.shape[0]):
        out_ref[at] = sums


def log_kernel(parts_ref, out_ref):
    sums = summed_parts(parts_ref)
    sums = jnp.concatenate([sums[:4], sums[4:]], axis=1)
    logs = jnp.log(sums[:2])
    out_ref[...] = jnp.zeros(out_ref.shape, F32)
    out_ref[:2] = logs
    out_ref[2:3] = sums[2:3] / sums[:1] - logs[:1] + logs[1:]


def totalled(kernel, parts, *sizes):
    return local_call(
        kernel,
        shape(*sizes),
        cost(parts.size, 4 * parts.size),
        limit=2 * 1024 * 1024,
        scalars=False,
    )(parts)


def join_kernel(*refs):
    firsts, seconds, (first_ref, second_ref) = refs[:4], refs[4:8], refs[8:]
    (rows, width), (block, _) = firsts[0].shape, seconds[0].shape
    for at in range(4):
        first_ref[:, at * width : (at + 1) * width] = firsts[at][...]
        second_ref[at * block : (at + 1) * block] = seconds[at][...]


def join(firsts, seconds):
    (rows, width), (block, across) = firsts[0].shape, seconds[0].shape
    return pl.pallas_call(
        join_kernel,
        out_shape=[
            jax.ShapeDtypeStruct((rows, 4 * width), BF16),
            jax.ShapeDtypeStruct((4 * block, across), BF16),
        ],
        compiler_params=pltpu.CompilerParams(vmem_limit_bytes=LIMIT),
        cost_estimate=cost(0, 16 * rows * width),
    )(*firsts, *seconds)


def head_kernel(rows_ref, weight_ref, done_ref, out_ref):
    out_ref[...] = jnp.dot(rows_ref[...], weight_ref[...], preferred_element_type=F32)


def head_partial(rows, weight, done):
    return pl.pallas_call(
        head_kernel,
        in_specs=[pl.BlockSpec(memory_space=pltpu.VMEM)] * 3,
        out_shape=jax.ShapeDtypeStruct((rows.shape[0], weight.shape[1]), F32),
        compiler_params=pltpu.CompilerParams(vmem_limit_bytes=LIMIT),
        cost_estimate=cost(HEAD_COST, 2 * (rows.size + weight.size)),
    )(rows, weight, done)


def gather_lines(heads):
    return gathered(heads, "z", 8).transpose(1, 0, 2).reshape(heads.shape[0], -1)


def gather_heads(lines, teacher):
    half = lines.shape[0] // 2
    first, second = join(from_peers(lines[:half], "y"), from_peers(lines[half:], "x"))
    blocks = settled(from_peers(first, "x") + from_peers(second, "y"), teacher)
    return blocks, [swap(block, "c", 1) for block in blocks]


def scatter_grad(own, other):
    rows, depth = own.shape
    mine = (own.astype(F32) + swap(other, "c", 1).astype(F32)).astype(BF16)
    half = rows // 2
    block = half // 4
    width = depth // 4
    first = [mine[i * block : (i + 1) * block] for i in range(4)]
    second = [mine[half:, i * width : (i + 1) * width] for i in range(4)]
    first, second = summed(first, "x"), summed(second, "y")
    first = [first[:, i * width : (i + 1) * width] for i in range(4)]
    second = [second[i * block : (i + 1) * block] for i in range(4)]
    first, second = summed(first, "y"), summed(second, "x")
    lines = jnp.concatenate([first, second], axis=0)
    sent = lines.reshape(2 * block, 8, -1).transpose(1, 0, 2)
    return jnp.sum(exchange(sent, "z").astype(F32), axis=0)


def shards(log_hidden, positions, offsets, head_weight, head_bias, vocab_head):
    reps, vocs = 32, 8
    in_width, out_width = head_weight.shape
    own = positions.shape[0]
    count = own * reps
    rows = count // vocs
    at_x, at_y, at_c = lax.axis_index("x"), lax.axis_index("y"), lax.axis_index("c")
    voc_index = at_x * 2 + at_c
    taken = jnp.concatenate([positions, positions + offsets])
    taken = jnp.take(log_hidden, taken, axis=0, mode="clip")
    inputs, targets = taken[:own], taken[own:]
    with jax.named_scope("gather_targets"):
        half = targets.shape[1] // 2
        target_half = lax.dynamic_slice_in_dim(targets, at_c * half, half, 1)
        target_half = lax.all_gather(target_half, REP, axis=0, tiled=True)
    with jax.named_scope("gather_inputs"):
        input_block = lax.dynamic_slice_in_dim(inputs, voc_index * in_width, in_width, 1)
        input_cols = inputs.reshape(own, reps, out_width).transpose(1, 0, 2)
        sent = jnp.concatenate(
            [jnp.broadcast_to(input_block[None], (reps, own, in_width)), input_cols], axis=2
        )
        got = exchange(sent, REP)
        input_rows = got[:, :, :in_width].reshape(count, in_width)
        residual = got[:, :, in_width:].reshape(count, out_width)
        residual = lax.dynamic_slice_in_dim(residual, voc_index * rows, rows, 0)
    steps = jnp.arange(16)
    order = ((at_x ^ (steps % 4)) * 2 + (at_c ^ (steps // 8))) * 2 + (steps // 4) % 2
    place = jnp.concatenate([order, at_y[None], at_c[None]]).astype(jnp.int32)
    with jax.named_scope("prepare"):
        across, down, done = prepare(place, vocab_head)
    with jax.named_scope("head"):
        partial_pre = head_partial(input_rows, head_weight, done)
        parts = exchange(partial_pre.reshape(vocs, rows, out_width), VOC)
        preact = jnp.sum(parts, axis=0) + head_bias
        heads = (residual.astype(F32) + jax.nn.silu(preact)).astype(BF16)
    with jax.named_scope("gather_heads"):
        lines = gather_lines(heads)
    with jax.named_scope("teacher"):
        target_half = pltpu.with_memory_space_constraint(target_half, pltpu.HBM)
        (target_half,) = settled([target_half], lines)
        other_half = swap(target_half, "c", 1)
        teacher = teacher_logits(place, target_half, other_half, down)
    with jax.named_scope("gather_heads"):
        own_blocks, other_blocks = gather_heads(lines, teacher)
    with jax.named_scope("student"):
        entries = vocab_head.shape[0]
        own_logits, table = own_student(entries, own_blocks, teacher, down)
        other_logits, sums = other_student(entries, place, other_blocks, teacher, down, table)
    with jax.named_scope("totals"):
        sums = totalled(total_kernel, exchange(sums, VOC), reps, 8, count // 2)
        logs = totalled(log_kernel, exchange(sums, REP), 8, count)
        loss = jnp.sum(logs[2]) / count
    with jax.named_scope("grad"):
        other_rows = grad_rows(1, place, teacher, other_logits, logs, across)
        own_rows = grad_rows(0, place, teacher, own_logits, logs, across)
    with jax.named_scope("reduce_grad"):
        grad_heads = scatter_grad(own_rows, other_rows)
    with jax.named_scope("finish"):
        sigma = jax.nn.sigmoid(preact)
        grad_pre = grad_heads * (sigma * (1.0 + preact * (1.0 - sigma)))
        bias_part = thirds(jnp.sum(grad_pre, axis=0))
        sent = jnp.concatenate(
            [grad_pre, bias_part, jnp.zeros((13, out_width), F32)], axis=0
        ).astype(BF16)
        got = gathered(sent, VOC, vocs)
        grad_all = got[:, :rows].reshape(count, out_width)
        grad_bias = jnp.sum(got[:, rows : rows + 3].astype(F32), axis=(0, 1))
        grad_weight = lax.dot_general(
            input_rows, grad_all, (((0,), (0,)), ((), ())), preferred_element_type=F32
        )
    return (loss, grad_weight, grad_bias)


def solution(mesh):
    fine = Mesh(mesh.devices.reshape(tuple(SIZES.values())), tuple(SIZES))
    return jax.shard_map(
        shards,
        mesh=fine,
        in_specs=(
            P(REP, None),
            P(REP),
            P(REP),
            P(VOC, REP),
            P(REP),
            P((*REP, *VOC), None),
        ),
        out_specs=(P(), P(VOC, REP), P(REP)),
        check_vma=False,
    )
```

```python
import functools

import jax
import jax.numpy as jnp
from jax import lax
from jax.experimental import pallas as pl
from jax.experimental.pallas import tpu as pltpu
from jax.sharding import Mesh, PartitionSpec as P

BF16 = jnp.bfloat16
F32 = jnp.float32
REP = ("y", "z")
VOC = ("x", "c")
CHUNKS = 4
PADDED = 512
LIMIT = 24 * 1024 * 1024
HEAD_COST = 90_000_000_000
SIZES = {"y": 4, "z": 8, "x": 4, "c": 2}


def exchange(blocks, axis):
    return lax.all_to_all(blocks, axis, split_axis=0, concat_axis=0, tiled=True)


def gathered(block, axis, count):
    return exchange(jnp.broadcast_to(block[None], (count, *block.shape)), axis)


def swap(block, axis, step):
    return lax.ppermute(block, axis, [(i, i ^ step) for i in range(SIZES[axis])])


def thirds(value):
    high = lax.reduce_precision(value, 8, 7)
    middle = lax.reduce_precision(value - high, 8, 7)
    return jnp.stack([high, middle, value - high - middle])


def from_peers(block, axis):
    return [block] + [swap(block, axis, step) for step in range(1, SIZES[axis])]


def summed(blocks, axis):
    total = blocks[0].astype(F32)
    for step in range(1, SIZES[axis]):
        total = total + swap(blocks[step], axis, step).astype(F32)
    return total.astype(BF16)


def cost(flops, bytes_accessed, transcendentals=0):
    return pl.CostEstimate(
        flops=flops, bytes_accessed=bytes_accessed, transcendentals=transcendentals
    )


def local_call(kernel, out_shape, estimate, scratch=(), limit=LIMIT, scalars=True):
    def call(*operands):
        specs = [pl.BlockSpec(memory_space=pltpu.VMEM)] * len(operands)
        if scalars:
            specs[0] = pl.BlockSpec(memory_space=pltpu.SMEM)
        return pl.pallas_call(
            kernel,
            in_specs=specs,
            out_specs=jax.tree.map(lambda _: pl.BlockSpec(memory_space=pltpu.VMEM), out_shape),
            out_shape=out_shape,
            scratch_shapes=scratch,
            compiler_params=pltpu.CompilerParams(vmem_limit_bytes=limit),
            cost_estimate=estimate,
        )(*operands)

    return call


def shape(*sizes, dtype=F32):
    return jax.ShapeDtypeStruct(sizes, dtype)


def prepare_kernel(place, vocab_ref, awaited_ref, across_ref, down_ref, wide):
    entries, depth = vocab_ref.shape
    width = depth // CHUNKS
    wide[...] = jnp.zeros(wide.shape, F32)
    for at in range(CHUNKS):
        start = pl.multiple_of((place[16] ^ at) * width, width)
        wide[:entries] = vocab_ref[:, pl.ds(start, width)].astype(F32)
        block = wide[...]
        across_ref[:, at * width : (at + 1) * width] = block.astype(BF16)
        down_ref[at * width : (at + 1) * width] = block.T.astype(BF16)


def prepare(place, vocab_head, awaited):
    depth = vocab_head.shape[1]
    vmem = pl.BlockSpec(memory_space=pltpu.VMEM)
    return pl.pallas_call(
        prepare_kernel,
        in_specs=[
            pl.BlockSpec(memory_space=pltpu.SMEM),
            vmem,
            pl.BlockSpec(memory_space=pl.ANY),
        ],
        out_specs=[vmem, vmem],
        out_shape=[shape(PADDED, depth, dtype=BF16), shape(depth, PADDED, dtype=BF16)],
        scratch_shapes=[pltpu.VMEM((PADDED, depth // CHUNKS), F32)],
        compiler_params=pltpu.CompilerParams(vmem_limit_bytes=LIMIT),
        cost_estimate=cost(0, 6 * PADDED * depth),
    )(place, vocab_head, awaited)


def teacher_kernel(place, target_ref, down_ref, out_ref, total):
    width = down_ref.shape[0] // CHUNKS
    for at in range(CHUNKS):
        start = pl.multiple_of((place[16] ^ at) * width, width)
        product = jnp.dot(
            target_ref[:, pl.ds(start, width)],
            down_ref[at * width : (at + 1) * width],
            preferred_element_type=F32,
        )
        total[...] = product if at == 0 else total[...] + product
    for at in range(16):
        start = pl.multiple_of(place[17 + at] * 16, 16)
        out_ref[at * 16 : (at + 1) * 16] = total[pl.ds(start, 16)]


def teacher_logits(place, target_all, down):
    count, depth = target_all.shape
    return local_call(
        teacher_kernel,
        shape(count, PADDED),
        cost(2 * count * PADDED * depth, 2 * (count + PADDED) * depth),
        [pltpu.VMEM((count, PADDED), F32)],
    )(place, target_all, down)


def student_part(entries, core, firsts, seconds, teacher_ref, down_ref, out_ref):
    width = down_ref.shape[0] // CHUNKS
    rows = out_ref.shape[0]
    for at in range(CHUNKS):
        blocks = [ref[:, at * width : (at + 1) * width] for ref in firsts] + [seconds[at][...]]
        product = jnp.dot(
            jnp.concatenate(blocks, axis=0),
            down_ref[at * width : (at + 1) * width],
            preferred_element_type=F32,
        )
        out_ref[...] = product if at == 0 else out_ref[...] + product
    student, teacher = out_ref[...], teacher_ref[core * rows : (core + 1) * rows]
    real = lax.broadcasted_iota(jnp.int32, student.shape, 1) < entries
    exp_teacher = jnp.where(real, jnp.exp(teacher), 0.0)
    columns = [
        jnp.sum(exp_teacher, axis=1, keepdims=True),
        jnp.sum(jnp.where(real, jnp.exp(student), 0.0), axis=1, keepdims=True),
        jnp.sum(exp_teacher * (teacher - student), axis=1, keepdims=True),
    ]
    lane = lax.broadcasted_iota(jnp.int32, (rows, 128), 1)
    table = jnp.zeros((rows, 128), F32)
    for at, column in enumerate(columns):
        table = jnp.where(lane == at, column, table)
    return table


def packed(table):
    lanes = table.shape[1] // 2
    return jnp.concatenate([table[:, :lanes], table[:, lanes:]], axis=0)


def own_student_kernel(entries, *refs):
    teacher_ref, down_ref, out_ref, table_ref = refs[8:]
    table_ref[...] = student_part(
        entries, 0, refs[:4], refs[4:8], teacher_ref, down_ref, out_ref
    )


def other_student_kernel(entries, place, *refs):
    teacher_ref, down_ref, own_ref, out_ref, sums_ref, turned = refs[8:]
    other = student_part(entries, 1, refs[:4], refs[4:8], teacher_ref, down_ref, out_ref)
    for core, table in enumerate((own_ref[...], other)):
        for at in range(8):
            start = pl.multiple_of(place[core * 8 + at] * 16, 16)
            turned[pl.ds(start, 16)] = table[at * 16 : (at + 1) * 16]
    sums = packed(turned[...].T[:4])
    for at in range(sums_ref.shape[0]):
        sums_ref[at] = sums


def own_student(entries, blocks, teacher, down):
    rows = teacher.shape[0] // 2
    return local_call(
        functools.partial(own_student_kernel, entries),
        [shape(rows, PADDED), shape(rows, 128)],
        cost(2 * rows * down.size, 2 * down.size, 2 * rows * PADDED),
        scalars=False,
    )(*blocks, teacher, down)


def other_student(entries, place, blocks, teacher, down, table):
    rows = teacher.shape[0] // 2
    return local_call(
        functools.partial(other_student_kernel, entries),
        [shape(rows, PADDED), shape(32, 8, rows)],
        cost(2 * rows * down.size, 2 * down.size, 2 * rows * PADDED),
        [pltpu.VMEM((2 * rows, 128), F32)],
    )(place, *blocks, teacher, down, table)


def grad_kernel(core, place, teacher_ref, student_ref, logs_ref, across_ref, out_ref, table, turned):
    rows, depth = out_ref.shape
    width = depth // CHUNKS
    table[...] = jnp.concatenate(
        [logs_ref[...], jnp.zeros((120, 2 * rows), F32)], axis=0
    ).T
    for at in range(8):
        start = pl.multiple_of(place[core * 8 + at] * 16, 16)
        turned[at * 16 : (at + 1) * 16] = table[pl.ds(start, 16)]
    student = jnp.exp(student_ref[...] - turned[:, 1:2])
    teacher = jnp.exp(teacher_ref[core * rows : (core + 1) * rows] - turned[:, 0:1])
    grad = (student - teacher).astype(BF16)
    for at in range(CHUNKS):
        columns = slice(at * width, (at + 1) * width)
        out_ref[:, columns] = jnp.dot(
            grad, across_ref[:, columns], preferred_element_type=F32
        ).astype(BF16)


def grad_rows(core, place, teacher, student, logs, across):
    rows, depth = student.shape[0], across.shape[1]
    return local_call(
        functools.partial(grad_kernel, core),
        shape(rows, depth, dtype=BF16),
        cost(2 * rows * across.size, 2 * across.size, 2 * rows * PADDED),
        [pltpu.VMEM((2 * rows, 128), F32), pltpu.VMEM((rows, 128), F32)],
    )(place, teacher, student, logs, across)


def pass_kernel(*refs):
    pass


def settled(blocks, awaited):
    return pl.pallas_call(
        pass_kernel,
        in_specs=[pl.BlockSpec(memory_space=pl.ANY)] * (len(blocks) + 1),
        out_specs=[pl.BlockSpec(memory_space=pl.ANY)] * len(blocks),
        out_shape=[shape(*block.shape, dtype=block.dtype) for block in blocks],
        input_output_aliases={at: at for at in range(len(blocks))},
        compiler_params=pltpu.CompilerParams(vmem_limit_bytes=1024 * 1024),
        cost_estimate=cost(0, 0),
    )(*blocks, awaited)


def summed_parts(parts_ref):
    parts = [parts_ref[at] for at in range(parts_ref.shape[0])]
    while len(parts) > 1:
        parts = [parts[at] + parts[at + 1] for at in range(0, len(parts), 2)]
    return parts[0]


def total_kernel(parts_ref, out_ref):
    sums = summed_parts(parts_ref)
    for at in range(out_ref.shape[0]):
        out_ref[at] = sums


def log_kernel(parts_ref, out_ref):
    sums = summed_parts(parts_ref)
    sums = jnp.concatenate([sums[:4], sums[4:]], axis=1)
    logs = jnp.log(sums[:2])
    out_ref[...] = jnp.zeros(out_ref.shape, F32)
    out_ref[:2] = logs
    out_ref[2:3] = sums[2:3] / sums[:1] - logs[:1] + logs[1:]


def totalled(kernel, parts, *sizes):
    return local_call(
        kernel,
        shape(*sizes),
        cost(parts.size, 4 * parts.size),
        limit=2 * 1024 * 1024,
        scalars=False,
    )(parts)


def join_kernel(*refs):
    firsts, seconds, (first_ref, second_ref) = refs[:4], refs[4:8], refs[8:]
    (rows, width), (block, _) = firsts[0].shape, seconds[0].shape
    for at in range(4):
        first_ref[:, at * width : (at + 1) * width] = firsts[at][...]
        second_ref[at * block : (at + 1) * block] = seconds[at][...]


def join(firsts, seconds):
    (rows, width), (block, across) = firsts[0].shape, seconds[0].shape
    return pl.pallas_call(
        join_kernel,
        out_shape=[
            jax.ShapeDtypeStruct((rows, 4 * width), BF16),
            jax.ShapeDtypeStruct((4 * block, across), BF16),
        ],
        compiler_params=pltpu.CompilerParams(vmem_limit_bytes=LIMIT),
        cost_estimate=cost(0, 16 * rows * width),
    )(*firsts, *seconds)


def stack_kernel(*refs):
    blocks, (out_ref, ready_ref) = refs[:4], refs[4:]
    rows = blocks[0].shape[0]
    for at, block in enumerate(blocks):
        out_ref[at * rows : (at + 1) * rows] = block[...]
    ready_ref[...] = jnp.zeros(ready_ref.shape, F32)


def stacked(blocks):
    rows, across = blocks[0].shape
    return local_call(
        stack_kernel,
        [shape(4 * rows, across, dtype=BF16), shape(8, 128)],
        cost(0, 16 * rows * across),
        limit=4 * 1024 * 1024,
        scalars=False,
    )(*blocks)


def head_kernel(rows_ref, weight_ref, ready_ref, out_ref):
    out_ref[...] = jnp.dot(rows_ref[...], weight_ref[...], preferred_element_type=F32)


def head_partial(rows, weight, ready):
    return pl.pallas_call(
        head_kernel,
        in_specs=[pl.BlockSpec(memory_space=pltpu.VMEM)] * 3,
        out_shape=jax.ShapeDtypeStruct((rows.shape[0], weight.shape[1]), F32),
        compiler_params=pltpu.CompilerParams(vmem_limit_bytes=LIMIT),
        cost_estimate=cost(HEAD_COST, 2 * (rows.size + weight.size)),
    )(rows, weight, ready)


def gather_lines(heads):
    return gathered(heads, "z", 8).transpose(1, 0, 2).reshape(heads.shape[0], -1)


def gather_heads(lines, teacher):
    half = lines.shape[0] // 2
    first, second = join(from_peers(lines[:half], "y"), from_peers(lines[half:], "x"))
    blocks = settled(from_peers(first, "x") + from_peers(second, "y"), teacher)
    return blocks, [swap(block, "c", 1) for block in blocks]


def scatter_grad(own, other):
    rows, depth = own.shape
    mine = (own.astype(F32) + swap(other, "c", 1).astype(F32)).astype(BF16)
    half = rows // 2
    block = half // 4
    width = depth // 4
    first = [mine[i * block : (i + 1) * block] for i in range(4)]
    second = [mine[half:, i * width : (i + 1) * width] for i in range(4)]
    first, second = summed(first, "x"), summed(second, "y")
    first = [first[:, i * width : (i + 1) * width] for i in range(4)]
    second = [second[i * block : (i + 1) * block] for i in range(4)]
    first, second = summed(first, "y"), summed(second, "x")
    lines = jnp.concatenate([first, second], axis=0)
    sent = lines.reshape(2 * block, 8, -1).transpose(1, 0, 2)
    return jnp.sum(exchange(sent, "z").astype(F32), axis=0)


def shards(log_hidden, positions, offsets, head_weight, head_bias, vocab_head):
    reps, vocs = 32, 8
    in_width, out_width = head_weight.shape
    own = positions.shape[0]
    count = own * reps
    rows = count // vocs
    at_x, at_y, at_c = lax.axis_index("x"), lax.axis_index("y"), lax.axis_index("c")
    voc_index = at_x * 2 + at_c
    taken = jnp.concatenate([positions, positions + offsets])
    taken = jnp.take(log_hidden, taken, axis=0, mode="clip")
    inputs = taken[:own]
    with jax.named_scope("gather_z"):
        blocks = lax.dynamic_slice_in_dim(
            taken.reshape(2, own, -1), voc_index * in_width, in_width, 2
        )
        input_cols = inputs.reshape(own, 4, 8, out_width).transpose(2, 0, 1, 3)
        sent = jnp.concatenate(
            [
                jnp.broadcast_to(blocks[0], (8, own, in_width)),
                jnp.broadcast_to(blocks[1], (8, own, in_width)),
                input_cols.reshape(8, own, -1),
            ],
            axis=2,
        )
        lines = exchange(sent, "z").reshape(8 * own, -1)
        input_lines, target_lines = lines[:, :in_width], lines[:, in_width : 2 * in_width]
        input_cols = lines[:, 2 * in_width :].reshape(-1, 4, out_width).transpose(1, 0, 2)
    with jax.named_scope("gather_inputs"):
        sent = jnp.concatenate(
            [jnp.broadcast_to(input_lines, (4, *input_lines.shape)), input_cols], axis=2
        )
        got = exchange(sent, "y")
        input_rows = got[:, :, :in_width].reshape(count, in_width)
        residual = got[:, :, in_width:].reshape(count, out_width)
        residual = lax.dynamic_slice_in_dim(residual, voc_index * rows, rows, 0)
    with jax.named_scope("gather_targets"):
        target_rows, ready = stacked(from_peers(target_lines, "y"))
        target_all = lax.all_gather(target_rows, VOC, axis=1, tiled=True)
    steps = jnp.arange(16)
    order = ((at_x ^ (steps % 4)) * 2 + (at_c ^ (steps // 8))) * 2 + (steps // 4) % 2
    target_order = (order // 4 ^ at_y) * 4 + order % 4
    place = jnp.concatenate([order, at_y[None], target_order]).astype(jnp.int32)
    with jax.named_scope("head"):
        partial_pre = head_partial(input_rows, head_weight, ready)
        parts = exchange(partial_pre.reshape(vocs, rows, out_width), VOC)
        preact = jnp.sum(parts, axis=0) + head_bias
        heads = (residual.astype(F32) + jax.nn.silu(preact)).astype(BF16)
    with jax.named_scope("gather_heads"):
        lines = gather_lines(heads)
    with jax.named_scope("teacher"):
        across, down = prepare(place, vocab_head, target_all)
        teacher = teacher_logits(place, target_all, down)
    with jax.named_scope("gather_heads"):
        own_blocks, other_blocks = gather_heads(lines, teacher)
    with jax.named_scope("student"):
        entries = vocab_head.shape[0]
        own_logits, table = own_student(entries, own_blocks, teacher, down)
        other_logits, sums = other_student(entries, place, other_blocks, teacher, down, table)
    with jax.named_scope("totals"):
        sums = totalled(total_kernel, exchange(sums, ("y", "x", "c")), 8, 8, count // 2)
        logs = totalled(log_kernel, exchange(sums, "z"), 8, count)
        loss = jnp.sum(logs[2]) / count
    with jax.named_scope("grad"):
        other_rows = grad_rows(1, place, teacher, other_logits, logs, across)
        own_rows = grad_rows(0, place, teacher, own_logits, logs, across)
    with jax.named_scope("reduce_grad"):
        grad_heads = scatter_grad(own_rows, other_rows)
    with jax.named_scope("finish"):
        sigma = jax.nn.sigmoid(preact)
        grad_pre = grad_heads * (sigma * (1.0 + preact * (1.0 - sigma)))
        bias_part = thirds(jnp.sum(grad_pre, axis=0))
        sent = jnp.concatenate(
            [grad_pre, bias_part, jnp.zeros((13, out_width), F32)], axis=0
        ).astype(BF16)
        got = gathered(sent, VOC, vocs)
        grad_all = got[:, :rows].reshape(count, out_width)
        grad_bias = jnp.sum(got[:, rows : rows + 3].astype(F32), axis=(0, 1))
        grad_weight = lax.dot_general(
            input_rows, grad_all, (((0,), (0,)), ((), ())), preferred_element_type=F32
        )
    return (loss, grad_weight, grad_bias)


def solution(mesh):
    fine = Mesh(mesh.devices.reshape(tuple(SIZES.values())), tuple(SIZES))
    return jax.shard_map(
        shards,
        mesh=fine,
        in_specs=(
            P(REP, None),
            P(REP),
            P(REP),
            P(VOC, REP),
            P(REP),
            P((*REP, *VOC), None),
        ),
        out_specs=(P(), P(VOC, REP), P(REP)),
        check_vma=False,
    )
```

```python
import functools

import jax
import jax.numpy as jnp
from jax import lax
from jax.experimental import pallas as pl
from jax.experimental.pallas import tpu as pltpu
from jax.sharding import Mesh, PartitionSpec as P

BF16 = jnp.bfloat16
F32 = jnp.float32
REP = ("y", "z")
VOC = ("x", "c")
CHUNKS = 4
PADDED = 512
LIMIT = 14 * 1024 * 1024
HEADS_COST = 60_000_000_000
SIZES = {"y": 4, "z": 8, "x": 4, "c": 2}


def exchange(blocks, axis):
    return lax.all_to_all(blocks, axis, split_axis=0, concat_axis=0, tiled=True)


def gathered(block, axis, count):
    return exchange(jnp.broadcast_to(block[None], (count, *block.shape)), axis)


def swap(block, axis, step):
    return lax.ppermute(block, axis, [(i, i ^ step) for i in range(SIZES[axis])])


def thirds(value):
    high = lax.reduce_precision(value, 8, 7)
    middle = lax.reduce_precision(value - high, 8, 7)
    return jnp.stack([high, middle, value - high - middle])


def from_peers(block, axis):
    return [block] + [swap(block, axis, step) for step in range(1, SIZES[axis])]


def summed(blocks, axis):
    total = blocks[0].astype(F32)
    for step in range(1, SIZES[axis]):
        total = total + swap(blocks[step], axis, step).astype(F32)
    return total.astype(BF16)


def cost(flops, bytes_accessed, transcendentals=0):
    return pl.CostEstimate(
        flops=flops, bytes_accessed=bytes_accessed, transcendentals=transcendentals
    )


def local_call(kernel, out_shape, estimate, scratch=(), limit=LIMIT, scalars=True):
    def call(*operands):
        specs = [pl.BlockSpec(memory_space=pltpu.VMEM)] * len(operands)
        if scalars:
            specs[0] = pl.BlockSpec(memory_space=pltpu.SMEM)
        return pl.pallas_call(
            kernel,
            in_specs=specs,
            out_specs=jax.tree.map(lambda _: pl.BlockSpec(memory_space=pltpu.VMEM), out_shape),
            out_shape=out_shape,
            scratch_shapes=scratch,
            compiler_params=pltpu.CompilerParams(vmem_limit_bytes=limit),
            cost_estimate=estimate,
        )(*operands)

    return call


def shape(*sizes, dtype=F32):
    return jax.ShapeDtypeStruct(sizes, dtype)


def prepare_kernel(place, vocab_ref, awaited_ref, across_ref, down_ref, wide):
    entries, depth = vocab_ref.shape
    width = depth // CHUNKS
    wide[...] = jnp.zeros(wide.shape, F32)
    for at in range(CHUNKS):
        start = pl.multiple_of((place[16] ^ at) * width, width)
        wide[:entries] = vocab_ref[:, pl.ds(start, width)].astype(F32)
        block = wide[...]
        across_ref[:, at * width : (at + 1) * width] = block.astype(BF16)
        down_ref[at * width : (at + 1) * width] = block.T.astype(BF16)


def prepare(place, vocab_head, awaited):
    depth = vocab_head.shape[1]
    vmem = pl.BlockSpec(memory_space=pltpu.VMEM)
    return pl.pallas_call(
        prepare_kernel,
        in_specs=[
            pl.BlockSpec(memory_space=pltpu.SMEM),
            vmem,
            pl.BlockSpec(memory_space=pl.ANY),
        ],
        out_specs=[vmem, vmem],
        out_shape=[shape(PADDED, depth, dtype=BF16), shape(depth, PADDED, dtype=BF16)],
        scratch_shapes=[pltpu.VMEM((PADDED, depth // CHUNKS), F32)],
        compiler_params=pltpu.CompilerParams(vmem_limit_bytes=LIMIT),
        cost_estimate=cost(0, 6 * PADDED * depth),
    )(place, vocab_head, awaited)


def teacher_kernel(place, target_ref, down_ref, out_ref, total):
    width = down_ref.shape[0] // CHUNKS
    for at in range(CHUNKS):
        start = pl.multiple_of((place[16] ^ at) * width, width)
        product = jnp.dot(
            target_ref[:, pl.ds(start, width)],
            down_ref[at * width : (at + 1) * width],
            preferred_element_type=F32,
        )
        total[...] = product if at == 0 else total[...] + product
    for at in range(16):
        start = pl.multiple_of(place[17 + at] * 16, 16)
        out_ref[at * 16 : (at + 1) * 16] = total[pl.ds(start, 16)]


def teacher_logits(place, target_all, down):
    count, depth = target_all.shape
    return local_call(
        teacher_kernel,
        shape(count, PADDED),
        cost(2 * count * PADDED * depth, 2 * (count + PADDED) * depth),
        [pltpu.VMEM((count, PADDED), F32)],
    )(place, target_all, down)


def student_part(entries, core, firsts, seconds, teacher_ref, down_ref, out_ref):
    width = down_ref.shape[0] // CHUNKS
    rows = out_ref.shape[0]
    for at in range(CHUNKS):
        blocks = [ref[:, at * width : (at + 1) * width] for ref in firsts] + [seconds[at][...]]
        product = jnp.dot(
            jnp.concatenate(blocks, axis=0),
            down_ref[at * width : (at + 1) * width],
            preferred_element_type=F32,
        )
        out_ref[...] = product if at == 0 else out_ref[...] + product
    student, teacher = out_ref[...], teacher_ref[core * rows : (core + 1) * rows]
    real = lax.broadcasted_iota(jnp.int32, student.shape, 1) < entries
    exp_teacher = jnp.where(real, jnp.exp(teacher), 0.0)
    columns = [
        jnp.sum(exp_teacher, axis=1, keepdims=True),
        jnp.sum(jnp.where(real, jnp.exp(student), 0.0), axis=1, keepdims=True),
        jnp.sum(exp_teacher * (teacher - student), axis=1, keepdims=True),
    ]
    lane = lax.broadcasted_iota(jnp.int32, (rows, 128), 1)
    table = jnp.zeros((rows, 128), F32)
    for at, column in enumerate(columns):
        table = jnp.where(lane == at, column, table)
    return table


def packed(table):
    lanes = table.shape[1] // 2
    return jnp.concatenate([table[:, :lanes], table[:, lanes:]], axis=0)


def own_student_kernel(entries, *refs):
    teacher_ref, down_ref, out_ref, table_ref = refs[8:]
    table_ref[...] = student_part(
        entries, 0, refs[:4], refs[4:8], teacher_ref, down_ref, out_ref
    )


def other_student_kernel(entries, place, *refs):
    teacher_ref, down_ref, own_ref, out_ref, sums_ref, turned = refs[8:]
    other = student_part(entries, 1, refs[:4], refs[4:8], teacher_ref, down_ref, out_ref)
    for core, table in enumerate((own_ref[...], other)):
        for at in range(8):
            start = pl.multiple_of(place[core * 8 + at] * 16, 16)
            turned[pl.ds(start, 16)] = table[at * 16 : (at + 1) * 16]
    sums = packed(turned[...].T[:4])
    for at in range(sums_ref.shape[0]):
        sums_ref[at] = sums


def own_student(entries, blocks, teacher, down):
    rows = teacher.shape[0] // 2
    return local_call(
        functools.partial(own_student_kernel, entries),
        [shape(rows, PADDED), shape(rows, 128)],
        cost(2 * rows * down.size, 2 * down.size, 2 * rows * PADDED),
        scalars=False,
    )(*blocks, teacher, down)


def other_student(entries, place, blocks, teacher, down, table):
    rows = teacher.shape[0] // 2
    return local_call(
        functools.partial(other_student_kernel, entries),
        [shape(rows, PADDED), shape(32, 8, rows)],
        cost(2 * rows * down.size, 2 * down.size, 2 * rows * PADDED),
        [pltpu.VMEM((2 * rows, 128), F32)],
    )(place, *blocks, teacher, down, table)


def grad_kernel(core, place, teacher_ref, student_ref, logs_ref, across_ref, out_ref, table, turned):
    rows, depth = out_ref.shape
    width = depth // CHUNKS
    table[...] = jnp.concatenate(
        [logs_ref[...], jnp.zeros((120, 2 * rows), F32)], axis=0
    ).T
    for at in range(8):
        start = pl.multiple_of(place[core * 8 + at] * 16, 16)
        turned[at * 16 : (at + 1) * 16] = table[pl.ds(start, 16)]
    student = jnp.exp(student_ref[...] - turned[:, 1:2])
    teacher = jnp.exp(teacher_ref[core * rows : (core + 1) * rows] - turned[:, 0:1])
    grad = (student - teacher).astype(BF16)
    for at in range(CHUNKS):
        columns = slice(at * width, (at + 1) * width)
        out_ref[:, columns] = jnp.dot(
            grad, across_ref[:, columns], preferred_element_type=F32
        ).astype(BF16)


def grad_rows(core, place, teacher, student, logs, across):
    rows, depth = student.shape[0], across.shape[1]
    return local_call(
        functools.partial(grad_kernel, core),
        shape(rows, depth, dtype=BF16),
        cost(2 * rows * across.size, 2 * across.size, 2 * rows * PADDED),
        [pltpu.VMEM((2 * rows, 128), F32), pltpu.VMEM((rows, 128), F32)],
    )(place, teacher, student, logs, across)


def pass_kernel(*refs):
    pass


def settled(blocks, awaited):
    return pl.pallas_call(
        pass_kernel,
        in_specs=[pl.BlockSpec(memory_space=pl.ANY)] * (len(blocks) + 1),
        out_specs=[pl.BlockSpec(memory_space=pl.ANY)] * len(blocks),
        out_shape=[shape(*block.shape, dtype=block.dtype) for block in blocks],
        input_output_aliases={at: at for at in range(len(blocks))},
        compiler_params=pltpu.CompilerParams(vmem_limit_bytes=1024 * 1024),
        cost_estimate=cost(0, 0),
    )(*blocks, awaited)


def summed_parts(parts_ref):
    parts = [parts_ref[at] for at in range(parts_ref.shape[0])]
    while len(parts) > 1:
        parts = [parts[at] + parts[at + 1] for at in range(0, len(parts), 2)]
    return parts[0]


def total_kernel(parts_ref, out_ref):
    sums = summed_parts(parts_ref)
    for at in range(out_ref.shape[0]):
        out_ref[at] = sums


def log_kernel(parts_ref, out_ref):
    sums = summed_parts(parts_ref)
    sums = jnp.concatenate([sums[:4], sums[4:]], axis=1)
    logs = jnp.log(sums[:2])
    out_ref[...] = jnp.zeros(out_ref.shape, F32)
    out_ref[:2] = logs
    out_ref[2:3] = sums[2:3] / sums[:1] - logs[:1] + logs[1:]


def totalled(kernel, parts, *sizes):
    return local_call(
        kernel,
        shape(*sizes),
        cost(parts.size, 4 * parts.size),
        limit=2 * 1024 * 1024,
        scalars=False,
    )(parts)


def join_kernel(*refs):
    firsts, seconds, (first_ref, second_ref) = refs[:4], refs[4:8], refs[-2:]
    (rows, width), (block, _) = firsts[0].shape, seconds[0].shape
    for at in range(4):
        first_ref[:, at * width : (at + 1) * width] = firsts[at][...]
        second_ref[at * block : (at + 1) * block] = seconds[at][...]


def join(firsts, seconds, awaited):
    (rows, width), (block, across) = firsts[0].shape, seconds[0].shape
    vmem = pl.BlockSpec(memory_space=pltpu.VMEM)
    return pl.pallas_call(
        join_kernel,
        in_specs=[vmem] * 8 + [pl.BlockSpec(memory_space=pl.ANY)],
        out_specs=[vmem] * 2,
        out_shape=[
            shape(rows, 4 * width, dtype=BF16),
            shape(4 * block, across, dtype=BF16),
        ],
        compiler_params=pltpu.CompilerParams(vmem_limit_bytes=4 * 1024 * 1024),
        cost_estimate=cost(0, 16 * rows * width),
    )(*firsts, *seconds, pltpu.with_memory_space_constraint(awaited, pltpu.HBM))


def stack_kernel(*refs):
    blocks, out_ref = refs[:4], refs[-1]
    rows = blocks[0].shape[0]
    for at, block in enumerate(blocks):
        out_ref[at * rows : (at + 1) * rows] = block[...]


def stacked(blocks, awaited):
    rows, across = blocks[0].shape
    return pl.pallas_call(
        stack_kernel,
        in_specs=[pl.BlockSpec(memory_space=pltpu.VMEM)] * 4 + [pl.BlockSpec(memory_space=pl.ANY)],
        out_specs=pl.BlockSpec(memory_space=pltpu.VMEM),
        out_shape=shape(4 * rows, across, dtype=BF16),
        compiler_params=pltpu.CompilerParams(vmem_limit_bytes=4 * 1024 * 1024),
        cost_estimate=cost(0, 16 * rows * across),
    )(*blocks, awaited)


def heads_kernel(parts_ref, residual_ref, bias_ref, heads_ref, preact_ref):
    preact = summed_parts(parts_ref) + bias_ref[...]
    preact_ref[...] = preact
    heads = residual_ref[...].astype(F32) + preact * jax.nn.sigmoid(preact)
    for at in range(heads_ref.shape[0]):
        heads_ref[at] = heads.astype(BF16)


def heads_of(parts, residual, bias):
    rows, across = residual.shape
    return local_call(
        heads_kernel,
        [shape(8, rows, across, dtype=BF16), shape(rows, across)],
        cost(HEADS_COST, 4 * parts.size),
        limit=4 * 1024 * 1024,
        scalars=False,
    )(parts, residual, bias[None])


def gather_lines(heads):
    return exchange(heads, "z").transpose(1, 0, 2).reshape(heads.shape[1], -1)


def gather_heads(lines, target_all, teacher):
    half = lines.shape[0] // 2
    first, second = join(
        from_peers(lines[:half], "y"), from_peers(lines[half:], "x"), target_all
    )
    blocks = settled(from_peers(first, "x") + from_peers(second, "y"), teacher)
    return blocks, [swap(block, "c", 1) for block in blocks]


def scatter_grad(own, other):
    rows, depth = own.shape
    mine = (own.astype(F32) + swap(other, "c", 1).astype(F32)).astype(BF16)
    half = rows // 2
    block = half // 4
    width = depth // 4
    first = [mine[i * block : (i + 1) * block] for i in range(4)]
    second = [mine[half:, i * width : (i + 1) * width] for i in range(4)]
    first, second = summed(first, "x"), summed(second, "y")
    first = [first[:, i * width : (i + 1) * width] for i in range(4)]
    second = [second[i * block : (i + 1) * block] for i in range(4)]
    first, second = summed(first, "y"), summed(second, "x")
    lines = jnp.concatenate([first, second], axis=0)
    sent = lines.reshape(2 * block, 8, -1).transpose(1, 0, 2)
    return jnp.sum(exchange(sent, "z").astype(F32), axis=0)


def shards(log_hidden, positions, offsets, head_weight, head_bias, vocab_head):
    reps, vocs = 32, 8
    in_width, out_width = head_weight.shape
    own = positions.shape[0]
    count = own * reps
    rows = count // vocs
    at_x, at_y, at_c = lax.axis_index("x"), lax.axis_index("y"), lax.axis_index("c")
    voc_index = at_x * 2 + at_c
    taken = jnp.concatenate([positions, positions + offsets])
    taken = jnp.take(log_hidden, taken, axis=0, mode="clip")
    inputs = taken[:own]
    with jax.named_scope("gather_z"):
        blocks = lax.dynamic_slice_in_dim(
            taken.reshape(2, own, -1), voc_index * in_width, in_width, 2
        )
        input_cols = inputs.reshape(own, 4, 8, out_width).transpose(2, 0, 1, 3)
        sent = jnp.concatenate(
            [
                jnp.broadcast_to(blocks[0], (8, own, in_width)),
                jnp.broadcast_to(blocks[1], (8, own, in_width)),
                input_cols.reshape(8, own, -1),
            ],
            axis=2,
        )
        lines = exchange(sent, "z").reshape(8 * own, -1)
        input_lines, target_lines = lines[:, :in_width], lines[:, in_width : 2 * in_width]
        input_cols = lines[:, 2 * in_width :].reshape(-1, 4, out_width).transpose(1, 0, 2)
    with jax.named_scope("gather_inputs"):
        sent = jnp.concatenate(
            [jnp.broadcast_to(input_lines, (4, *input_lines.shape)), input_cols], axis=2
        )
        got = exchange(sent, "y")
        input_rows = got[:, :, :in_width].reshape(count, in_width)
        residual = got[:, :, in_width:].reshape(count, out_width)
        residual = lax.dynamic_slice_in_dim(residual, voc_index * rows, rows, 0)
    with jax.named_scope("head"):
        partial_pre = jnp.dot(input_rows, head_weight, preferred_element_type=F32)
        parts = exchange(partial_pre.reshape(vocs, rows, out_width), VOC)
        heads, preact = heads_of(parts, residual, head_bias)
    with jax.named_scope("gather_targets"):
        target_rows = stacked(from_peers(target_lines, "y"), partial_pre)
        target_all = lax.all_gather(target_rows, VOC, axis=1, tiled=True)
    steps = jnp.arange(16)
    order = ((at_x ^ (steps % 4)) * 2 + (at_c ^ (steps // 8))) * 2 + (steps // 4) % 2
    target_order = (order // 4 ^ at_y) * 4 + order % 4
    place = jnp.concatenate([order, at_y[None], target_order]).astype(jnp.int32)
    with jax.named_scope("gather_heads"):
        lines = gather_lines(heads)
    with jax.named_scope("teacher"):
        across, down = prepare(place, vocab_head, target_all)
        teacher = teacher_logits(place, target_all, down)
    with jax.named_scope("gather_heads"):
        own_blocks, other_blocks = gather_heads(lines, target_all, teacher)
    with jax.named_scope("student"):
        entries = vocab_head.shape[0]
        own_logits, table = own_student(entries, own_blocks, teacher, down)
        other_logits, sums = other_student(entries, place, other_blocks, teacher, down, table)
    with jax.named_scope("totals"):
        sums = totalled(total_kernel, exchange(sums, ("y", "x", "c")), 8, 8, count // 2)
        logs = totalled(log_kernel, exchange(sums, "z"), 8, count)
        loss = jnp.sum(logs[2]) / count
    with jax.named_scope("grad"):
        other_rows = grad_rows(1, place, teacher, other_logits, logs, across)
        own_rows = grad_rows(0, place, teacher, own_logits, logs, across)
    with jax.named_scope("reduce_grad"):
        grad_heads = scatter_grad(own_rows, other_rows)
    with jax.named_scope("finish"):
        sigma = jax.nn.sigmoid(preact)
        grad_pre = grad_heads * (sigma * (1.0 + preact * (1.0 - sigma)))
        bias_part = thirds(jnp.sum(grad_pre, axis=0))
        sent = jnp.concatenate(
            [grad_pre, bias_part, jnp.zeros((13, out_width), F32)], axis=0
        ).astype(BF16)
        got = gathered(sent, VOC, vocs)
        grad_all = got[:, :rows].reshape(count, out_width)
        grad_bias = jnp.sum(got[:, rows : rows + 3].astype(F32), axis=(0, 1))
        grad_weight = lax.dot_general(
            input_rows, grad_all, (((0,), (0,)), ((), ())), preferred_element_type=F32
        )
    return (loss, grad_weight, grad_bias)


def solution(mesh):
    fine = Mesh(mesh.devices.reshape(tuple(SIZES.values())), tuple(SIZES))
    return jax.shard_map(
        shards,
        mesh=fine,
        in_specs=(
            P(REP, None),
            P(REP),
            P(REP),
            P(VOC, REP),
            P(REP),
            P((*REP, *VOC), None),
        ),
        out_specs=(P(), P(VOC, REP), P(REP)),
        check_vma=False,
    )
```

```python
import functools

import jax
import jax.numpy as jnp
from jax import lax
from jax.experimental import pallas as pl
from jax.experimental.pallas import tpu as pltpu
from jax.sharding import Mesh, PartitionSpec as P

BF16 = jnp.bfloat16
F32 = jnp.float32
REP = ("y", "z")
VOC = ("x", "c")
CHUNKS = 4
PADDED = 512
LIMIT = 14 * 1024 * 1024
HEADS_COST = 60_000_000_000
SIZES = {"y": 4, "z": 8, "x": 4, "c": 2}


def exchange(blocks, axis):
    return lax.all_to_all(blocks, axis, split_axis=0, concat_axis=0, tiled=True)


def gathered(block, axis, count):
    return exchange(jnp.broadcast_to(block[None], (count, *block.shape)), axis)


def swap(block, axis, step):
    return lax.ppermute(block, axis, [(i, i ^ step) for i in range(SIZES[axis])])


def from_peers(block, axis):
    return [block] + [swap(block, axis, step) for step in range(1, SIZES[axis])]


def summed(blocks, axis):
    total = blocks[0].astype(F32)
    for step in range(1, SIZES[axis]):
        total = total + swap(blocks[step], axis, step).astype(F32)
    return total.astype(BF16)


def cost(flops, bytes_accessed, transcendentals=0):
    return pl.CostEstimate(
        flops=flops, bytes_accessed=bytes_accessed, transcendentals=transcendentals
    )


def local_call(kernel, out_shape, estimate, scratch=(), limit=LIMIT, scalars=True):
    def call(*operands):
        specs = [pl.BlockSpec(memory_space=pltpu.VMEM)] * len(operands)
        if scalars:
            specs[0] = pl.BlockSpec(memory_space=pltpu.SMEM)
        return pl.pallas_call(
            kernel,
            in_specs=specs,
            out_specs=jax.tree.map(lambda _: pl.BlockSpec(memory_space=pltpu.VMEM), out_shape),
            out_shape=out_shape,
            scratch_shapes=scratch,
            compiler_params=pltpu.CompilerParams(vmem_limit_bytes=limit),
            cost_estimate=estimate,
        )(*operands)

    return call


def shape(*sizes, dtype=F32):
    return jax.ShapeDtypeStruct(sizes, dtype)


def prepare_kernel(place, vocab_ref, down_ref, done_ref, wide):
    entries, depth = vocab_ref.shape
    width = depth // CHUNKS
    done_ref[...] = jnp.zeros(done_ref.shape, F32)
    wide[...] = jnp.zeros(wide.shape, F32)
    for at in range(CHUNKS):
        start = pl.multiple_of((place[16] ^ at) * width, width)
        wide[:entries] = vocab_ref[:, pl.ds(start, width)].astype(F32)
        down_ref[at * width : (at + 1) * width] = wide[...].T.astype(BF16)


def prepare(place, vocab_head):
    depth = vocab_head.shape[1]
    return local_call(
        prepare_kernel,
        [shape(depth, PADDED, dtype=BF16), shape(8, 128)],
        cost(0, 4 * PADDED * depth),
        [pltpu.VMEM((PADDED, depth // CHUNKS), F32)],
    )(place, vocab_head)


def teacher_kernel(place, target_ref, stored_ref, out_ref, down_ref, total, arrived):
    width = down_ref.shape[0] // CHUNKS
    copies = []
    for at in range(CHUNKS):
        rows = pl.ds(at * width, width)
        copies.append(
            pltpu.make_async_copy(stored_ref.at[rows], down_ref.at[rows], arrived.at[at])
        )
        copies[at].start()
    for at in range(CHUNKS):
        start = pl.multiple_of((place[16] ^ at) * width, width)
        copies[at].wait()
        product = jnp.dot(
            target_ref[:, pl.ds(start, width)],
            down_ref[at * width : (at + 1) * width],
            preferred_element_type=F32,
        )
        total[...] = product if at == 0 else total[...] + product
    for at in range(16):
        start = pl.multiple_of(place[17 + at] * 16, 16)
        out_ref[at * 16 : (at + 1) * 16] = total[pl.ds(start, 16)]


def teacher_logits(place, target_all, stored):
    count, depth = target_all.shape
    vmem = pl.BlockSpec(memory_space=pltpu.VMEM)
    return pl.pallas_call(
        teacher_kernel,
        in_specs=[
            pl.BlockSpec(memory_space=pltpu.SMEM),
            vmem,
            pl.BlockSpec(memory_space=pl.ANY),
        ],
        out_specs=[vmem, vmem],
        out_shape=[shape(count, PADDED), shape(*stored.shape, dtype=BF16)],
        scratch_shapes=[pltpu.VMEM((count, PADDED), F32), pltpu.SemaphoreType.DMA((CHUNKS,))],
        compiler_params=pltpu.CompilerParams(vmem_limit_bytes=LIMIT),
        cost_estimate=cost(2 * count * PADDED * depth, 2 * (count + PADDED) * depth),
    )(place, target_all, pltpu.with_memory_space_constraint(stored, pltpu.HBM))


def student_part(entries, core, firsts, seconds, teacher_ref, down_ref, out_ref):
    width = down_ref.shape[0] // CHUNKS
    rows = out_ref.shape[0]
    for at in range(CHUNKS):
        blocks = [ref[:, at * width : (at + 1) * width] for ref in firsts] + [seconds[at][...]]
        product = jnp.dot(
            jnp.concatenate(blocks, axis=0),
            down_ref[at * width : (at + 1) * width],
            preferred_element_type=F32,
        )
        out_ref[...] = product if at == 0 else out_ref[...] + product
    student, teacher = out_ref[...], teacher_ref[core * rows : (core + 1) * rows]
    real = lax.broadcasted_iota(jnp.int32, student.shape, 1) < entries
    exp_teacher = jnp.where(real, jnp.exp(teacher), 0.0)
    columns = [
        jnp.sum(exp_teacher, axis=1, keepdims=True),
        jnp.sum(jnp.where(real, jnp.exp(student), 0.0), axis=1, keepdims=True),
        jnp.sum(exp_teacher * (teacher - student), axis=1, keepdims=True),
    ]
    lane = lax.broadcasted_iota(jnp.int32, (rows, 128), 1)
    table = jnp.zeros((rows, 128), F32)
    for at, column in enumerate(columns):
        table = jnp.where(lane == at, column, table)
    return table


def packed(table):
    lanes = table.shape[1] // 2
    return jnp.concatenate([table[:, :lanes], table[:, lanes:]], axis=0)


def own_student_kernel(entries, *refs):
    teacher_ref, down_ref, out_ref, table_ref = refs[8:]
    table_ref[...] = student_part(
        entries, 0, refs[:4], refs[4:8], teacher_ref, down_ref, out_ref
    )


def other_student_kernel(entries, place, *refs):
    teacher_ref, down_ref, own_ref, out_ref, sums_ref, turned = refs[8:]
    other = student_part(entries, 1, refs[:4], refs[4:8], teacher_ref, down_ref, out_ref)
    for core, table in enumerate((own_ref[...], other)):
        for at in range(8):
            start = pl.multiple_of(place[core * 8 + at] * 16, 16)
            turned[pl.ds(start, 16)] = table[at * 16 : (at + 1) * 16]
    sums = packed(turned[...].T[:4])
    for at in range(sums_ref.shape[0]):
        sums_ref[at] = sums


def own_student(entries, blocks, teacher, down):
    rows = teacher.shape[0] // 2
    return local_call(
        functools.partial(own_student_kernel, entries),
        [shape(rows, PADDED), shape(rows, 128)],
        cost(2 * rows * down.size, 2 * down.size, 2 * rows * PADDED),
        scalars=False,
    )(*blocks, teacher, down)


def other_student(entries, place, blocks, teacher, down, table):
    rows = teacher.shape[0] // 2
    return local_call(
        functools.partial(other_student_kernel, entries),
        [shape(rows, PADDED), shape(32, 8, rows)],
        cost(2 * rows * down.size, 2 * down.size, 2 * rows * PADDED),
        [pltpu.VMEM((2 * rows, 128), F32)],
    )(place, *blocks, teacher, down, table)


def grad_kernel(core, place, teacher_ref, student_ref, logs_ref, vocab_ref, out_ref, table, turned):
    rows, depth = out_ref.shape
    entries, width = vocab_ref.shape[0], depth // CHUNKS
    table[...] = jnp.concatenate(
        [logs_ref[...], jnp.zeros((120, 2 * rows), F32)], axis=0
    ).T
    for at in range(8):
        start = pl.multiple_of(place[core * 8 + at] * 16, 16)
        turned[at * 16 : (at + 1) * 16] = table[pl.ds(start, 16)]
    student = jnp.exp(student_ref[...] - turned[:, 1:2])
    teacher = jnp.exp(teacher_ref[core * rows : (core + 1) * rows] - turned[:, 0:1])
    grad = (student - teacher)[:, :entries].astype(BF16)
    for at in range(CHUNKS):
        start = pl.multiple_of((place[16] ^ at) * width, width)
        out_ref[:, at * width : (at + 1) * width] = jnp.dot(
            grad, vocab_ref[:, pl.ds(start, width)], preferred_element_type=F32
        ).astype(BF16)


def grad_rows(core, place, teacher, student, logs, vocab_head):
    rows, depth = student.shape[0], vocab_head.shape[1]
    return local_call(
        functools.partial(grad_kernel, core),
        shape(rows, depth, dtype=BF16),
        cost(2 * rows * vocab_head.size, 2 * vocab_head.size, 2 * rows * PADDED),
        [pltpu.VMEM((2 * rows, 128), F32), pltpu.VMEM((rows, 128), F32)],
    )(place, teacher, student, logs, vocab_head)


def finish_kernel(parts_ref, preact_ref, out_ref):
    grad_heads = parts_ref[0].astype(F32)
    for at in range(1, parts_ref.shape[0]):
        grad_heads = grad_heads + parts_ref[at].astype(F32)
    preact = preact_ref[...]
    sigma = jax.nn.sigmoid(preact)
    grad_pre = grad_heads * (sigma * (1.0 + preact * (1.0 - sigma)))
    total = jnp.sum(grad_pre, axis=0, keepdims=True)
    high = total.astype(BF16).astype(F32)
    middle = (total - high).astype(BF16).astype(F32)
    row = lax.broadcasted_iota(jnp.int32, (16, grad_pre.shape[1]), 0)
    extra = jnp.where(row == 0, high, jnp.where(row == 1, middle, total - high - middle))
    extra = jnp.where(row < 3, extra, 0.0).astype(BF16)
    for at in range(out_ref.shape[0]):
        out_ref[at, : grad_pre.shape[0]] = grad_pre.astype(BF16)
        out_ref[at, grad_pre.shape[0] :] = extra


def finished(parts, preact):
    rows, across = preact.shape
    return local_call(
        finish_kernel,
        shape(8, rows + 16, across, dtype=BF16),
        cost(0, 4 * parts.size),
        limit=4 * 1024 * 1024,
        scalars=False,
    )(parts, preact)


def pass_kernel(*refs):
    pass


def settled(blocks, awaited):
    return pl.pallas_call(
        pass_kernel,
        in_specs=[pl.BlockSpec(memory_space=pl.ANY)] * (len(blocks) + 1),
        out_specs=[pl.BlockSpec(memory_space=pl.ANY)] * len(blocks),
        out_shape=[shape(*block.shape, dtype=block.dtype) for block in blocks],
        input_output_aliases={at: at for at in range(len(blocks))},
        compiler_params=pltpu.CompilerParams(vmem_limit_bytes=1024 * 1024),
        cost_estimate=cost(0, 0),
    )(*blocks, awaited)


def summed_parts(parts_ref):
    parts = [parts_ref[at] for at in range(parts_ref.shape[0])]
    while len(parts) > 1:
        parts = [parts[at] + parts[at + 1] for at in range(0, len(parts), 2)]
    return parts[0]


def total_kernel(parts_ref, out_ref):
    sums = summed_parts(parts_ref)
    for at in range(out_ref.shape[0]):
        out_ref[at] = sums


def log_kernel(parts_ref, out_ref):
    sums = summed_parts(parts_ref)
    sums = jnp.concatenate([sums[:4], sums[4:]], axis=1)
    logs = jnp.log(sums[:2])
    out_ref[...] = jnp.zeros(out_ref.shape, F32)
    out_ref[:2] = logs
    out_ref[2:3] = sums[2:3] / sums[:1] - logs[:1] + logs[1:]


def totalled(kernel, parts, *sizes):
    return local_call(
        kernel,
        shape(*sizes),
        cost(parts.size, 4 * parts.size),
        limit=2 * 1024 * 1024,
        scalars=False,
    )(parts)


def join_kernel(*refs):
    firsts, seconds, (first_ref, second_ref) = refs[:4], refs[4:8], refs[-2:]
    (rows, width), (block, _) = firsts[0].shape, seconds[0].shape
    for at in range(4):
        first_ref[:, at * width : (at + 1) * width] = firsts[at][...]
        second_ref[at * block : (at + 1) * block] = seconds[at][...]


def join(firsts, seconds, awaited):
    (rows, width), (block, across) = firsts[0].shape, seconds[0].shape
    vmem = pl.BlockSpec(memory_space=pltpu.VMEM)
    return pl.pallas_call(
        join_kernel,
        in_specs=[vmem] * 8 + [pl.BlockSpec(memory_space=pl.ANY)],
        out_specs=[vmem] * 2,
        out_shape=[
            shape(rows, 4 * width, dtype=BF16),
            shape(4 * block, across, dtype=BF16),
        ],
        compiler_params=pltpu.CompilerParams(vmem_limit_bytes=4 * 1024 * 1024),
        cost_estimate=cost(0, 16 * rows * width),
    )(*firsts, *seconds, pltpu.with_memory_space_constraint(awaited, pltpu.HBM))


def stack_kernel(*refs):
    blocks, out_ref = refs[:4], refs[-1]
    rows = blocks[0].shape[0]
    for at, block in enumerate(blocks):
        out_ref[at * rows : (at + 1) * rows] = block[...]


def stacked(blocks, awaited):
    rows, across = blocks[0].shape
    return pl.pallas_call(
        stack_kernel,
        in_specs=[pl.BlockSpec(memory_space=pltpu.VMEM)] * 4 + [pl.BlockSpec(memory_space=pl.ANY)],
        out_specs=pl.BlockSpec(memory_space=pltpu.VMEM),
        out_shape=shape(4 * rows, across, dtype=BF16),
        compiler_params=pltpu.CompilerParams(vmem_limit_bytes=4 * 1024 * 1024),
        cost_estimate=cost(0, 16 * rows * across),
    )(*blocks, awaited)


def heads_kernel(parts_ref, residual_ref, bias_ref, heads_ref, preact_ref):
    preact = summed_parts(parts_ref) + bias_ref[...]
    preact_ref[...] = preact
    heads = residual_ref[...].astype(F32) + preact * jax.nn.sigmoid(preact)
    for at in range(heads_ref.shape[0]):
        heads_ref[at] = heads.astype(BF16)


def heads_of(parts, residual, bias):
    rows, across = residual.shape
    return local_call(
        heads_kernel,
        [shape(8, rows, across, dtype=BF16), shape(rows, across)],
        cost(HEADS_COST, 4 * parts.size),
        limit=4 * 1024 * 1024,
        scalars=False,
    )(parts, residual, bias[None])


def gather_lines(heads):
    return exchange(heads, "z").transpose(1, 0, 2).reshape(heads.shape[1], -1)


def gather_heads(lines, target_all, teacher):
    half = lines.shape[0] // 2
    first, second = join(
        from_peers(lines[:half], "y"), from_peers(lines[half:], "x"), target_all
    )
    blocks = settled(from_peers(first, "x") + from_peers(second, "y"), teacher)
    return blocks, [swap(block, "c", 1) for block in blocks]


def scatter_grad(own, other):
    rows, depth = own.shape
    mine = (own.astype(F32) + swap(other, "c", 1).astype(F32)).astype(BF16)
    half = rows // 2
    block = half // 4
    width = depth // 4
    first = [mine[i * block : (i + 1) * block] for i in range(4)]
    second = [mine[half:, i * width : (i + 1) * width] for i in range(4)]
    first, second = summed(first, "x"), summed(second, "y")
    first = [first[:, i * width : (i + 1) * width] for i in range(4)]
    second = [second[i * block : (i + 1) * block] for i in range(4)]
    first, second = summed(first, "y"), summed(second, "x")
    lines = jnp.concatenate([first, second], axis=0)
    sent = lines.reshape(2 * block, 8, -1).transpose(1, 0, 2)
    return exchange(sent, "z")


def shards(log_hidden, positions, offsets, head_weight, head_bias, vocab_head):
    reps, vocs = 32, 8
    in_width, out_width = head_weight.shape
    own = positions.shape[0]
    count = own * reps
    rows = count // vocs
    at_x, at_y, at_c = lax.axis_index("x"), lax.axis_index("y"), lax.axis_index("c")
    voc_index = at_x * 2 + at_c
    taken = jnp.concatenate([positions, positions + offsets])
    taken = jnp.take(log_hidden, taken, axis=0, mode="clip")
    inputs = taken[:own]
    steps = jnp.arange(16)
    order = ((at_x ^ (steps % 4)) * 2 + (at_c ^ (steps // 8))) * 2 + (steps // 4) % 2
    target_order = (order // 4 ^ at_y) * 4 + order % 4
    place = jnp.concatenate([order, at_y[None], target_order]).astype(jnp.int32)
    with jax.named_scope("prepare"):
        stored, done = prepare(place, vocab_head)
    with jax.named_scope("gather_z"):
        blocks = lax.dynamic_slice_in_dim(
            taken.reshape(2, own, -1), voc_index * in_width, in_width, 2
        )
        input_cols = inputs.reshape(own, 4, 8, out_width).transpose(2, 0, 1, 3)
        sent = jnp.concatenate(
            [
                jnp.broadcast_to(blocks[0], (8, own, in_width)),
                jnp.broadcast_to(blocks[1], (8, own, in_width)),
                input_cols.reshape(8, own, -1),
            ],
            axis=2,
        )
        (lines,) = settled([exchange(sent, "z")], done)
        lines = lines.reshape(8 * own, -1)
        input_lines, target_lines = lines[:, :in_width], lines[:, in_width : 2 * in_width]
        input_cols = lines[:, 2 * in_width :].reshape(-1, 4, out_width).transpose(1, 0, 2)
    with jax.named_scope("gather_inputs"):
        sent = jnp.concatenate(
            [jnp.broadcast_to(input_lines, (4, *input_lines.shape)), input_cols], axis=2
        )
        got = exchange(sent, "y")
        input_rows = got[:, :, :in_width].reshape(count, in_width)
        residual = got[:, :, in_width:].reshape(count, out_width)
        residual = lax.dynamic_slice_in_dim(residual, voc_index * rows, rows, 0)
    with jax.named_scope("head"):
        partial_pre = jnp.dot(input_rows, head_weight, preferred_element_type=F32)
        parts = exchange(partial_pre.reshape(vocs, rows, out_width), VOC)
        heads, preact = heads_of(parts, residual, head_bias)
    with jax.named_scope("gather_targets"):
        target_rows = stacked(from_peers(target_lines, "y"), partial_pre)
        target_all = lax.all_gather(target_rows, VOC, axis=1, tiled=True)
    with jax.named_scope("gather_heads"):
        lines = gather_lines(heads)
    with jax.named_scope("teacher"):
        teacher, down = teacher_logits(place, target_all, stored)
    with jax.named_scope("gather_heads"):
        own_blocks, other_blocks = gather_heads(lines, target_all, teacher)
    with jax.named_scope("student"):
        entries = vocab_head.shape[0]
        own_logits, table = own_student(entries, own_blocks, teacher, down)
        other_logits, sums = other_student(entries, place, other_blocks, teacher, down, table)
    with jax.named_scope("totals"):
        sums = totalled(total_kernel, exchange(sums, ("y", "x", "c")), 8, 8, count // 2)
        logs = totalled(log_kernel, exchange(sums, "z"), 8, count)
        loss = jnp.sum(logs[2]) / count
    with jax.named_scope("grad"):
        other_rows = grad_rows(1, place, teacher, other_logits, logs, vocab_head)
        own_rows = grad_rows(0, place, teacher, own_logits, logs, vocab_head)
    with jax.named_scope("reduce_grad"):
        grad_parts = scatter_grad(own_rows, other_rows)
    with jax.named_scope("finish"):
        got = exchange(finished(grad_parts, preact), VOC)
        grad_all = got[:, :rows].reshape(count, out_width)
        grad_bias = jnp.sum(got[:, rows : rows + 3].astype(F32), axis=(0, 1))
        grad_weight = lax.dot_general(
            input_rows, grad_all, (((0,), (0,)), ((), ())), preferred_element_type=F32
        )
    return (loss, grad_weight, grad_bias)


def solution(mesh):
    fine = Mesh(mesh.devices.reshape(tuple(SIZES.values())), tuple(SIZES))
    return jax.shard_map(
        shards,
        mesh=fine,
        in_specs=(
            P(REP, None),
            P(REP),
            P(REP),
            P(VOC, REP),
            P(REP),
            P((*REP, *VOC), None),
        ),
        out_specs=(P(), P(VOC, REP), P(REP)),
        check_vma=False,
    )
```

```python
import functools

import jax
import jax.numpy as jnp
from jax import lax
from jax.experimental import pallas as pl
from jax.experimental.pallas import tpu as pltpu
from jax.sharding import Mesh, PartitionSpec as P

BF16 = jnp.bfloat16
F32 = jnp.float32
REP = ("y", "z")
VOC = ("x", "c")
CHUNKS = 4
PADDED = 512
LIMIT = 14 * 1024 * 1024
HEADS_COST = 60_000_000_000
SIZES = {"y": 4, "z": 8, "x": 4, "c": 2}


def exchange(blocks, axis):
    return lax.all_to_all(blocks, axis, split_axis=0, concat_axis=0, tiled=True)


def gathered(block, axis, count):
    return exchange(jnp.broadcast_to(block[None], (count, *block.shape)), axis)


PEERS = (0, 2, 3, 1)
SETTLED = (*PEERS, *(4 + at for at in PEERS))


def swap(block, axis, step):
    return lax.ppermute(block, axis, [(i, i ^ step) for i in range(SIZES[axis])])


def from_peers(block, axis):
    return [block] + [swap(block, axis, step) for step in range(1, SIZES[axis])]


def summed(blocks, axis):
    total = blocks[0].astype(F32)
    for step in range(1, SIZES[axis]):
        total = total + swap(blocks[step], axis, step).astype(F32)
    return total.astype(BF16)


def cost(flops, bytes_accessed, transcendentals=0):
    return pl.CostEstimate(
        flops=flops, bytes_accessed=bytes_accessed, transcendentals=transcendentals
    )


def local_call(kernel, out_shape, estimate, scratch=(), limit=LIMIT, scalars=True):
    def call(*operands):
        specs = [pl.BlockSpec(memory_space=pltpu.VMEM)] * len(operands)
        if scalars:
            specs[0] = pl.BlockSpec(memory_space=pltpu.SMEM)
        return pl.pallas_call(
            kernel,
            in_specs=specs,
            out_specs=jax.tree.map(lambda _: pl.BlockSpec(memory_space=pltpu.VMEM), out_shape),
            out_shape=out_shape,
            scratch_shapes=scratch,
            compiler_params=pltpu.CompilerParams(vmem_limit_bytes=limit),
            cost_estimate=estimate,
        )(*operands)

    return call


def shape(*sizes, dtype=F32):
    return jax.ShapeDtypeStruct(sizes, dtype)


def prepare_kernel(place, vocab_ref, down_ref, done_ref, wide):
    entries, depth = vocab_ref.shape
    width = depth // CHUNKS
    done_ref[...] = jnp.zeros(done_ref.shape, F32)
    wide[...] = jnp.zeros(wide.shape, F32)
    for at in range(CHUNKS):
        start = pl.multiple_of((place[16] ^ at) * width, width)
        wide[:entries] = vocab_ref[:, pl.ds(start, width)].astype(F32)
        down_ref[at * width : (at + 1) * width] = wide[...].T.astype(BF16)


def prepare(place, vocab_head):
    depth = vocab_head.shape[1]
    return local_call(
        prepare_kernel,
        [shape(depth, PADDED, dtype=BF16), shape(8, 128)],
        cost(0, 4 * PADDED * depth),
        [pltpu.VMEM((PADDED, depth // CHUNKS), F32)],
    )(place, vocab_head)


def teacher_kernel(place, target_ref, stored_ref, out_ref, down_ref, total, arrived):
    width = down_ref.shape[0] // CHUNKS
    copies = []
    for at in range(CHUNKS):
        rows = pl.ds(at * width, width)
        copies.append(
            pltpu.make_async_copy(stored_ref.at[rows], down_ref.at[rows], arrived.at[at])
        )
        copies[at].start()
    for at in range(CHUNKS):
        start = pl.multiple_of((place[16] ^ at) * width, width)
        copies[at].wait()
        product = jnp.dot(
            target_ref[:, pl.ds(start, width)],
            down_ref[at * width : (at + 1) * width],
            preferred_element_type=F32,
        )
        total[...] = product if at == 0 else total[...] + product
    for at in range(16):
        start = pl.multiple_of(place[17 + at] * 16, 16)
        out_ref[at * 16 : (at + 1) * 16] = total[pl.ds(start, 16)]


def teacher_logits(place, target_all, stored):
    count, depth = target_all.shape
    vmem = pl.BlockSpec(memory_space=pltpu.VMEM)
    return pl.pallas_call(
        teacher_kernel,
        in_specs=[
            pl.BlockSpec(memory_space=pltpu.SMEM),
            vmem,
            pl.BlockSpec(memory_space=pl.ANY),
        ],
        out_specs=[vmem, vmem],
        out_shape=[shape(count, PADDED), shape(*stored.shape, dtype=BF16)],
        scratch_shapes=[pltpu.VMEM((count, PADDED), F32), pltpu.SemaphoreType.DMA((CHUNKS,))],
        compiler_params=pltpu.CompilerParams(vmem_limit_bytes=LIMIT),
        cost_estimate=cost(2 * count * PADDED * depth, 2 * (count + PADDED) * depth),
    )(place, target_all, pltpu.with_memory_space_constraint(stored, pltpu.HBM))


def student_part(entries, core, firsts, seconds, teacher_ref, down_ref, out_ref):
    width = down_ref.shape[0] // CHUNKS
    rows = out_ref.shape[0]
    for at in range(CHUNKS):
        blocks = [ref[:, at * width : (at + 1) * width] for ref in firsts] + [seconds[at][...]]
        product = jnp.dot(
            jnp.concatenate(blocks, axis=0),
            down_ref[at * width : (at + 1) * width],
            preferred_element_type=F32,
        )
        out_ref[...] = product if at == 0 else out_ref[...] + product
    student, teacher = out_ref[...], teacher_ref[core * rows : (core + 1) * rows]
    real = lax.broadcasted_iota(jnp.int32, student.shape, 1) < entries
    exp_teacher = jnp.where(real, jnp.exp(teacher), 0.0)
    columns = [
        jnp.sum(exp_teacher, axis=1, keepdims=True),
        jnp.sum(jnp.where(real, jnp.exp(student), 0.0), axis=1, keepdims=True),
        jnp.sum(exp_teacher * (teacher - student), axis=1, keepdims=True),
    ]
    lane = lax.broadcasted_iota(jnp.int32, (rows, 128), 1)
    table = jnp.zeros((rows, 128), F32)
    for at, column in enumerate(columns):
        table = jnp.where(lane == at, column, table)
    return table


def packed(table):
    lanes = table.shape[1] // 2
    return jnp.concatenate([table[:, :lanes], table[:, lanes:]], axis=0)


def own_student_kernel(entries, *refs):
    teacher_ref, down_ref, out_ref, table_ref = refs[8:]
    table_ref[...] = student_part(
        entries, 0, refs[:4], refs[4:8], teacher_ref, down_ref, out_ref
    )


def other_student_kernel(entries, place, *refs):
    teacher_ref, down_ref, own_ref, out_ref, sums_ref, turned = refs[8:]
    other = student_part(entries, 1, refs[:4], refs[4:8], teacher_ref, down_ref, out_ref)
    for core, table in enumerate((own_ref[...], other)):
        for at in range(8):
            start = pl.multiple_of(place[core * 8 + at] * 16, 16)
            turned[pl.ds(start, 16)] = table[at * 16 : (at + 1) * 16]
    sums = packed(turned[...].T[:4])
    for at in range(sums_ref.shape[0]):
        sums_ref[at] = sums


def own_student(entries, blocks, teacher, down):
    rows = teacher.shape[0] // 2
    return local_call(
        functools.partial(own_student_kernel, entries),
        [shape(rows, PADDED), shape(rows, 128)],
        cost(2 * rows * down.size, 2 * down.size, 2 * rows * PADDED),
        scalars=False,
    )(*blocks, teacher, down)


def other_student(entries, place, blocks, teacher, down, table):
    rows = teacher.shape[0] // 2
    return local_call(
        functools.partial(other_student_kernel, entries),
        [shape(rows, PADDED), shape(32, 8, rows)],
        cost(2 * rows * down.size, 2 * down.size, 2 * rows * PADDED),
        [pltpu.VMEM((2 * rows, 128), F32)],
    )(place, *blocks, teacher, down, table)


def grad_kernel(core, place, teacher_ref, student_ref, logs_ref, vocab_ref, out_ref, table, turned):
    rows, depth = out_ref.shape
    entries, width = vocab_ref.shape[0], depth // CHUNKS
    table[...] = jnp.concatenate(
        [logs_ref[...], jnp.zeros((120, 2 * rows), F32)], axis=0
    ).T
    for at in range(8):
        start = pl.multiple_of(place[core * 8 + at] * 16, 16)
        turned[at * 16 : (at + 1) * 16] = table[pl.ds(start, 16)]
    student = jnp.exp(student_ref[...] - turned[:, 1:2])
    teacher = jnp.exp(teacher_ref[core * rows : (core + 1) * rows] - turned[:, 0:1])
    grad = (student - teacher)[:, :entries].astype(BF16)
    for at in range(CHUNKS):
        start = pl.multiple_of((place[16] ^ at) * width, width)
        out_ref[:, at * width : (at + 1) * width] = jnp.dot(
            grad, vocab_ref[:, pl.ds(start, width)], preferred_element_type=F32
        ).astype(BF16)


def grad_rows(core, place, teacher, student, logs, vocab_head):
    rows, depth = student.shape[0], vocab_head.shape[1]
    return local_call(
        functools.partial(grad_kernel, core),
        shape(rows, depth, dtype=BF16),
        cost(2 * rows * vocab_head.size, 2 * vocab_head.size, 2 * rows * PADDED),
        [pltpu.VMEM((2 * rows, 128), F32), pltpu.VMEM((rows, 128), F32)],
    )(place, teacher, student, logs, vocab_head)


def finish_kernel(parts_ref, preact_ref, out_ref):
    grad_heads = parts_ref[0].astype(F32)
    for at in range(1, parts_ref.shape[0]):
        grad_heads = grad_heads + parts_ref[at].astype(F32)
    preact = preact_ref[...]
    sigma = jax.nn.sigmoid(preact)
    grad_pre = grad_heads * (sigma * (1.0 + preact * (1.0 - sigma)))
    total = jnp.sum(grad_pre, axis=0, keepdims=True)
    high = total.astype(BF16).astype(F32)
    middle = (total - high).astype(BF16).astype(F32)
    row = lax.broadcasted_iota(jnp.int32, (16, grad_pre.shape[1]), 0)
    extra = jnp.where(row == 0, high, jnp.where(row == 1, middle, total - high - middle))
    extra = jnp.where(row < 3, extra, 0.0).astype(BF16)
    for at in range(out_ref.shape[0]):
        out_ref[at, : grad_pre.shape[0]] = grad_pre.astype(BF16)
        out_ref[at, grad_pre.shape[0] :] = extra


def finished(parts, preact):
    rows, across = preact.shape
    return local_call(
        finish_kernel,
        shape(8, rows + 16, across, dtype=BF16),
        cost(0, 4 * parts.size),
        limit=4 * 1024 * 1024,
        scalars=False,
    )(parts, preact)


def pass_kernel(*refs):
    pass


def settled(blocks, awaited):
    return pl.pallas_call(
        pass_kernel,
        in_specs=[pl.BlockSpec(memory_space=pl.ANY)] * (len(blocks) + 1),
        out_specs=[pl.BlockSpec(memory_space=pl.ANY)] * len(blocks),
        out_shape=[shape(*block.shape, dtype=block.dtype) for block in blocks],
        input_output_aliases={at: at for at in range(len(blocks))},
        compiler_params=pltpu.CompilerParams(vmem_limit_bytes=1024 * 1024),
        cost_estimate=cost(0, 0),
    )(*blocks, awaited)


def summed_parts(parts_ref):
    parts = [parts_ref[at] for at in range(parts_ref.shape[0])]
    while len(parts) > 1:
        parts = [parts[at] + parts[at + 1] for at in range(0, len(parts), 2)]
    return parts[0]


def total_kernel(parts_ref, out_ref):
    sums = summed_parts(parts_ref)
    for at in range(out_ref.shape[0]):
        out_ref[at] = sums


def log_kernel(parts_ref, out_ref):
    sums = summed_parts(parts_ref)
    sums = jnp.concatenate([sums[:4], sums[4:]], axis=1)
    logs = jnp.log(sums[:2])
    out_ref[...] = jnp.zeros(out_ref.shape, F32)
    out_ref[:2] = logs
    out_ref[2:3] = sums[2:3] / sums[:1] - logs[:1] + logs[1:]


def totalled(kernel, parts, *sizes):
    return local_call(
        kernel,
        shape(*sizes),
        cost(parts.size, 4 * parts.size),
        limit=2 * 1024 * 1024,
        scalars=False,
    )(parts)


def join_kernel(*refs):
    firsts, seconds, (first_ref, second_ref) = refs[:4], refs[4:8], refs[-2:]
    (rows, width), (block, _) = firsts[0].shape, seconds[0].shape
    for at, peer in enumerate(PEERS):
        first_ref[:, peer * width : (peer + 1) * width] = firsts[at][...]
        second_ref[peer * block : (peer + 1) * block] = seconds[at][...]


def join(firsts, seconds, awaited):
    (rows, width), (block, across) = firsts[0].shape, seconds[0].shape
    firsts, seconds = [firsts[peer] for peer in PEERS], [seconds[peer] for peer in PEERS]
    vmem = pl.BlockSpec(memory_space=pltpu.VMEM)
    return pl.pallas_call(
        join_kernel,
        in_specs=[vmem] * 8 + [pl.BlockSpec(memory_space=pl.ANY)],
        out_specs=[vmem] * 2,
        out_shape=[
            shape(rows, 4 * width, dtype=BF16),
            shape(4 * block, across, dtype=BF16),
        ],
        compiler_params=pltpu.CompilerParams(vmem_limit_bytes=4 * 1024 * 1024),
        cost_estimate=cost(0, 16 * rows * width),
    )(*firsts, *seconds, pltpu.with_memory_space_constraint(awaited, pltpu.HBM))


def stack_kernel(*refs):
    blocks, out_ref = refs[:4], refs[-1]
    rows = blocks[0].shape[0]
    for at, block in enumerate(blocks):
        out_ref[at * rows : (at + 1) * rows] = block[...]


def stacked(blocks, awaited):
    rows, across = blocks[0].shape
    return pl.pallas_call(
        stack_kernel,
        in_specs=[pl.BlockSpec(memory_space=pltpu.VMEM)] * 4 + [pl.BlockSpec(memory_space=pl.ANY)],
        out_specs=pl.BlockSpec(memory_space=pltpu.VMEM),
        out_shape=shape(4 * rows, across, dtype=BF16),
        compiler_params=pltpu.CompilerParams(vmem_limit_bytes=4 * 1024 * 1024),
        cost_estimate=cost(0, 16 * rows * across),
    )(*blocks, awaited)


def heads_kernel(parts_ref, residual_ref, bias_ref, heads_ref, preact_ref):
    preact = summed_parts(parts_ref) + bias_ref[...]
    preact_ref[...] = preact
    heads = residual_ref[...].astype(F32) + preact * jax.nn.sigmoid(preact)
    for at in range(heads_ref.shape[0]):
        heads_ref[at] = heads.astype(BF16)


def heads_of(parts, residual, bias):
    rows, across = residual.shape
    return local_call(
        heads_kernel,
        [shape(8, rows, across, dtype=BF16), shape(rows, across)],
        cost(HEADS_COST, 4 * parts.size),
        limit=4 * 1024 * 1024,
        scalars=False,
    )(parts, residual, bias[None])


def gather_lines(heads):
    return exchange(heads, "z").transpose(1, 0, 2).reshape(heads.shape[1], -1)


def gather_heads(lines, target_all, teacher):
    half = lines.shape[0] // 2
    first, second = join(
        from_peers(lines[:half], "y"), from_peers(lines[half:], "x"), target_all
    )
    blocks = from_peers(first, "x") + from_peers(second, "y")
    blocks = settled([blocks[at] for at in SETTLED], teacher)
    blocks = [blocks[SETTLED.index(at)] for at in range(8)]
    return blocks, [swap(block, "c", 1) for block in blocks]


def scatter_grad(own, other):
    rows, depth = own.shape
    mine = (own.astype(F32) + swap(other, "c", 1).astype(F32)).astype(BF16)
    half = rows // 2
    block = half // 4
    width = depth // 4
    first = [mine[i * block : (i + 1) * block] for i in range(4)]
    second = [mine[half:, i * width : (i + 1) * width] for i in range(4)]
    first, second = summed(first, "x"), summed(second, "y")
    first = [first[:, i * width : (i + 1) * width] for i in range(4)]
    second = [second[i * block : (i + 1) * block] for i in range(4)]
    first, second = summed(first, "y"), summed(second, "x")
    lines = jnp.concatenate([first, second], axis=0)
    sent = lines.reshape(2 * block, 8, -1).transpose(1, 0, 2)
    return exchange(sent, "z")


def shards(log_hidden, positions, offsets, head_weight, head_bias, vocab_head):
    reps, vocs = 32, 8
    in_width, out_width = head_weight.shape
    own = positions.shape[0]
    count = own * reps
    rows = count // vocs
    at_x, at_y, at_c = lax.axis_index("x"), lax.axis_index("y"), lax.axis_index("c")
    voc_index = at_x * 2 + at_c
    taken = jnp.concatenate([positions, positions + offsets])
    taken = jnp.take(log_hidden, taken, axis=0, mode="clip")
    inputs = taken[:own]
    steps = jnp.arange(16)
    order = ((at_x ^ (steps % 4)) * 2 + (at_c ^ (steps // 8))) * 2 + (steps // 4) % 2
    target_order = (order // 4 ^ at_y) * 4 + order % 4
    place = jnp.concatenate([order, at_y[None], target_order]).astype(jnp.int32)
    with jax.named_scope("prepare"):
        stored, done = prepare(place, vocab_head)
    with jax.named_scope("gather_z"):
        blocks = lax.dynamic_slice_in_dim(
            taken.reshape(2, own, -1), voc_index * in_width, in_width, 2
        )
        input_cols = inputs.reshape(own, 4, 8, out_width).transpose(2, 0, 1, 3)
        sent = jnp.concatenate(
            [
                jnp.broadcast_to(blocks[0], (8, own, in_width)),
                jnp.broadcast_to(blocks[1], (8, own, in_width)),
                input_cols.reshape(8, own, -1),
            ],
            axis=2,
        )
        (lines,) = settled([exchange(sent, "z")], done)
        lines = lines.reshape(8 * own, -1)
        input_lines, target_lines = lines[:, :in_width], lines[:, in_width : 2 * in_width]
        input_cols = lines[:, 2 * in_width :].reshape(-1, 4, out_width).transpose(1, 0, 2)
    with jax.named_scope("gather_inputs"):
        sent = jnp.concatenate(
            [jnp.broadcast_to(input_lines, (4, *input_lines.shape)), input_cols], axis=2
        )
        got = exchange(sent, "y")
        input_rows = got[:, :, :in_width].reshape(count, in_width)
        residual = got[:, :, in_width:].reshape(count, out_width)
        residual = lax.dynamic_slice_in_dim(residual, voc_index * rows, rows, 0)
    with jax.named_scope("head"):
        partial_pre = jnp.dot(input_rows, head_weight, preferred_element_type=F32)
        parts = exchange(partial_pre.reshape(vocs, rows, out_width), VOC)
        heads, preact = heads_of(parts, residual, head_bias)
    with jax.named_scope("gather_targets"):
        target_rows = stacked(from_peers(target_lines, "y"), partial_pre)
        target_all = lax.all_gather(target_rows, VOC, axis=1, tiled=True)
    with jax.named_scope("gather_heads"):
        lines = gather_lines(heads)
    with jax.named_scope("teacher"):
        teacher, down = teacher_logits(place, target_all, stored)
    with jax.named_scope("gather_heads"):
        own_blocks, other_blocks = gather_heads(lines, target_all, teacher)
    with jax.named_scope("student"):
        entries = vocab_head.shape[0]
        own_logits, table = own_student(entries, own_blocks, teacher, down)
        other_logits, sums = other_student(entries, place, other_blocks, teacher, down, table)
    with jax.named_scope("totals"):
        sums = totalled(total_kernel, exchange(sums, ("y", "x", "c")), 8, 8, count // 2)
        logs = totalled(log_kernel, exchange(sums, "z"), 8, count)
        loss = jnp.sum(logs[2]) / count
    with jax.named_scope("grad"):
        other_rows = grad_rows(1, place, teacher, other_logits, logs, vocab_head)
        own_rows = grad_rows(0, place, teacher, own_logits, logs, vocab_head)
    with jax.named_scope("reduce_grad"):
        grad_parts = scatter_grad(own_rows, other_rows)
    with jax.named_scope("finish"):
        got = exchange(finished(grad_parts, preact), VOC)
        grad_all = got[:, :rows].reshape(count, out_width)
        grad_bias = jnp.sum(got[:, rows : rows + 3].astype(F32), axis=(0, 1))
        grad_weight = lax.dot_general(
            input_rows, grad_all, (((0,), (0,)), ((), ())), preferred_element_type=F32
        )
    return (loss, grad_weight, grad_bias)


def solution(mesh):
    fine = Mesh(mesh.devices.reshape(tuple(SIZES.values())), tuple(SIZES))
    return jax.shard_map(
        shards,
        mesh=fine,
        in_specs=(
            P(REP, None),
            P(REP),
            P(REP),
            P(VOC, REP),
            P(REP),
            P((*REP, *VOC), None),
        ),
        out_specs=(P(), P(VOC, REP), P(REP)),
        check_vma=False,
    )
```

```python
import functools

import jax
import jax.numpy as jnp
from jax import lax
from jax.experimental import pallas as pl
from jax.experimental.pallas import tpu as pltpu
from jax.sharding import Mesh, PartitionSpec as P

BF16 = jnp.bfloat16
F32 = jnp.float32
REP = ("y", "z")
VOC = ("x", "c")
CHUNKS = 4
PADDED = 512
LIMIT = 14 * 1024 * 1024
HEADS_COST = 110_000_000_000
SIZES = {"y": 4, "z": 8, "x": 4, "c": 2}


def exchange(blocks, axis):
    return lax.all_to_all(blocks, axis, split_axis=0, concat_axis=0, tiled=True)


def gathered(block, axis, count):
    return exchange(jnp.broadcast_to(block[None], (count, *block.shape)), axis)


PEERS = (0, 2, 3, 1)
SETTLED = (*PEERS, *(4 + at for at in PEERS))


def swap(block, axis, step):
    return lax.ppermute(block, axis, [(i, i ^ step) for i in range(SIZES[axis])])


def from_peers(block, axis):
    return [block] + [swap(block, axis, step) for step in range(1, SIZES[axis])]


def summed(blocks, axis):
    total = blocks[0].astype(F32)
    for step in range(1, SIZES[axis]):
        total = total + swap(blocks[step], axis, step).astype(F32)
    return total.astype(BF16)


def cost(flops, bytes_accessed, transcendentals=0):
    return pl.CostEstimate(
        flops=flops, bytes_accessed=bytes_accessed, transcendentals=transcendentals
    )


def local_call(kernel, out_shape, estimate, scratch=(), limit=LIMIT, scalars=True):
    def call(*operands):
        specs = [pl.BlockSpec(memory_space=pltpu.VMEM)] * len(operands)
        if scalars:
            specs[0] = pl.BlockSpec(memory_space=pltpu.SMEM)
        return pl.pallas_call(
            kernel,
            in_specs=specs,
            out_specs=jax.tree.map(lambda _: pl.BlockSpec(memory_space=pltpu.VMEM), out_shape),
            out_shape=out_shape,
            scratch_shapes=scratch,
            compiler_params=pltpu.CompilerParams(vmem_limit_bytes=limit),
            cost_estimate=estimate,
        )(*operands)

    return call


def shape(*sizes, dtype=F32):
    return jax.ShapeDtypeStruct(sizes, dtype)


def taken_kernel(in_width, out_width, voc, positions, offsets, log_ref, out_ref):
    own, rows = positions.shape[0], log_ref.shape[0]
    row = lax.broadcasted_iota(jnp.int32, (own, rows), 0)
    column = lax.broadcasted_iota(jnp.int32, (own, rows), 1)
    source = jnp.zeros((own, rows), jnp.int32)
    target = source
    for at in range(own):
        source = jnp.where(row == at, positions[at], source)
        target = jnp.where(row == at, positions[at] + offsets[at], target)
    source = jnp.where(source == column, 1.0, 0.0).astype(BF16)
    target = jnp.where(target == column, 1.0, 0.0).astype(BF16)
    block = log_ref[:, pl.ds(pl.multiple_of(voc[0] * in_width, in_width), in_width)]
    inputs = jnp.dot(source, block, preferred_element_type=F32)
    targets = jnp.dot(target, block, preferred_element_type=F32)
    every = jnp.dot(source, log_ref[...], preferred_element_type=F32)
    parts = []
    for z in range(8):
        starts = [(y * 8 + z) * out_width for y in range(4)]
        parts.append(jnp.concatenate([every[:, at : at + out_width] for at in starts], axis=1))
    out_ref[:, :in_width] = jnp.concatenate([inputs] * 8, axis=0).astype(BF16)
    out_ref[:, in_width : 2 * in_width] = jnp.concatenate([targets] * 8, axis=0).astype(BF16)
    out_ref[:, 2 * in_width :] = jnp.concatenate(parts, axis=0).astype(BF16)


def taken(voc, positions, offsets, log_hidden, in_width, out_width):
    own = positions.shape[0]
    smem, vmem = (pl.BlockSpec(memory_space=kind) for kind in (pltpu.SMEM, pltpu.VMEM))
    return pl.pallas_call(
        functools.partial(taken_kernel, in_width, out_width),
        in_specs=[smem, smem, smem, vmem],
        out_specs=vmem,
        out_shape=shape(8 * own, 2 * in_width + 4 * out_width, dtype=BF16),
        compiler_params=pltpu.CompilerParams(vmem_limit_bytes=8 * 1024 * 1024),
        cost_estimate=cost(4 * own * log_hidden.size, 2 * log_hidden.size),
    )(voc, positions, offsets, log_hidden)


def prepare_kernel(place, vocab_ref, down_ref, done_ref, wide):
    entries, depth = vocab_ref.shape
    width = depth // CHUNKS
    done_ref[...] = jnp.zeros(done_ref.shape, F32)
    wide[...] = jnp.zeros(wide.shape, F32)
    for at in range(CHUNKS):
        start = pl.multiple_of((place[16] ^ at) * width, width)
        wide[:entries] = vocab_ref[:, pl.ds(start, width)].astype(F32)
        down_ref[at * width : (at + 1) * width] = wide[...].T.astype(BF16)


def prepare(place, vocab_head):
    depth = vocab_head.shape[1]
    return local_call(
        prepare_kernel,
        [shape(depth, PADDED, dtype=BF16), shape(8, 128)],
        cost(0, 4 * PADDED * depth),
        [pltpu.VMEM((PADDED, depth // CHUNKS), F32)],
    )(place, vocab_head)


def teacher_kernel(place, target_ref, stored_ref, out_ref, down_ref, total, arrived):
    width = down_ref.shape[0] // CHUNKS
    copies = []
    for at in range(CHUNKS):
        rows = pl.ds(at * width, width)
        copies.append(
            pltpu.make_async_copy(stored_ref.at[rows], down_ref.at[rows], arrived.at[at])
        )
        copies[at].start()
    for at in range(CHUNKS):
        start = pl.multiple_of((place[16] ^ at) * width, width)
        copies[at].wait()
        product = jnp.dot(
            target_ref[:, pl.ds(start, width)],
            down_ref[at * width : (at + 1) * width],
            preferred_element_type=F32,
        )
        total[...] = product if at == 0 else total[...] + product
    for at in range(16):
        start = pl.multiple_of(place[17 + at] * 16, 16)
        out_ref[at * 16 : (at + 1) * 16] = total[pl.ds(start, 16)]


def teacher_logits(place, target_all, stored):
    count, depth = target_all.shape
    vmem = pl.BlockSpec(memory_space=pltpu.VMEM)
    return pl.pallas_call(
        teacher_kernel,
        in_specs=[
            pl.BlockSpec(memory_space=pltpu.SMEM),
            vmem,
            pl.BlockSpec(memory_space=pl.ANY),
        ],
        out_specs=[vmem, vmem],
        out_shape=[shape(count, PADDED), shape(*stored.shape, dtype=BF16)],
        scratch_shapes=[pltpu.VMEM((count, PADDED), F32), pltpu.SemaphoreType.DMA((CHUNKS,))],
        compiler_params=pltpu.CompilerParams(vmem_limit_bytes=LIMIT),
        cost_estimate=cost(2 * count * PADDED * depth, 2 * (count + PADDED) * depth),
    )(place, target_all, pltpu.with_memory_space_constraint(stored, pltpu.HBM))


def student_part(entries, core, firsts, seconds, teacher_ref, down_ref, out_ref):
    width = down_ref.shape[0] // CHUNKS
    rows = out_ref.shape[0]
    for at in range(CHUNKS):
        blocks = [ref[:, at * width : (at + 1) * width] for ref in firsts] + [seconds[at][...]]
        product = jnp.dot(
            jnp.concatenate(blocks, axis=0),
            down_ref[at * width : (at + 1) * width],
            preferred_element_type=F32,
        )
        out_ref[...] = product if at == 0 else out_ref[...] + product
    student, teacher = out_ref[...], teacher_ref[core * rows : (core + 1) * rows]
    real = lax.broadcasted_iota(jnp.int32, student.shape, 1) < entries
    exp_teacher = jnp.where(real, jnp.exp(teacher), 0.0)
    columns = [
        jnp.sum(exp_teacher, axis=1, keepdims=True),
        jnp.sum(jnp.where(real, jnp.exp(student), 0.0), axis=1, keepdims=True),
        jnp.sum(exp_teacher * (teacher - student), axis=1, keepdims=True),
    ]
    lane = lax.broadcasted_iota(jnp.int32, (rows, 128), 1)
    table = jnp.zeros((rows, 128), F32)
    for at, column in enumerate(columns):
        table = jnp.where(lane == at, column, table)
    return table


def packed(table):
    lanes = table.shape[1] // 2
    return jnp.concatenate([table[:, :lanes], table[:, lanes:]], axis=0)


def own_student_kernel(entries, *refs):
    teacher_ref, down_ref, out_ref, table_ref = refs[8:]
    table_ref[...] = student_part(
        entries, 0, refs[:4], refs[4:8], teacher_ref, down_ref, out_ref
    )


def other_student_kernel(entries, place, *refs):
    teacher_ref, down_ref, own_ref, out_ref, sums_ref, turned = refs[8:]
    other = student_part(entries, 1, refs[:4], refs[4:8], teacher_ref, down_ref, out_ref)
    for core, table in enumerate((own_ref[...], other)):
        for at in range(8):
            start = pl.multiple_of(place[core * 8 + at] * 16, 16)
            turned[pl.ds(start, 16)] = table[at * 16 : (at + 1) * 16]
    sums = packed(turned[...].T[:4])
    for at in range(sums_ref.shape[0]):
        sums_ref[at] = sums


def own_student(entries, blocks, teacher, down):
    rows = teacher.shape[0] // 2
    return local_call(
        functools.partial(own_student_kernel, entries),
        [shape(rows, PADDED), shape(rows, 128)],
        cost(2 * rows * down.size, 2 * down.size, 2 * rows * PADDED),
        scalars=False,
    )(*blocks, teacher, down)


def other_student(entries, place, blocks, teacher, down, table):
    rows = teacher.shape[0] // 2
    return local_call(
        functools.partial(other_student_kernel, entries),
        [shape(rows, PADDED), shape(32, 8, rows)],
        cost(2 * rows * down.size, 2 * down.size, 2 * rows * PADDED),
        [pltpu.VMEM((2 * rows, 128), F32)],
    )(place, *blocks, teacher, down, table)


def grad_kernel(core, place, teacher_ref, student_ref, logs_ref, vocab_ref, out_ref, table, turned):
    rows, depth = out_ref.shape
    entries, width = vocab_ref.shape[0], depth // CHUNKS
    table[...] = jnp.concatenate(
        [logs_ref[...], jnp.zeros((120, 2 * rows), F32)], axis=0
    ).T
    for at in range(8):
        start = pl.multiple_of(place[core * 8 + at] * 16, 16)
        turned[at * 16 : (at + 1) * 16] = table[pl.ds(start, 16)]
    student = jnp.exp(student_ref[...] - turned[:, 1:2])
    teacher = jnp.exp(teacher_ref[core * rows : (core + 1) * rows] - turned[:, 0:1])
    grad = (student - teacher)[:, :entries].astype(BF16)
    for at in range(CHUNKS):
        start = pl.multiple_of((place[16] ^ at) * width, width)
        out_ref[:, at * width : (at + 1) * width] = jnp.dot(
            grad, vocab_ref[:, pl.ds(start, width)], preferred_element_type=F32
        ).astype(BF16)


def grad_rows(core, place, teacher, student, logs, vocab_head):
    rows, depth = student.shape[0], vocab_head.shape[1]
    return local_call(
        functools.partial(grad_kernel, core),
        shape(rows, depth, dtype=BF16),
        cost(2 * rows * vocab_head.size, 2 * vocab_head.size, 2 * rows * PADDED),
        [pltpu.VMEM((2 * rows, 128), F32), pltpu.VMEM((rows, 128), F32)],
    )(place, teacher, student, logs, vocab_head)


def finish_kernel(parts_ref, preact_ref, out_ref):
    grad_heads = parts_ref[0].astype(F32)
    for at in range(1, parts_ref.shape[0]):
        grad_heads = grad_heads + parts_ref[at].astype(F32)
    preact = preact_ref[...]
    sigma = jax.nn.sigmoid(preact)
    grad_pre = grad_heads * (sigma * (1.0 + preact * (1.0 - sigma)))
    total = jnp.sum(grad_pre, axis=0, keepdims=True)
    high = total.astype(BF16).astype(F32)
    middle = (total - high).astype(BF16).astype(F32)
    row = lax.broadcasted_iota(jnp.int32, (16, grad_pre.shape[1]), 0)
    extra = jnp.where(row == 0, high, jnp.where(row == 1, middle, total - high - middle))
    extra = jnp.where(row < 3, extra, 0.0).astype(BF16)
    for at in range(out_ref.shape[0]):
        out_ref[at, : grad_pre.shape[0]] = grad_pre.astype(BF16)
        out_ref[at, grad_pre.shape[0] :] = extra


def finished(parts, preact):
    rows, across = preact.shape
    return local_call(
        finish_kernel,
        shape(8, rows + 16, across, dtype=BF16),
        cost(0, 4 * parts.size),
        limit=4 * 1024 * 1024,
        scalars=False,
    )(parts, preact)


def pass_kernel(*refs):
    pass


def settled(blocks, awaited):
    return pl.pallas_call(
        pass_kernel,
        in_specs=[pl.BlockSpec(memory_space=pl.ANY)] * (len(blocks) + 1),
        out_specs=[pl.BlockSpec(memory_space=pl.ANY)] * len(blocks),
        out_shape=[shape(*block.shape, dtype=block.dtype) for block in blocks],
        input_output_aliases={at: at for at in range(len(blocks))},
        compiler_params=pltpu.CompilerParams(vmem_limit_bytes=1024 * 1024),
        cost_estimate=cost(0, 0),
    )(*blocks, awaited)


def summed_parts(parts_ref):
    parts = [parts_ref[at] for at in range(parts_ref.shape[0])]
    while len(parts) > 1:
        parts = [parts[at] + parts[at + 1] for at in range(0, len(parts), 2)]
    return parts[0]


def total_kernel(parts_ref, out_ref):
    sums = summed_parts(parts_ref)
    for at in range(out_ref.shape[0]):
        out_ref[at] = sums


def log_kernel(parts_ref, out_ref):
    sums = summed_parts(parts_ref)
    sums = jnp.concatenate([sums[:4], sums[4:]], axis=1)
    logs = jnp.log(sums[:2])
    out_ref[...] = jnp.zeros(out_ref.shape, F32)
    out_ref[:2] = logs
    out_ref[2:3] = sums[2:3] / sums[:1] - logs[:1] + logs[1:]


def totalled(kernel, parts, *sizes):
    return local_call(
        kernel,
        shape(*sizes),
        cost(parts.size, 4 * parts.size),
        limit=2 * 1024 * 1024,
        scalars=False,
    )(parts)


def join_kernel(*refs):
    firsts, seconds, (first_ref, second_ref) = refs[:4], refs[4:8], refs[-2:]
    (rows, width), (block, _) = firsts[0].shape, seconds[0].shape
    for at, peer in enumerate(PEERS):
        first_ref[:, peer * width : (peer + 1) * width] = firsts[at][...]
        second_ref[peer * block : (peer + 1) * block] = seconds[at][...]


def join(firsts, seconds, awaited):
    (rows, width), (block, across) = firsts[0].shape, seconds[0].shape
    firsts, seconds = [firsts[peer] for peer in PEERS], [seconds[peer] for peer in PEERS]
    vmem = pl.BlockSpec(memory_space=pltpu.VMEM)
    return pl.pallas_call(
        join_kernel,
        in_specs=[vmem] * 8 + [pl.BlockSpec(memory_space=pl.ANY)],
        out_specs=[vmem] * 2,
        out_shape=[
            shape(rows, 4 * width, dtype=BF16),
            shape(4 * block, across, dtype=BF16),
        ],
        compiler_params=pltpu.CompilerParams(vmem_limit_bytes=4 * 1024 * 1024),
        cost_estimate=cost(0, 16 * rows * width),
    )(*firsts, *seconds, pltpu.with_memory_space_constraint(awaited, pltpu.HBM))


def stack_kernel(*refs):
    blocks, out_ref = refs[:4], refs[-1]
    rows = blocks[0].shape[0]
    for at, block in enumerate(blocks):
        out_ref[at * rows : (at + 1) * rows] = block[...]


def stacked(blocks, awaited):
    rows, across = blocks[0].shape
    return pl.pallas_call(
        stack_kernel,
        in_specs=[pl.BlockSpec(memory_space=pltpu.VMEM)] * 4 + [pl.BlockSpec(memory_space=pl.ANY)],
        out_specs=pl.BlockSpec(memory_space=pltpu.VMEM),
        out_shape=shape(4 * rows, across, dtype=BF16),
        compiler_params=pltpu.CompilerParams(vmem_limit_bytes=4 * 1024 * 1024),
        cost_estimate=cost(0, 16 * rows * across),
    )(*blocks, awaited)


def heads_kernel(parts_ref, residual_ref, bias_ref, heads_ref, preact_ref):
    preact = summed_parts(parts_ref) + bias_ref[...]
    preact_ref[...] = preact
    heads = residual_ref[...].astype(F32) + preact * jax.nn.sigmoid(preact)
    for at in range(heads_ref.shape[0]):
        heads_ref[at] = heads.astype(BF16)


def heads_of(parts, residual, bias):
    rows, across = residual.shape
    return local_call(
        heads_kernel,
        [shape(8, rows, across, dtype=BF16), shape(rows, across)],
        cost(HEADS_COST, 4 * parts.size),
        limit=4 * 1024 * 1024,
        scalars=False,
    )(parts, residual, bias[None])


def gather_lines(heads):
    return exchange(heads, "z").transpose(1, 0, 2).reshape(heads.shape[1], -1)


def gather_heads(lines, target_all, teacher):
    half = lines.shape[0] // 2
    first, second = join(
        from_peers(lines[:half], "y"), from_peers(lines[half:], "x"), target_all
    )
    blocks = from_peers(first, "x") + from_peers(second, "y")
    blocks = settled([blocks[at] for at in SETTLED], teacher)
    blocks = [blocks[SETTLED.index(at)] for at in range(8)]
    return blocks, [swap(block, "c", 1) for block in blocks]


def scatter_grad(own, other):
    rows, depth = own.shape
    mine = (own.astype(F32) + swap(other, "c", 1).astype(F32)).astype(BF16)
    half = rows // 2
    block = half // 4
    width = depth // 4
    first = [mine[i * block : (i + 1) * block] for i in range(4)]
    second = [mine[half:, i * width : (i + 1) * width] for i in range(4)]
    first, second = summed(first, "x"), summed(second, "y")
    first = [first[:, i * width : (i + 1) * width] for i in range(4)]
    second = [second[i * block : (i + 1) * block] for i in range(4)]
    first, second = summed(first, "y"), summed(second, "x")
    lines = jnp.concatenate([first, second], axis=0)
    sent = lines.reshape(2 * block, 8, -1).transpose(1, 0, 2)
    return exchange(sent, "z")


def shards(log_hidden, positions, offsets, head_weight, head_bias, vocab_head):
    reps, vocs = 32, 8
    in_width, out_width = head_weight.shape
    own = positions.shape[0]
    count = own * reps
    rows = count // vocs
    at_x, at_y, at_c = lax.axis_index("x"), lax.axis_index("y"), lax.axis_index("c")
    voc_index = at_x * 2 + at_c
    steps = jnp.arange(16)
    order = ((at_x ^ (steps % 4)) * 2 + (at_c ^ (steps // 8))) * 2 + (steps // 4) % 2
    target_order = (order // 4 ^ at_y) * 4 + order % 4
    place = jnp.concatenate([order, at_y[None], target_order]).astype(jnp.int32)
    with jax.named_scope("prepare"):
        stored, done = prepare(place, vocab_head)
    with jax.named_scope("gather_z"):
        sent = taken(voc_index[None], positions, offsets, log_hidden, in_width, out_width)
        sent = sent.reshape(8, own, -1)
        (lines,) = settled([exchange(sent, "z")], done)
        lines = lines.reshape(8 * own, -1)
        input_lines, target_lines = lines[:, :in_width], lines[:, in_width : 2 * in_width]
        input_cols = lines[:, 2 * in_width :].reshape(-1, 4, out_width).transpose(1, 0, 2)
    with jax.named_scope("gather_inputs"):
        sent = jnp.concatenate(
            [jnp.broadcast_to(input_lines, (4, *input_lines.shape)), input_cols], axis=2
        )
        got = exchange(sent, "y")
        input_rows = got[:, :, :in_width].reshape(count, in_width)
        residual = got[:, :, in_width:].reshape(count, out_width)
        residual = lax.dynamic_slice_in_dim(residual, voc_index * rows, rows, 0)
    with jax.named_scope("head"):
        partial_pre = jnp.dot(input_rows, head_weight, preferred_element_type=F32)
        parts = exchange(partial_pre.reshape(vocs, rows, out_width), VOC)
        heads, preact = heads_of(parts, residual, head_bias)
    with jax.named_scope("gather_targets"):
        target_rows = stacked(from_peers(target_lines, "y"), partial_pre)
        target_all = lax.all_gather(target_rows, VOC, axis=1, tiled=True)
    with jax.named_scope("gather_heads"):
        lines = gather_lines(heads)
    with jax.named_scope("teacher"):
        teacher, down = teacher_logits(place, target_all, stored)
    with jax.named_scope("gather_heads"):
        own_blocks, other_blocks = gather_heads(lines, target_all, teacher)
    with jax.named_scope("student"):
        entries = vocab_head.shape[0]
        own_logits, table = own_student(entries, own_blocks, teacher, down)
        other_logits, sums = other_student(entries, place, other_blocks, teacher, down, table)
    with jax.named_scope("totals"):
        sums = totalled(total_kernel, exchange(sums, ("y", "x", "c")), 8, 8, count // 2)
        logs = totalled(log_kernel, exchange(sums, "z"), 8, count)
        loss = jnp.sum(logs[2]) / count
    with jax.named_scope("grad"):
        other_rows = grad_rows(1, place, teacher, other_logits, logs, vocab_head)
        own_rows = grad_rows(0, place, teacher, own_logits, logs, vocab_head)
    with jax.named_scope("reduce_grad"):
        grad_parts = scatter_grad(own_rows, other_rows)
    with jax.named_scope("finish"):
        got = exchange(finished(grad_parts, preact), VOC)
        grad_all = got[:, :rows].reshape(count, out_width)
        grad_bias = jnp.sum(got[:, rows : rows + 3].astype(F32), axis=(0, 1))
        grad_weight = lax.dot_general(
            input_rows, grad_all, (((0,), (0,)), ((), ())), preferred_element_type=F32
        )
    return (loss, grad_weight, grad_bias)


def solution(mesh):
    fine = Mesh(mesh.devices.reshape(tuple(SIZES.values())), tuple(SIZES))
    return jax.shard_map(
        shards,
        mesh=fine,
        in_specs=(
            P(REP, None),
            P(REP),
            P(REP),
            P(VOC, REP),
            P(REP),
            P((*REP, *VOC), None),
        ),
        out_specs=(P(), P(VOC, REP), P(REP)),
        check_vma=False,
    )
```

```python
import functools

import jax
import jax.numpy as jnp
from jax import lax
from jax.experimental import pallas as pl
from jax.experimental.pallas import tpu as pltpu
from jax.sharding import Mesh, PartitionSpec as P

BF16 = jnp.bfloat16
F32 = jnp.float32
REP = ("y", "z")
VOC = ("x", "c")
CHUNKS = 4
PADDED = 512
LIMIT = 14 * 1024 * 1024
HEADS_COST = 60_000_000_000
SIZES = {"y": 4, "z": 8, "x": 4, "c": 2}


def exchange(blocks, axis):
    return lax.all_to_all(blocks, axis, split_axis=0, concat_axis=0, tiled=True)


def gathered(block, axis, count):
    return exchange(jnp.broadcast_to(block[None], (count, *block.shape)), axis)


PEERS = (0, 2, 3, 1)
SETTLED = (*PEERS, *(4 + at for at in PEERS))


def swap(block, axis, step):
    return lax.ppermute(block, axis, [(i, i ^ step) for i in range(SIZES[axis])])


def from_peers(block, axis):
    return [block] + [swap(block, axis, step) for step in range(1, SIZES[axis])]


def summed(blocks, axis):
    total = blocks[0].astype(F32)
    for step in range(1, SIZES[axis]):
        total = total + swap(blocks[step], axis, step).astype(F32)
    return total.astype(BF16)


def cost(flops, bytes_accessed, transcendentals=0):
    return pl.CostEstimate(
        flops=flops, bytes_accessed=bytes_accessed, transcendentals=transcendentals
    )


def local_call(kernel, out_shape, estimate, scratch=(), limit=LIMIT, scalars=True):
    def call(*operands):
        specs = [pl.BlockSpec(memory_space=pltpu.VMEM)] * len(operands)
        if scalars:
            specs[0] = pl.BlockSpec(memory_space=pltpu.SMEM)
        return pl.pallas_call(
            kernel,
            in_specs=specs,
            out_specs=jax.tree.map(lambda _: pl.BlockSpec(memory_space=pltpu.VMEM), out_shape),
            out_shape=out_shape,
            scratch_shapes=scratch,
            compiler_params=pltpu.CompilerParams(vmem_limit_bytes=limit),
            cost_estimate=estimate,
        )(*operands)

    return call


def shape(*sizes, dtype=F32):
    return jax.ShapeDtypeStruct(sizes, dtype)


def prepare_kernel(place, vocab_ref, down_ref, done_ref, wide):
    entries, depth = vocab_ref.shape
    width = depth // CHUNKS
    done_ref[...] = jnp.zeros(done_ref.shape, F32)
    wide[...] = jnp.zeros(wide.shape, F32)
    for at in range(CHUNKS):
        start = pl.multiple_of((place[16] ^ at) * width, width)
        wide[:entries] = vocab_ref[:, pl.ds(start, width)].astype(F32)
        down_ref[at * width : (at + 1) * width] = wide[...].T.astype(BF16)


def prepare(place, vocab_head):
    depth = vocab_head.shape[1]
    return local_call(
        prepare_kernel,
        [shape(depth, PADDED, dtype=BF16), shape(8, 128)],
        cost(0, 4 * PADDED * depth),
        [pltpu.VMEM((PADDED, depth // CHUNKS), F32)],
    )(place, vocab_head)


def teacher_kernel(place, target_ref, stored_ref, out_ref, down_ref, total, arrived):
    width = down_ref.shape[0] // CHUNKS
    copies = []
    for at in range(CHUNKS):
        rows = pl.ds(at * width, width)
        copies.append(
            pltpu.make_async_copy(stored_ref.at[rows], down_ref.at[rows], arrived.at[at])
        )
        copies[at].start()
    for at in range(CHUNKS):
        start = pl.multiple_of((place[16] ^ at) * width, width)
        copies[at].wait()
        product = jnp.dot(
            target_ref[:, pl.ds(start, width)],
            down_ref[at * width : (at + 1) * width],
            preferred_element_type=F32,
        )
        total[...] = product if at == 0 else total[...] + product
    for at in range(16):
        start = pl.multiple_of(place[17 + at] * 16, 16)
        out_ref[at * 16 : (at + 1) * 16] = total[pl.ds(start, 16)]


def teacher_logits(place, target_all, stored):
    count, depth = target_all.shape
    vmem = pl.BlockSpec(memory_space=pltpu.VMEM)
    return pl.pallas_call(
        teacher_kernel,
        in_specs=[
            pl.BlockSpec(memory_space=pltpu.SMEM),
            vmem,
            pl.BlockSpec(memory_space=pl.ANY),
        ],
        out_specs=[vmem, vmem],
        out_shape=[shape(count, PADDED), shape(*stored.shape, dtype=BF16)],
        scratch_shapes=[pltpu.VMEM((count, PADDED), F32), pltpu.SemaphoreType.DMA((CHUNKS,))],
        compiler_params=pltpu.CompilerParams(vmem_limit_bytes=LIMIT),
        cost_estimate=cost(2 * count * PADDED * depth, 2 * (count + PADDED) * depth),
    )(place, target_all, pltpu.with_memory_space_constraint(stored, pltpu.HBM))


def student_part(entries, core, firsts, seconds, teacher_ref, down_ref, out_ref):
    width = down_ref.shape[0] // CHUNKS
    rows = out_ref.shape[0]
    for at in range(CHUNKS):
        blocks = [ref[:, at * width : (at + 1) * width] for ref in firsts] + [seconds[at][...]]
        product = jnp.dot(
            jnp.concatenate(blocks, axis=0),
            down_ref[at * width : (at + 1) * width],
            preferred_element_type=F32,
        )
        out_ref[...] = product if at == 0 else out_ref[...] + product
    student, teacher = out_ref[...], teacher_ref[core * rows : (core + 1) * rows]
    real = lax.broadcasted_iota(jnp.int32, student.shape, 1) < entries
    exp_teacher = jnp.where(real, jnp.exp(teacher), 0.0)
    columns = [
        jnp.sum(exp_teacher, axis=1, keepdims=True),
        jnp.sum(jnp.where(real, jnp.exp(student), 0.0), axis=1, keepdims=True),
        jnp.sum(exp_teacher * (teacher - student), axis=1, keepdims=True),
    ]
    lane = lax.broadcasted_iota(jnp.int32, (rows, 128), 1)
    table = jnp.zeros((rows, 128), F32)
    for at, column in enumerate(columns):
        table = jnp.where(lane == at, column, table)
    return table


def packed(table):
    lanes = table.shape[1] // 2
    return jnp.concatenate([table[:, :lanes], table[:, lanes:]], axis=0)


def own_student_kernel(entries, *refs):
    teacher_ref, down_ref, out_ref, table_ref = refs[8:]
    table_ref[...] = student_part(
        entries, 0, refs[:4], refs[4:8], teacher_ref, down_ref, out_ref
    )


def other_student_kernel(entries, place, *refs):
    teacher_ref, down_ref, own_ref, out_ref, sums_ref, turned = refs[8:]
    other = student_part(entries, 1, refs[:4], refs[4:8], teacher_ref, down_ref, out_ref)
    for core, table in enumerate((own_ref[...], other)):
        for at in range(8):
            start = pl.multiple_of(place[core * 8 + at] * 16, 16)
            turned[pl.ds(start, 16)] = table[at * 16 : (at + 1) * 16]
    sums = packed(turned[...].T[:4])
    for at in range(sums_ref.shape[0]):
        sums_ref[at] = sums


def own_student(entries, blocks, teacher, down):
    rows = teacher.shape[0] // 2
    return local_call(
        functools.partial(own_student_kernel, entries),
        [shape(rows, PADDED), shape(rows, 128)],
        cost(2 * rows * down.size, 2 * down.size, 2 * rows * PADDED),
        scalars=False,
    )(*blocks, teacher, down)


def other_student(entries, place, blocks, teacher, down, table):
    rows = teacher.shape[0] // 2
    return local_call(
        functools.partial(other_student_kernel, entries),
        [shape(rows, PADDED), shape(32, 8, rows)],
        cost(2 * rows * down.size, 2 * down.size, 2 * rows * PADDED),
        [pltpu.VMEM((2 * rows, 128), F32)],
    )(place, *blocks, teacher, down, table)


def grad_kernel(core, place, teacher_ref, student_ref, logs_ref, vocab_ref, out_ref, table, turned):
    rows, depth = out_ref.shape
    entries, width = vocab_ref.shape[0], depth // CHUNKS
    table[...] = jnp.concatenate(
        [logs_ref[...], jnp.zeros((120, 2 * rows), F32)], axis=0
    ).T
    for at in range(8):
        start = pl.multiple_of(place[core * 8 + at] * 16, 16)
        turned[at * 16 : (at + 1) * 16] = table[pl.ds(start, 16)]
    student = jnp.exp(student_ref[...] - turned[:, 1:2])
    teacher = jnp.exp(teacher_ref[core * rows : (core + 1) * rows] - turned[:, 0:1])
    grad = (student - teacher)[:, :entries].astype(BF16)
    for at in range(CHUNKS):
        start = pl.multiple_of((place[16] ^ at) * width, width)
        out_ref[:, at * width : (at + 1) * width] = jnp.dot(
            grad, vocab_ref[:, pl.ds(start, width)], preferred_element_type=F32
        ).astype(BF16)


def grad_rows(core, place, teacher, student, logs, vocab_head):
    rows, depth = student.shape[0], vocab_head.shape[1]
    return local_call(
        functools.partial(grad_kernel, core),
        shape(rows, depth, dtype=BF16),
        cost(2 * rows * vocab_head.size, 2 * vocab_head.size, 2 * rows * PADDED),
        [pltpu.VMEM((2 * rows, 128), F32), pltpu.VMEM((rows, 128), F32)],
    )(place, teacher, student, logs, vocab_head)


def finish_kernel(parts_ref, preact_ref, out_ref):
    grad_heads = parts_ref[0].astype(F32)
    for at in range(1, parts_ref.shape[0]):
        grad_heads = grad_heads + parts_ref[at].astype(F32)
    preact = preact_ref[...]
    sigma = jax.nn.sigmoid(preact)
    grad_pre = grad_heads * (sigma * (1.0 + preact * (1.0 - sigma)))
    total = jnp.sum(grad_pre, axis=0, keepdims=True)
    high = total.astype(BF16).astype(F32)
    middle = (total - high).astype(BF16).astype(F32)
    row = lax.broadcasted_iota(jnp.int32, (16, grad_pre.shape[1]), 0)
    extra = jnp.where(row == 0, high, jnp.where(row == 1, middle, total - high - middle))
    extra = jnp.where(row < 3, extra, 0.0).astype(BF16)
    for at in range(out_ref.shape[0]):
        out_ref[at, : grad_pre.shape[0]] = grad_pre.astype(BF16)
        out_ref[at, grad_pre.shape[0] :] = extra


def finished(parts, preact):
    rows, across = preact.shape
    return local_call(
        finish_kernel,
        shape(8, rows + 16, across, dtype=BF16),
        cost(0, 4 * parts.size),
        limit=4 * 1024 * 1024,
        scalars=False,
    )(parts, preact)


def pass_kernel(*refs):
    pass


def settled(blocks, awaited):
    return pl.pallas_call(
        pass_kernel,
        in_specs=[pl.BlockSpec(memory_space=pl.ANY)] * (len(blocks) + 1),
        out_specs=[pl.BlockSpec(memory_space=pl.ANY)] * len(blocks),
        out_shape=[shape(*block.shape, dtype=block.dtype) for block in blocks],
        input_output_aliases={at: at for at in range(len(blocks))},
        compiler_params=pltpu.CompilerParams(vmem_limit_bytes=1024 * 1024),
        cost_estimate=cost(0, 0),
    )(*blocks, awaited)


def summed_parts(parts_ref):
    parts = [parts_ref[at] for at in range(parts_ref.shape[0])]
    while len(parts) > 1:
        parts = [parts[at] + parts[at + 1] for at in range(0, len(parts), 2)]
    return parts[0]


def total_kernel(parts_ref, out_ref):
    sums = summed_parts(parts_ref)
    for at in range(out_ref.shape[0]):
        out_ref[at] = sums


def log_kernel(parts_ref, out_ref):
    sums = summed_parts(parts_ref)
    sums = jnp.concatenate([sums[:4], sums[4:]], axis=1)
    logs = jnp.log(sums[:2])
    out_ref[...] = jnp.zeros(out_ref.shape, F32)
    out_ref[:2] = logs
    out_ref[2:3] = sums[2:3] / sums[:1] - logs[:1] + logs[1:]


def totalled(kernel, parts, *sizes):
    return local_call(
        kernel,
        shape(*sizes),
        cost(parts.size, 4 * parts.size),
        limit=2 * 1024 * 1024,
        scalars=False,
    )(parts)


def join_kernel(*refs):
    firsts, seconds, (first_ref, second_ref) = refs[:4], refs[4:8], refs[-2:]
    (rows, width), (block, _) = firsts[0].shape, seconds[0].shape
    for at, peer in enumerate(PEERS):
        first_ref[:, peer * width : (peer + 1) * width] = firsts[at][...]
        second_ref[peer * block : (peer + 1) * block] = seconds[at][...]


def join(firsts, seconds, awaited):
    (rows, width), (block, across) = firsts[0].shape, seconds[0].shape
    firsts, seconds = [firsts[peer] for peer in PEERS], [seconds[peer] for peer in PEERS]
    vmem = pl.BlockSpec(memory_space=pltpu.VMEM)
    return pl.pallas_call(
        join_kernel,
        in_specs=[vmem] * 8 + [pl.BlockSpec(memory_space=pl.ANY)],
        out_specs=[vmem] * 2,
        out_shape=[
            shape(rows, 4 * width, dtype=BF16),
            shape(4 * block, across, dtype=BF16),
        ],
        compiler_params=pltpu.CompilerParams(vmem_limit_bytes=4 * 1024 * 1024),
        cost_estimate=cost(0, 16 * rows * width),
    )(*firsts, *seconds, pltpu.with_memory_space_constraint(awaited, pltpu.HBM))


def stack_kernel(*refs):
    blocks, out_ref = refs[:4], refs[-1]
    rows = blocks[0].shape[0]
    for peer, block in zip(PEERS, blocks):
        out_ref[peer * rows : (peer + 1) * rows] = block[...]


def stacked(blocks, awaited):
    rows, across = blocks[0].shape
    return pl.pallas_call(
        stack_kernel,
        in_specs=[pl.BlockSpec(memory_space=pltpu.VMEM)] * 4 + [pl.BlockSpec(memory_space=pl.ANY)],
        out_specs=pl.BlockSpec(memory_space=pltpu.VMEM),
        out_shape=shape(4 * rows, across, dtype=BF16),
        compiler_params=pltpu.CompilerParams(vmem_limit_bytes=4 * 1024 * 1024),
        cost_estimate=cost(0, 16 * rows * across),
    )(*[blocks[peer] for peer in PEERS], awaited)


def heads_kernel(parts_ref, residual_ref, bias_ref, heads_ref, preact_ref):
    preact = summed_parts(parts_ref) + bias_ref[...]
    preact_ref[...] = preact
    heads = residual_ref[...].astype(F32) + preact * jax.nn.sigmoid(preact)
    for at in range(heads_ref.shape[0]):
        heads_ref[at] = heads.astype(BF16)


def heads_of(parts, residual, bias):
    rows, across = residual.shape
    return local_call(
        heads_kernel,
        [shape(8, rows, across, dtype=BF16), shape(rows, across)],
        cost(HEADS_COST, 4 * parts.size),
        limit=4 * 1024 * 1024,
        scalars=False,
    )(parts, residual, bias[None])


def gather_lines(heads):
    return exchange(heads, "z").transpose(1, 0, 2).reshape(heads.shape[1], -1)


def gather_heads(lines, target_all, teacher):
    half = lines.shape[0] // 2
    first, second = join(
        from_peers(lines[:half], "y"), from_peers(lines[half:], "x"), target_all
    )
    blocks = from_peers(first, "x") + from_peers(second, "y")
    blocks = settled([blocks[at] for at in SETTLED], teacher)
    blocks = [blocks[SETTLED.index(at)] for at in range(8)]
    return blocks, [swap(block, "c", 1) for block in blocks]


def scatter_grad(own, other):
    rows, depth = own.shape
    mine = (own.astype(F32) + swap(other, "c", 1).astype(F32)).astype(BF16)
    half = rows // 2
    block = half // 4
    width = depth // 4
    first = [mine[i * block : (i + 1) * block] for i in range(4)]
    second = [mine[half:, i * width : (i + 1) * width] for i in range(4)]
    first, second = summed(first, "x"), summed(second, "y")
    first = [first[:, i * width : (i + 1) * width] for i in range(4)]
    second = [second[i * block : (i + 1) * block] for i in range(4)]
    first, second = summed(first, "y"), summed(second, "x")
    lines = jnp.concatenate([first, second], axis=0)
    sent = lines.reshape(2 * block, 8, -1).transpose(1, 0, 2)
    return exchange(sent, "z")


def shards(log_hidden, positions, offsets, head_weight, head_bias, vocab_head):
    reps, vocs = 32, 8
    in_width, out_width = head_weight.shape
    own = positions.shape[0]
    count = own * reps
    rows = count // vocs
    at_x, at_y, at_c = lax.axis_index("x"), lax.axis_index("y"), lax.axis_index("c")
    voc_index = at_x * 2 + at_c
    taken = jnp.concatenate([positions, positions + offsets])
    taken = jnp.take(log_hidden, taken, axis=0, mode="clip")
    inputs = taken[:own]
    steps = jnp.arange(16)
    order = ((at_x ^ (steps % 4)) * 2 + (at_c ^ (steps // 8))) * 2 + (steps // 4) % 2
    target_order = (order // 4 ^ at_y) * 4 + order % 4
    place = jnp.concatenate([order, at_y[None], target_order]).astype(jnp.int32)
    with jax.named_scope("prepare"):
        stored, done = prepare(place, vocab_head)
    with jax.named_scope("gather_z"):
        blocks = lax.dynamic_slice_in_dim(
            taken.reshape(2, own, -1), voc_index * in_width, in_width, 2
        )
        input_cols = inputs.reshape(own, 4, 8, out_width).transpose(2, 0, 1, 3)
        sent = jnp.concatenate(
            [
                jnp.broadcast_to(blocks[0], (8, own, in_width)),
                jnp.broadcast_to(blocks[1], (8, own, in_width)),
                input_cols.reshape(8, own, -1),
            ],
            axis=2,
        )
        (lines,) = settled([exchange(sent, "z")], done)
        lines = lines.reshape(8 * own, -1)
        input_lines, target_lines = lines[:, :in_width], lines[:, in_width : 2 * in_width]
        input_cols = lines[:, 2 * in_width :].reshape(-1, 4, out_width).transpose(1, 0, 2)
    with jax.named_scope("gather_inputs"):
        sent = jnp.concatenate(
            [jnp.broadcast_to(input_lines, (4, *input_lines.shape)), input_cols], axis=2
        )
        got = exchange(sent, "y")
        input_rows = got[:, :, :in_width].reshape(count, in_width)
        residual = got[:, :, in_width:].reshape(count, out_width)
        residual = lax.dynamic_slice_in_dim(residual, voc_index * rows, rows, 0)
    with jax.named_scope("head"):
        partial_pre = jnp.dot(input_rows, head_weight, preferred_element_type=F32)
        parts = exchange(partial_pre.reshape(vocs, rows, out_width), VOC)
        heads, preact = heads_of(parts, residual, head_bias)
    with jax.named_scope("gather_targets"):
        target_rows = stacked(from_peers(target_lines, "y"), partial_pre)
        target_all = lax.all_gather(target_rows, VOC, axis=1, tiled=True)
    with jax.named_scope("gather_heads"):
        lines = gather_lines(heads)
    with jax.named_scope("teacher"):
        teacher, down = teacher_logits(place, target_all, stored)
    with jax.named_scope("gather_heads"):
        own_blocks, other_blocks = gather_heads(lines, target_all, teacher)
    with jax.named_scope("student"):
        entries = vocab_head.shape[0]
        own_logits, table = own_student(entries, own_blocks, teacher, down)
        other_logits, sums = other_student(entries, place, other_blocks, teacher, down, table)
    with jax.named_scope("totals"):
        sums = totalled(total_kernel, exchange(sums, ("y", "x", "c")), 8, 8, count // 2)
        logs = totalled(log_kernel, exchange(sums, "z"), 8, count)
        loss = jnp.sum(logs[2]) / count
    with jax.named_scope("grad"):
        other_rows = grad_rows(1, place, teacher, other_logits, logs, vocab_head)
        own_rows = grad_rows(0, place, teacher, own_logits, logs, vocab_head)
    with jax.named_scope("reduce_grad"):
        grad_parts = scatter_grad(own_rows, other_rows)
    with jax.named_scope("finish"):
        got = exchange(finished(grad_parts, preact), VOC)
        grad_all = got[:, :rows].reshape(count, out_width)
        grad_bias = jnp.sum(got[:, rows : rows + 3].astype(F32), axis=(0, 1))
        grad_weight = lax.dot_general(
            input_rows, grad_all, (((0,), (0,)), ((), ())), preferred_element_type=F32
        )
    return (loss, grad_weight, grad_bias)


def solution(mesh):
    fine = Mesh(mesh.devices.reshape(tuple(SIZES.values())), tuple(SIZES))
    return jax.shard_map(
        shards,
        mesh=fine,
        in_specs=(
            P(REP, None),
            P(REP),
            P(REP),
            P(VOC, REP),
            P(REP),
            P((*REP, *VOC), None),
        ),
        out_specs=(P(), P(VOC, REP), P(REP)),
        check_vma=False,
    )
```
